32 devices in a mesh: ctx: 2 (over x), exp: 16 (over z, y, core).
Axes of the slice: x: 2, y: 2, z: 4, core: 2. Of those that a mesh axis runs over, the one named last changes fastest.
Arguments:
- hidden: bfloat16 [16, 16, 5120], P('exp', 'ctx'), may hold values from -6 to 6
- queries: bfloat16 [256, 36864], P('ctx', 'exp'), may hold values from -50 to 50
- latents: bfloat16 [256, 576], P('ctx'), may hold values from -6.5 to 6.5
- expert_ids: int32 [16, 16, 6], P('exp', 'ctx'), may hold values from 0 to 15, all different within a row; in each aligned block of 8 rows (0 to 7, 8 to 15, ..., all dimensions but the last counted through in order) at most 4 rows name the same one
- route_weight: float32 [16, 16, 6], P('exp', 'ctx'), may hold values from 0.1 to 1
- w_gate: bfloat16 [16, 1536, 5120], P('exp', 'ctx'), may hold values from -0.078125 to 0.078125
- w_up: bfloat16 [16, 1536, 5120], P('exp', 'ctx'), may hold values from -0.078125 to 0.078125
- w_down: bfloat16 [16, 5120, 1536], P('exp', 'ctx'), may hold values from -0.15625 to 0.15625
Outputs:
- attended: bfloat16 [256, 32768], P('ctx', 'exp')
- moe_out: bfloat16 [16, 16, 5120], P('exp', 'ctx')
The draws below stay inside these ranges and needn't reach their ends.
Inputs may be any that keep to these rules, and one draw needn't show every extreme that they name: `expert_ids`: each token names 6 different experts. Within the 8 rows of one device (aligned blocks of rows of one group) no expert is named by more than 4 rows, a bound that some block reaches.
All inputs are finite; a program needn't handle non-finite values.
Results may differ from the reference program's by a relative error of at most 0.0057.
Values may be sent and summed in bfloat16 or wider, within the bound.
No kernel may reach another device: no remote copies, remote signals or barrier semaphores. Data moves between devices by JAX's collectives and lax.ppermute only.
A program may use at most 64 MiB of HBM per device.

```python
import math
import jax
import jax.numpy as jnp
import numpy as np
from jax import lax

D = 5120
LATENT = 512
ROPE = 64
HID = 1536
TOPK = 6
HEADS = 64
TOK_DEV = 128
MOE_DEV = 8
EXPERTS = 16
CAP = 4
MAXROWS = 128
GROUPS = 16
ROWS = 16
LEN = 256
N_EXP = 16


def latent_pair(key):
    base = jax.random.fold_in(key, 4711)
    key_kv, key_q = jax.random.split(base, 2)
    width = LATENT + ROPE
    latent = jnp.clip(jax.random.normal(key_kv, (LEN, width), jnp.float32), -6.0, 6.0)
    query = jnp.clip(jax.random.normal(key_q, (LEN, HEADS, width), jnp.float32), -6.0, 6.0)
    return (query.reshape(LEN, HEADS * width), latent)


def draw_queries(key, part):
    return latent_pair(key)[0].astype(jnp.bfloat16)


def draw_latents(key, part):
    return latent_pair(key)[1].astype(jnp.bfloat16)


def levels(key, shape, shards, smallest, top_value):
    gain = 1.0
    for position, shards_of in shards:
        steps = jax.random.uniform(jax.random.fold_in(jax.random.fold_in(key, 6), position), (shards_of,), jnp.float32, smallest / len(shards), top_value / len(shards))
        gain = gain * jnp.repeat(jnp.exp(steps), shape[position] // shards_of).reshape((-1,) + (1,) * (len(shape) - 1 - position))
    return gain


def assign_block(stream_key, own, number, rows, number_of, top, limit, skew):
    order = jax.random.permutation(stream_key, number_of)
    packed, ordinary = shares(number_of, rows * top, limit, skew, True), shares(number_of, rows * top, limit, skew, False)
    places = jnp.arange(number_of)

    def named(sizes, offset_by):
        used = int((sizes > 0).sum())
        fixed = max(1, used // 4)
        shifted = fixed + (places - fixed + offset_by * (used - fixed)) % max(1, number_of - fixed)
        return jnp.zeros((number_of,), jnp.int32).at[order[jnp.where(places < fixed, places, shifted)]].set(jnp.asarray(sizes, jnp.int32))

    sizes = jnp.where(number % 4 == 0, named(packed, number // 4), named(ordinary, number - number // 4 - 1))
    mixed = jax.random.permutation(jax.random.fold_in(own, 3), number_of)
    source_of, receiver = mixed[0:number_of // 2 * 2:2], mixed[1:number_of // 2 * 2:2]
    slack = jnp.minimum(sizes[source_of] - 1, limit - sizes[receiver]) // 2
    slack = jnp.where((source_of == order[0]) | (receiver == order[0]) | (sizes[receiver] == 0), 0, jnp.maximum(slack, 0))
    shifted = jax.random.randint(jax.random.fold_in(own, 4), (number_of // 2,), 0, 1 << 20) % (slack + 1)
    sizes = sizes.at[source_of].add(-shifted).at[receiver].add(shifted)
    labels = jnp.searchsorted(jnp.cumsum(sizes), jnp.arange(rows * top), side="right").astype(jnp.int32)
    grid = labels.reshape(top, rows).T
    grid = grid[jax.random.permutation(jax.random.fold_in(own, 1), rows)]
    offset_by = jax.random.randint(jax.random.fold_in(own, 2), (rows, 1), 0, top)
    return jnp.take_along_axis(grid, (jnp.arange(top)[None, :] + offset_by) % top, axis=1)


def shares(number_of, total, bound, lean, full):
    portions = [(1 << 20) // math.isqrt(grade ** lean) + 1 for grade in range(1, number_of + 1)]
    largest = bound if full else min(bound, max(-(-total // number_of), total * portions[0] // sum(portions)))
    least = 1 if total - largest >= number_of - 1 else 0
    counts, spare = [largest] + [least] * (number_of - 1), total - largest - least * (number_of - 1)
    while spare > 0:
        candidates = [i for i in range(1, number_of) if counts[i] < largest] or [i for i in range(1, number_of) if counts[i] < bound]
        pool, budget = sum([portions[i] for i in candidates]), spare
        for i in candidates:
            extra = min(bound - counts[i], max(1, budget * portions[i] // pool), spare)
            counts[i] = counts[i] + extra
            spare = spare - extra
    return np.array(counts)


def normal_values(stream_key, shape, scale, reach, cuts=(), kind=jnp.bfloat16):
    entries = scale * jax.random.normal(stream_key, shape, jnp.float32)
    if cuts:
        entries = entries * levels(stream_key, shape, cuts, -0.22, 0.18)
    return jnp.clip(entries, -reach, reach).astype(kind)


def setup_inputs(seed: int = 0) -> dict:
    streams_of = jax.random.split(jax.random.key(seed), 9)
    hidden = normal_values(streams_of[0], (GROUPS, ROWS, D), 1.0, 6.0, ((0, 16), (1, 2)))
    queries = draw_queries(jax.random.fold_in(streams_of[8], 71), 0)
    latents = draw_latents(jax.random.fold_in(streams_of[8], 71), 0)
    expert_ids_keys = jax.random.split(jax.random.fold_in(streams_of[3], 1), GROUPS * ROWS // MOE_DEV)
    expert_ids_turns = jax.random.permutation(jax.random.fold_in(streams_of[3], 3), GROUPS * ROWS // MOE_DEV)
    expert_ids = jax.vmap(lambda own, number: assign_block(jax.random.fold_in(streams_of[3], 2), own, number, MOE_DEV, N_EXP, TOPK, CAP, 0))(expert_ids_keys, expert_ids_turns).reshape((GROUPS, ROWS, TOPK))
    route_weight = jnp.clip(0.1 + 0.9 * jax.random.uniform(streams_of[4], (GROUPS, ROWS, TOPK), jnp.float32) ** levels(streams_of[4], (GROUPS, ROWS, TOPK), ((0, 16), (1, 2)), -0.2, 0.2), 0.1, 1.0)
    w_gate = normal_values(streams_of[5], (EXPERTS, HID, D), D ** -0.5, 0.078125, ((0, 16), (1, 2)))
    w_up = normal_values(streams_of[6], (EXPERTS, HID, D), D ** -0.5, 0.078125, ((0, 16), (1, 2)))
    w_down = normal_values(streams_of[7], (EXPERTS, D, HID), HID ** -0.5, 0.15625, ((0, 16), (1, 2)))
    return {"hidden": hidden, "queries": queries, "latents": latents, "expert_ids": expert_ids, "route_weight": route_weight, "w_gate": w_gate, "w_up": w_up, "w_down": w_down}


SCALE = 0.07216878364870322


def attend(queries, latents):
    length = latents.shape[0]
    width = LATENT + ROPE
    qv = queries.reshape(length, HEADS, width)
    keys = latents.astype(jnp.float32)
    pos = jnp.arange(length, dtype=jnp.int32)
    block = pos // TOK_DEV
    same = (block[:, None] == block[None, :]) & (pos[None, :] <= pos[:, None])
    before = block[None, :] == block[:, None] - 1
    visible = same | before

    def one_head(index):
        query_head = lax.dynamic_index_in_dim(qv, index, 1, keepdims=False).astype(jnp.float32)
        scores = jnp.einsum("ic,jc->ij", query_head, keys) * SCALE
        scores = jnp.where(visible, scores, jnp.float32(-1e30))
        top = jnp.max(scores, axis=-1, keepdims=True)
        expo = jnp.exp(scores - top)
        probs = (expo / jnp.sum(expo, axis=-1, keepdims=True)).astype(jnp.bfloat16)
        result = jnp.einsum("ij,jc->ic", probs.astype(jnp.float32), keys[:, :LATENT])
        return result.astype(jnp.bfloat16)

    per_head = lax.map(one_head, jnp.arange(HEADS, dtype=jnp.int32))
    return jnp.transpose(per_head, (1, 0, 2)).reshape(length, HEADS * LATENT)


def reference(hidden, queries, latents, expert_ids, route_weight, w_gate, w_up, w_down):
    attended = attend(queries, latents)
    rows_all = hidden.reshape(-1, D)
    picks = expert_ids.reshape(-1, TOPK)
    weights = route_weight.reshape(-1, TOPK)

    def one_expert(total, index):
        hit = picks == index
        rowhit = jnp.any(hit, axis=1)
        count = jnp.sum(rowhit.astype(jnp.int32))
        chosen = jnp.nonzero(rowhit, size=MAXROWS, fill_value=0)[0].astype(jnp.int32)
        valid = jnp.arange(MAXROWS, dtype=jnp.int32) < count
        coef = jnp.sum(jnp.where(hit, weights, jnp.zeros_like(weights)), axis=1)[chosen]
        coef = jnp.where(valid, coef, jnp.zeros_like(coef))
        rows = rows_all[chosen]
        gate_w = lax.dynamic_index_in_dim(w_gate, index, 0, keepdims=False)
        up_w = lax.dynamic_index_in_dim(w_up, index, 0, keepdims=False)
        down_w = lax.dynamic_index_in_dim(w_down, index, 0, keepdims=False)
        gate = jnp.dot(rows, gate_w.T, preferred_element_type=jnp.float32)
        upper = jnp.dot(rows, up_w.T, preferred_element_type=jnp.float32)
        act = (jax.nn.silu(gate) * upper).astype(jnp.bfloat16)
        out_rows = jnp.dot(act, down_w.T, preferred_element_type=jnp.float32).astype(jnp.bfloat16)
        total = total.at[chosen].add(coef[:, None] * out_rows.astype(jnp.float32))
        return total, None

    start = jnp.zeros((rows_all.shape[0], D), jnp.float32)
    total, _ = lax.scan(one_expert, start, jnp.arange(EXPERTS, dtype=jnp.int32))
    moe_out = total.astype(jnp.bfloat16).reshape(hidden.shape)
    return attended, moe_out
```

```python
import jax
import jax.numpy as jnp
from jax import lax
from jax.sharding import PartitionSpec as P

LATENT = 512
ROPE = 64


SCALE = 0.07216878364870322


def shifted(block, axis, distance):
    devices = range(lax.axis_size(axis))
    route = [(i - distance, i) for i in devices if i - distance in devices]
    return lax.ppermute(block, axis, route)


def place_picks(picks, experts, capacity):
    flat = picks.reshape(-1)
    onehot = (flat[:, None] == jnp.arange(experts, dtype=jnp.int32)[None, :]).astype(jnp.int32)
    earlier = jnp.cumsum(onehot, axis=0) - onehot
    rank = jnp.sum(earlier * onehot, axis=1)
    target = flat * capacity + rank
    return (target[:, None] == jnp.arange(experts * capacity, dtype=jnp.int32)[None, :]).astype(
        jnp.float32
    )


def token_table(tok_count, topk):
    owner = jnp.arange(tok_count * topk, dtype=jnp.int32) // topk
    return (owner[:, None] == jnp.arange(tok_count, dtype=jnp.int32)[None, :]).astype(jnp.float32)


def times_rows(left, right):
    return lax.dot_general(
        left, right, (((1,), (1,)), ((), ())), preferred_element_type=jnp.float32
    )


def swapped(block, axis, bit):
    return lax.ppermute(block, axis, [(i, i ^ bit) for i in range(lax.axis_size(axis))])


def moved(block, steps):
    count = lax.axis_size("exp")
    return lax.ppermute(block, "exp", [(i, (i + 4 * steps) % count) for i in range(count)])


def attention(queries, latents, earlier_kv):
    tok_att = latents.shape[0]
    heads_dev = queries.shape[1] // (LATENT + ROPE)
    keys = jnp.concatenate([earlier_kv, latents], axis=0)
    query_rows = queries.reshape(tok_att, heads_dev, LATENT + ROPE)
    scores = jnp.einsum("thc,kc->htk", query_rows, keys, preferred_element_type=jnp.float32) * SCALE
    row_pos = jnp.arange(tok_att, dtype=jnp.int32)
    key_pos = jnp.arange(2 * tok_att, dtype=jnp.int32)
    seen_own = (key_pos[None, :] >= tok_att) & (key_pos[None, :] - tok_att <= row_pos[:, None])
    seen_prev = (key_pos[None, :] < tok_att) & (lax.axis_index("ctx") > 0)
    scores = jnp.where((seen_own | seen_prev)[None, :, :], scores, jnp.float32(-1e30))
    top = jnp.max(scores, axis=-1, keepdims=True)
    expo = jnp.exp(scores - top)
    probs = (expo / jnp.sum(expo, axis=-1, keepdims=True)).astype(jnp.bfloat16)
    mixed_heads = jnp.einsum(
        "htk,kc->thc", probs, keys[:, :LATENT], preferred_element_type=jnp.float32
    )
    return mixed_heads.astype(jnp.bfloat16).reshape(tok_att, heads_dev * LATENT)


def on_device_gathered(
    hidden, queries, latents, expert_ids, route_weight, w_gate, w_up, w_down
):
    tok_dev = hidden.shape[1]
    width = hidden.shape[2]
    topk = expert_ids.shape[2]
    experts = lax.axis_size("exp")
    line = experts // 4
    capacity = min(tok_dev, max(2, 3 * topk * tok_dev // (2 * experts)))
    half = width // 2
    unit = line * tok_dev
    bf16, f32 = jnp.bfloat16, jnp.float32
    first = lax.axis_index("ctx") == 0
    earlier_kv = shifted(latents, "ctx", 1)

    weight = route_weight[0]
    high = weight.astype(bf16)
    low = (weight - high.astype(f32)).astype(bf16)
    notes = jnp.concatenate([expert_ids[0].astype(bf16), high, low], axis=1)
    notes = jnp.pad(notes, ((0, 0), (0, 128 - notes.shape[1])))
    rows = jnp.concatenate([hidden[0], notes], axis=1)

    along = jnp.concatenate([rows] + [moved(rows, d) for d in range(1, line)], axis=0)
    left, right = along[:, :half], along[:, half:]
    left_y = swapped(left, "exp", 2)
    right_x = swapped(right, "ctx", 1)
    left_2 = jnp.concatenate([left, left_y], axis=0)
    right_2 = jnp.concatenate([right, right_x], axis=0)
    left_x = swapped(left_2, "ctx", 1)
    right_y = swapped(right_2, "exp", 2)
    left_4 = jnp.concatenate([left_2, left_x], axis=0)
    right_4 = jnp.concatenate([right, right_y[:unit], right_x, right_y[unit:]], axis=0)
    chip = jnp.concatenate([left_4, right_4], axis=1)
    every = jnp.concatenate([chip, swapped(chip, "exp", 1)], axis=0)

    count = every.shape[0]
    names = every[:, width : width + topk].astype(f32)
    weights = every[:, width + topk : width + 2 * topk].astype(f32) + every[
        :, width + 2 * topk : width + 3 * topk
    ].astype(f32)
    mine = names == lax.axis_index("exp").astype(f32)
    coef = jnp.sum(jnp.where(mine, weights, 0.0), axis=1)
    hit = jnp.any(mine, axis=1)
    by_block = hit.reshape(count // tok_dev, tok_dev).astype(jnp.int32)
    rank = jnp.cumsum(by_block, axis=1) - by_block
    slot = (jnp.arange(count // tok_dev, dtype=jnp.int32)[:, None] * capacity + rank).reshape(-1)
    slots = count // tok_dev * capacity
    pick = ((jnp.arange(slots, dtype=jnp.int32)[:, None] == slot[None, :]) & hit[None, :]).astype(bf16)

    tokens = every[:, :width]
    gate = times_rows(tokens, w_gate[0])
    upper = times_rows(tokens, w_up[0])
    act = (jax.nn.silu(gate) * upper).astype(bf16)
    packed = jnp.dot(pick, act, preferred_element_type=f32).astype(bf16)
    other = swapped(packed, "ctx", 1)
    other = other.reshape(2, 2, slots // 4, other.shape[1])[:, ::-1].reshape(packed.shape)
    other = jnp.dot(pick.T, other, preferred_element_type=f32).astype(bf16)
    units = jnp.concatenate(
        [jnp.where(first, act, other), jnp.where(first, other, act)], axis=1
    )
    projected = times_rows(units, w_down[0])
    share = (projected * coef[:, None]).astype(bf16).reshape(2, count // 2, -1)

    columns = share.shape[2]
    total = share[0].astype(f32) + swapped(share[1], "exp", 1).astype(f32)
    total = total.reshape(2, 2, unit, columns)
    total = total[:, 0] + swapped(total[:, 1].astype(bf16), "exp", 2).astype(f32)
    total = total.reshape(2, line, tok_dev, columns)
    parts = [moved(total[:, d].astype(bf16), line - d) for d in range(1, line)]
    total = total[:, 0] + sum(part.astype(f32) for part in parts)
    total = total.astype(bf16)
    far = swapped(total[1], "ctx", 1)
    near = total[0]
    mixed = jnp.concatenate(
        [jnp.where(first, near, far), jnp.where(first, far, near)], axis=1
    )
    return (attention(queries, latents, earlier_kv), mixed[None])


def on_device_slots(hidden, queries, latents, expert_ids, route_weight, w_gate, w_up, w_down):
    tok_att = latents.shape[0]
    heads_dev = queries.shape[1] // (LATENT + ROPE)
    tok_dev = hidden.shape[1]
    width = hidden.shape[2]
    topk = expert_ids.shape[2]
    experts = lax.axis_size("exp")
    groups = lax.axis_size("ctx")
    capacity = min(tok_dev, max(2, 3 * topk * tok_dev // (2 * experts)))
    slots = experts * capacity
    earlier_kv = shifted(latents, "ctx", 1)
    keys = jnp.concatenate([earlier_kv, latents], axis=0)
    query_rows = queries.reshape(tok_att, heads_dev, LATENT + ROPE)
    scores = jnp.einsum("thc,kc->htk", query_rows, keys, preferred_element_type=jnp.float32) * SCALE
    row_pos = jnp.arange(tok_att, dtype=jnp.int32)
    key_pos = jnp.arange(2 * tok_att, dtype=jnp.int32)
    seen_own = (key_pos[None, :] >= tok_att) & (key_pos[None, :] - tok_att <= row_pos[:, None])
    seen_prev = (key_pos[None, :] < tok_att) & (lax.axis_index("ctx") > 0)
    scores = jnp.where((seen_own | seen_prev)[None, :, :], scores, jnp.float32(-1e30))
    top = jnp.max(scores, axis=-1, keepdims=True)
    expo = jnp.exp(scores - top)
    probs = (expo / jnp.sum(expo, axis=-1, keepdims=True)).astype(jnp.bfloat16)
    mixed_heads = jnp.einsum(
        "htk,kc->thc", probs, keys[:, :LATENT], preferred_element_type=jnp.float32
    )
    attended = mixed_heads.astype(jnp.bfloat16).reshape(tok_att, heads_dev * LATENT)
    tokens = hidden[0]
    picks = expert_ids[0]
    pick_weight = route_weight[0].reshape(-1)
    tok_hot = token_table(tok_dev, topk)
    slot_hot = place_picks(picks, experts, capacity)
    gate_w = w_gate[0]
    up_w = w_up[0]
    down_w = w_down[0]
    send_matrix = jnp.dot(slot_hot.T, tok_hot).astype(jnp.bfloat16)
    outgoing = jnp.dot(send_matrix, tokens, preferred_element_type=jnp.float32).astype(jnp.bfloat16)
    outgoing = outgoing.reshape(experts, capacity, width)
    arrived = lax.all_to_all(outgoing, "exp", split_axis=0, concat_axis=0, tiled=True)
    piece = lax.all_gather(arrived.reshape(slots, width), "ctx", axis=0, tiled=True)
    gate = times_rows(piece, gate_w)
    upper = times_rows(piece, up_w)
    hidden_units = (jax.nn.silu(gate) * upper).astype(jnp.bfloat16)
    projected = times_rows(lax.all_gather(hidden_units, "ctx", axis=1, tiled=True), down_w)
    columns = projected.astype(jnp.bfloat16).reshape(groups, experts, capacity, down_w.shape[0])
    by_block = lax.all_to_all(columns, "ctx", split_axis=0, concat_axis=3, tiled=True)
    returned = lax.all_to_all(by_block, "exp", split_axis=1, concat_axis=1, tiled=True)
    combine_matrix = jnp.dot(
        slot_hot.T, tok_hot * pick_weight[:, None], precision=lax.Precision.HIGHEST
    )
    back_rows = returned.reshape(slots, width).astype(jnp.float32)
    mixed = jnp.dot(combine_matrix.T, back_rows, precision=lax.Precision.HIGHEST).astype(
        jnp.bfloat16
    )
    return (attended, mixed[None])


def solution(mesh):
    experts, groups = mesh.shape["exp"], mesh.shape["ctx"]
    whole = groups == 2 and experts % 4 == 0 and experts <= 16
    on_device = on_device_gathered if whole else on_device_slots
    placed = (
        P("exp", "ctx", None),
        P("ctx", "exp"),
        P("ctx", None),
        P("exp", "ctx", None),
        P("exp", "ctx", None),
        P("exp", "ctx", None),
        P("exp", "ctx", None),
        P("exp", "ctx", None),
    )
    return jax.shard_map(
        on_device,
        mesh=mesh,
        in_specs=placed,
        out_specs=(P("ctx", "exp"), P("exp", "ctx", None)),
        check_vma=False,
    )
```

```python
import jax
import jax.numpy as jnp
from jax import lax
from jax.experimental import pallas as pl
from jax.experimental.pallas import tpu as pltpu
from jax.sharding import PartitionSpec as P

LATENT = 512
ROPE = 64


SCALE = 0.07216878364870322


def shifted(block, axis, distance):
    devices = range(lax.axis_size(axis))
    route = [(i - distance, i) for i in devices if i - distance in devices]
    return lax.ppermute(block, axis, route)


def place_picks(picks, experts, capacity):
    flat = picks.reshape(-1)
    onehot = (flat[:, None] == jnp.arange(experts, dtype=jnp.int32)[None, :]).astype(jnp.int32)
    earlier = jnp.cumsum(onehot, axis=0) - onehot
    rank = jnp.sum(earlier * onehot, axis=1)
    target = flat * capacity + rank
    return (target[:, None] == jnp.arange(experts * capacity, dtype=jnp.int32)[None, :]).astype(
        jnp.float32
    )


def token_table(tok_count, topk):
    owner = jnp.arange(tok_count * topk, dtype=jnp.int32) // topk
    return (owner[:, None] == jnp.arange(tok_count, dtype=jnp.int32)[None, :]).astype(jnp.float32)


def times_rows(left, right):
    return lax.dot_general(
        left, right, (((1,), (1,)), ((), ())), preferred_element_type=jnp.float32
    )


def swapped(block, axis, bit):
    return lax.ppermute(block, axis, [(i, i ^ bit) for i in range(lax.axis_size(axis))])


def moved(block, steps):
    count = lax.axis_size("exp")
    return lax.ppermute(block, "exp", [(i, (i + 4 * steps) % count) for i in range(count)])


def paired(block, partner):
    count = lax.axis_size("exp")
    both = lax.axis_size("ctx") * count
    route = []
    for i in range(both):
        ctx, exp = partner(i // count, i % count)
        route.append((i, ctx * count + exp))
    return lax.ppermute(block, ("ctx", "exp"), route)


def over_y(ctx, exp):
    return ctx, exp ^ 2


def over_x(ctx, exp):
    return 1 - ctx, exp


def y_then_x(ctx, exp):
    return over_x(ctx, exp) if exp % 2 else over_y(ctx, exp)


def x_then_y(ctx, exp):
    return over_y(ctx, exp) if exp % 2 else over_x(ctx, exp)


def times_rows_in(left, right):
    return lax.dot_general(
        left, right, (((1,), (1,)), ((), ())), preferred_element_type=jnp.float32
    )


def in_vmem(array):
    return pltpu.with_memory_space_constraint(array, pltpu.VMEM)


def in_hbm(array):
    return pltpu.with_memory_space_constraint(array, pltpu.HBM)


def local_kernel(body, ins, outs, scratch, name, cost=None):
    kinds = {"vmem": pltpu.VMEM, "hbm": pl.ANY}
    place = {"vmem": in_vmem, "hbm": in_hbm}
    made = [
        pltpu.VMEM(shape, dtype) if kind == "vmem" else jax.ShapeDtypeStruct(shape, dtype)
        for shape, dtype, kind in outs
    ]
    return pl.pallas_call(
        body,
        in_specs=[pl.BlockSpec(memory_space=kinds[kind]) for _, kind in ins],
        out_specs=[pl.BlockSpec(memory_space=kinds[kind]) for _, _, kind in outs],
        out_shape=made,
        scratch_shapes=scratch,
        compiler_params=pltpu.CompilerParams(vmem_limit_bytes=20 * 1024 * 1024),
        cost_estimate=cost,
        name=name,
    )(*[place[kind](array) for array, kind in ins])


def start_copies(pairs, sems, pieces):
    copies = []
    for number, (source, target) in enumerate(pairs):
        step = target.shape[0] // pieces
        for piece in range(pieces):
            span = pl.ds(piece * step, step)
            copy = pltpu.make_async_copy(
                source.at[span, :], target.at[span, :], sems.at[number * pieces + piece]
            )
            copy.start()
            copies.append(copy)
    return copies


PIECES = 4


def rows_kernel(tokens_in, names_in, weights_in, out, tokens, names, weights, sems, *, half, topk):
    copies = [
        pltpu.make_async_copy(source, target, sems.at[number])
        for number, (source, target) in enumerate(
            ((tokens_in, tokens), (names_in, names), (weights_in, weights))
        )
    ]
    for copy in copies:
        copy.start()
    for copy in copies:
        copy.wait()
    count = tokens.shape[0]
    width = tokens.shape[1]
    out[:, :half] = tokens[:, :half]
    out[:, half + 128 :] = tokens[:, half:width]
    lane = lax.broadcasted_iota(jnp.int32, (count, 128), 1)
    same = lax.broadcasted_iota(jnp.int32, (count, count), 0) == lax.broadcasted_iota(
        jnp.int32, (count, count), 1
    )

    def column(row):
        return jnp.sum(
            jnp.where(same, jnp.broadcast_to(row, same.shape), 0.0), axis=1, keepdims=True
        )

    note = jnp.zeros((count, 128), jnp.float32)
    for k in range(topk):
        name = column(names[k].astype(jnp.float32))
        weight = column(weights[k])
        low = weight - weight.astype(jnp.bfloat16).astype(jnp.float32)
        for value, at in ((name, k), (weight, topk + k), (low, 2 * topk + k)):
            note = jnp.where(lane == at, value, note)
    out[:, half : half + 128] = note.astype(jnp.bfloat16)


def fetch_kernel(after, gate_w, up_w, gate_out, up_out, sems):
    half = gate_out.shape[1]
    pairs = [(gate_w.at[:, :half], gate_out), (up_w.at[:, :half], up_out)]
    for copy in start_copies(pairs, sems, PIECES):
        copy.wait()


def stack_kernel(*refs, cuts):
    ins, outs = refs[: len(refs) - len(cuts)], refs[len(refs) - len(cuts) :]
    for out, (low, high) in zip(outs, cuts):
        if ins[0].shape[0] % 16 == 0:
            at = 0
            for ref in ins:
                out[at : at + ref.shape[0], :] = ref[:, low:high]
                at += ref.shape[0]
        else:
            rows = [ref[:, low:high].astype(jnp.float32) for ref in ins]
            out[...] = jnp.concatenate(rows, axis=0).astype(out.dtype)


def attention_kernel(
    after, earlier, queries_in, latents_in, gate_all, up_all,
    attended, gate_next, up_next, queries, latents, even, odd, mixed, sems, copy_sems,
):
    width, rows = latents.shape
    half = gate_next.shape[1]
    pad = even.shape[0] - width
    loads = [
        pltpu.make_async_copy(queries_in, queries, sems.at[0]),
        pltpu.make_async_copy(latents_in, latents, sems.at[1]),
    ]
    for copy in loads:
        copy.start()
    pairs = [(gate_all.at[:, half:], gate_next), (up_all.at[:, half:], up_next)]
    copies = start_copies(pairs, copy_sems, PIECES)
    for copy in loads:
        copy.wait()
    even[width:, :] = jnp.zeros((pad, 2 * rows), jnp.bfloat16)
    odd[:pad, :] = jnp.zeros((pad, 2 * rows), jnp.bfloat16)
    even[:width, :rows] = earlier[...]
    even[:width, rows:] = latents[...]
    odd[pad:, :rows] = earlier[...]
    odd[pad:, rows:] = latents[...]
    row = lax.broadcasted_iota(jnp.int32, (rows, 2 * rows), 0)
    key = lax.broadcasted_iota(jnp.int32, (rows, 2 * rows), 1)
    nearest = jnp.where(lax.axis_index("ctx") > 0, 0, rows)
    seen = (key >= nearest) & (key <= row + rows)
    heads = attended.shape[1] // LATENT
    writes = []
    for head in range(heads):
        start = head * width
        keys, start = (even, start) if start % 128 == 0 else (odd, start - pad)
        scores = jnp.dot(
            queries[:, start : start + width + pad], keys[...], preferred_element_type=jnp.float32
        )
        scores = jnp.where(seen, scores * SCALE, jnp.float32(-1e30))
        expo = jnp.exp(scores - jnp.max(scores, axis=-1, keepdims=True))
        probs = (expo / jnp.sum(expo, axis=-1, keepdims=True)).astype(jnp.bfloat16)
        span = slice(head * LATENT, (head + 1) * LATENT)
        mixed[:, span] = times_rows_in(probs, even[:LATENT, :]).astype(jnp.bfloat16)
        write = pltpu.make_async_copy(mixed.at[:, span], attended.at[:, span], sems.at[2 + head])
        write.start()
        writes.append(write)
    for copy in writes + copies:
        copy.wait()


def assemble(place, core, two_ref, far_ref, two_other_ref, far_other_ref, unit, start=0):
    span = slice(start, start + place.shape[1])
    for lane, two, far in ((0, two_ref, far_ref), (1, two_other_ref, far_other_ref)):
        went_x = core if lane == 0 else 1 - core
        base = lane * 4 * unit
        near = pl.multiple_of(base + (2 - went_x) * unit, unit)
        next_ = pl.multiple_of(base + (1 + went_x) * unit, unit)
        place[base : base + unit, :] = two[:unit, span]
        place[pl.ds(near, unit), :] = two[unit:, span]
        place[pl.ds(next_, unit), :] = far[:unit, span]
        place[base + 3 * unit : base + 4 * unit, :] = far[unit:, span]


def first_kernel(
    two, far, two_other, far_other, gate_w, up_w,
    gate_out, up_out, pick_out, pick_far_out, coef_out,
    tokens, notes, *, unit, tok_dev, capacity, topk,
):
    width = tokens.shape[1]
    rows = tokens.shape[0]
    slots = pick_out.shape[1]
    expert = lax.axis_index("exp")
    assemble(tokens, expert % 2, two, far, two_other, far_other, unit)
    gate_out[...] = times_rows_in(tokens[...], gate_w[...])
    up_out[...] = times_rows_in(tokens[...], up_w[...])

    assemble(notes, expert % 2, two, far, two_other, far_other, unit, width)
    note = notes[...].astype(jnp.float32)
    lane = lax.broadcasted_iota(jnp.int32, note.shape, 1)
    mine = (note == expert.astype(jnp.float32)) & (lane < topk)
    weight = pltpu.roll(note, 128 - topk, 1) + pltpu.roll(note, 128 - 2 * topk, 1)
    coef = jnp.sum(jnp.where(mine, weight, 0.0), axis=1, keepdims=True)
    hit = jnp.sum(mine.astype(jnp.float32), axis=1, keepdims=True)
    shift = tok_dev.bit_length() - 1
    at = lax.broadcasted_iota(jnp.int32, (rows, rows), 0)
    before = lax.broadcasted_iota(jnp.int32, (rows, rows), 1)
    earlier = ((at >> shift) == (before >> shift)) & (before < at)
    hits = jnp.broadcast_to(hit, (rows, slots))
    rank = jnp.dot(
        earlier.astype(jnp.float32).astype(jnp.bfloat16),
        hits.astype(jnp.bfloat16),
        preferred_element_type=jnp.float32,
    ).astype(jnp.int32)
    row = lax.broadcasted_iota(jnp.int32, (rows, slots), 0)
    slot = (row >> shift) * capacity + rank
    group = unit // tok_dev * capacity
    away = ((row >> (unit.bit_length() - 1)) & 1) == 0
    slot_far = slot + jnp.where(away, group, -group)
    column = lax.broadcasted_iota(jnp.int32, (rows, slots), 1)
    pick_out[...] = jnp.where(slot == column, hits, 0.0).astype(jnp.bfloat16)
    pick_far_out[...] = jnp.where(slot_far == column, hits, 0.0).astype(jnp.bfloat16)
    coef_out[...] = jnp.broadcast_to(coef, coef_out.shape)


def second_kernel(
    two, far, two_other, far_other, gate_w, up_w, gate_in, up_in, pick,
    act_out, packed_out, tokens, *, unit, wide,
):
    units = act_out.shape[1]
    assemble(tokens, lax.axis_index("exp") % 2, two, far, two_other, far_other, unit)
    for n in range(0, units, wide):
        span = slice(n, n + wide)
        gate = gate_in[:, span] + times_rows_in(tokens[...], gate_w[span, :])
        upper = up_in[:, span] + times_rows_in(tokens[...], up_w[span, :])
        act = (gate / (1.0 + jnp.exp(-gate)) * upper).astype(jnp.bfloat16)
        act_out[:, span] = act
        packed_out[:, span] = lax.dot_general(
            pick[...], act, (((0,), (0,)), ((), ())), preferred_element_type=jnp.float32
        ).astype(jnp.bfloat16)


def own_kernel(act, down_w, out, down_other, down_own, sems):
    units = act.shape[1]
    ctx = lax.axis_index("ctx")
    own_at = pl.multiple_of(ctx * units, 128)
    other_at = pl.multiple_of((1 - ctx) * units, 128)
    pairs = [
        (down_w.at[:, pl.ds(own_at, units)], down_own),
        (down_w.at[:, pl.ds(other_at, units)], down_other),
    ]
    copies = start_copies(pairs, sems, PIECES)
    tall = out.shape[1] // PIECES
    for piece in range(PIECES):
        copies[piece].wait()
        span = slice(piece * tall, (piece + 1) * tall)
        out[:, span] = times_rows_in(act[...], down_own[span, :])
    for copy in copies[PIECES:]:
        copy.wait()


def other_kernel(packed, pick, coef, down_w, own, keep, give, act, *, tall, start):
    act[...] = jnp.dot(pick[...], packed[...], preferred_element_type=jnp.float32).astype(
        jnp.bfloat16
    )
    half = keep.shape[0]
    for n in range(0, keep.shape[1], tall):
        span = slice(start + n, start + n + tall)
        projected = own[:, span] + times_rows_in(act[...], down_w[span, :])
        projected = projected * coef[:, :1]
        keep[:, n : n + tall] = projected[:half].astype(jnp.bfloat16)
        give[:, n : n + tall] = projected[half:].astype(jnp.bfloat16)


def on_device_gathered(
    hidden, queries, latents, expert_ids, route_weight, w_gate, w_up, w_down
):
    tok_dev = hidden.shape[1]
    width = hidden.shape[2]
    topk = expert_ids.shape[2]
    units = w_gate.shape[1]
    columns = w_down.shape[1]
    tok_att, key_width = latents.shape
    heads_dev = queries.shape[1] // key_width
    experts = lax.axis_size("exp")
    line = experts // 4
    capacity = min(tok_dev, max(2, 3 * topk * tok_dev // (2 * experts)))
    half = width // 2
    unit = line * tok_dev
    count = 8 * unit
    slots = count // tok_dev * capacity
    bf16, f32 = jnp.bfloat16, jnp.float32
    first = lax.axis_index("ctx") == 0
    copy_sems = pltpu.SemaphoreType.DMA((2 * PIECES,))

    (rows,) = local_kernel(
        lambda *refs: rows_kernel(*refs, half=half, topk=topk),
        [
            (hidden[0], "hbm"),
            (jnp.transpose(expert_ids, (2, 0, 1)), "hbm"),
            (jnp.transpose(route_weight, (2, 0, 1)), "hbm"),
        ],
        [((tok_dev, width + 128), bf16, "vmem")],
        [
            pltpu.VMEM((tok_dev, width), bf16),
            pltpu.VMEM((topk, 1, tok_dev), jnp.int32),
            pltpu.VMEM((topk, 1, tok_dev), f32),
            pltpu.SemaphoreType.DMA((3,)),
        ],
        "rows",
    )
    along = [rows] + [moved(rows, d) for d in range(1, line)]
    earlier_kv = swapped(latents.T, "ctx", 1)
    gate_1, up_1 = local_kernel(
        fetch_kernel,
        [(rows, "vmem"), (w_gate[0], "hbm"), (w_up[0], "hbm")],
        [((units, half), bf16, "vmem")] * 2,
        [copy_sems],
        "fetch",
    )
    *along, earlier_kv, gate_1, up_1 = lax.optimization_barrier((*along, earlier_kv, gate_1, up_1))
    cuts = ((0, half + 128), (half + 128, width + 128))
    nears = local_kernel(
        lambda *refs: stack_kernel(*refs, cuts=cuts),
        [(row, "vmem") for row in along],
        [((unit, high - low), bf16, "vmem") for low, high in cuts],
        [],
        "stack_line",
    )
    pad = -key_width % 128
    attended, gate_2, up_2 = local_kernel(
        attention_kernel,
        [
            (nears[1], "vmem"), (earlier_kv, "vmem"), (queries, "hbm"), (latents.T, "hbm"),
            (w_gate[0], "hbm"), (w_up[0], "hbm"),
        ],
        [((tok_att, heads_dev * LATENT), bf16, "hbm")] + [((units, half), bf16, "vmem")] * 2,
        [
            pltpu.VMEM((tok_att, heads_dev * key_width), bf16),
            pltpu.VMEM((key_width, tok_att), bf16),
            pltpu.VMEM((key_width + pad, 2 * tok_att), bf16),
            pltpu.VMEM((key_width + pad, 2 * tok_att), bf16),
            pltpu.VMEM((tok_att, heads_dev * LATENT), bf16),
            pltpu.SemaphoreType.DMA((2 + heads_dev,)),
            copy_sems,
        ],
        "attention",
    )
    passed = [paired(near, y_then_x) for near in nears]
    passed[0], gate_2, up_2 = lax.optimization_barrier((passed[0], gate_2, up_2))
    pieces = []
    for near, got in zip(nears, passed):
        shape = (2 * unit, near.shape[1])
        (two,) = local_kernel(
            lambda *refs, cut=near.shape[1]: stack_kernel(*refs, cuts=((0, cut),)),
            [(near, "vmem"), (got, "vmem")],
            [(shape, bf16, "vmem")],
            [],
            "stack_two",
        )
        far = paired(two, x_then_y)
        group = (two, far, swapped(two, "exp", 1), swapped(far, "exp", 1))
        pieces.append([(piece, "vmem") for piece in group])

    gate, up, pick, pick_far, coef = local_kernel(
        lambda *refs: first_kernel(
            *refs, unit=unit, tok_dev=tok_dev, capacity=capacity, topk=topk
        ),
        [*pieces[0], (gate_1, "vmem"), (up_1, "vmem")],
        [((count, units), f32, "vmem")] * 2
        + [((count, slots), bf16, "vmem")] * 2
        + [((count, 128), f32, "vmem")],
        [pltpu.VMEM((count, half), bf16), pltpu.VMEM((count, 128), bf16)],
        "gate_up_first",
    )
    act, packed = local_kernel(
        lambda *refs: second_kernel(*refs, unit=unit, wide=256),
        [
            *pieces[1], (gate_2, "vmem"), (up_2, "vmem"),
            (gate, "vmem"), (up, "vmem"), (pick, "vmem"),
        ],
        [((count, units), bf16, "vmem"), ((slots, units), bf16, "vmem")],
        [pltpu.VMEM((count, half), bf16)],
        "gate_up_second",
    )
    other = swapped(packed, "ctx", 1)
    own, down_other = local_kernel(
        own_kernel,
        [(act, "vmem"), (w_down[0], "hbm")],
        [((count, columns), f32, "vmem"), ((columns, units), bf16, "vmem")],
        [pltpu.VMEM((columns, units), bf16), copy_sems],
        "down_own",
    )
    sums = []
    part = columns // 2
    for start in (0, part):
        keep, give = local_kernel(
            lambda *refs, start=start: other_kernel(*refs, tall=256, start=start),
            [
                (other, "vmem"), (pick_far, "vmem"), (coef, "vmem"),
                (down_other, "vmem"), (own, "vmem"),
            ],
            [((count // 2, part), bf16, "vmem")] * 2,
            [pltpu.VMEM((count, units), bf16)],
            "down_other",
        )
        total = keep.astype(f32) + swapped(give, "exp", 1).astype(f32)
        total = total[: 2 * unit] + swapped(total[2 * unit :].astype(bf16), "exp", 2).astype(f32)
        sums.append(total)
    total = jnp.concatenate(sums, axis=1).reshape(2, line, tok_dev, columns)
    parts = [moved(total[:, d].astype(bf16), line - d) for d in range(1, line)]
    total = total[:, 0] + sum(part.astype(f32) for part in parts)
    total = total.astype(bf16)
    far = swapped(total[1], "ctx", 1)
    near = total[0]
    mixed = jnp.concatenate(
        [jnp.where(first, near, far), jnp.where(first, far, near)], axis=1
    )
    return (attended, mixed[None])


def on_device_slots(hidden, queries, latents, expert_ids, route_weight, w_gate, w_up, w_down):
    tok_att = latents.shape[0]
    heads_dev = queries.shape[1] // (LATENT + ROPE)
    tok_dev = hidden.shape[1]
    width = hidden.shape[2]
    topk = expert_ids.shape[2]
    experts = lax.axis_size("exp")
    groups = lax.axis_size("ctx")
    capacity = min(tok_dev, max(2, 3 * topk * tok_dev // (2 * experts)))
    slots = experts * capacity
    earlier_kv = shifted(latents, "ctx", 1)
    keys = jnp.concatenate([earlier_kv, latents], axis=0)
    query_rows = queries.reshape(tok_att, heads_dev, LATENT + ROPE)
    scores = jnp.einsum("thc,kc->htk", query_rows, keys, preferred_element_type=jnp.float32) * SCALE
    row_pos = jnp.arange(tok_att, dtype=jnp.int32)
    key_pos = jnp.arange(2 * tok_att, dtype=jnp.int32)
    seen_own = (key_pos[None, :] >= tok_att) & (key_pos[None, :] - tok_att <= row_pos[:, None])
    seen_prev = (key_pos[None, :] < tok_att) & (lax.axis_index("ctx") > 0)
    scores = jnp.where((seen_own | seen_prev)[None, :, :], scores, jnp.float32(-1e30))
    top = jnp.max(scores, axis=-1, keepdims=True)
    expo = jnp.exp(scores - top)
    probs = (expo / jnp.sum(expo, axis=-1, keepdims=True)).astype(jnp.bfloat16)
    mixed_heads = jnp.einsum(
        "htk,kc->thc", probs, keys[:, :LATENT], preferred_element_type=jnp.float32
    )
    attended = mixed_heads.astype(jnp.bfloat16).reshape(tok_att, heads_dev * LATENT)
    tokens = hidden[0]
    picks = expert_ids[0]
    pick_weight = route_weight[0].reshape(-1)
    tok_hot = token_table(tok_dev, topk)
    slot_hot = place_picks(picks, experts, capacity)
    gate_w = w_gate[0]
    up_w = w_up[0]
    down_w = w_down[0]
    send_matrix = jnp.dot(slot_hot.T, tok_hot).astype(jnp.bfloat16)
    outgoing = jnp.dot(send_matrix, tokens, preferred_element_type=jnp.float32).astype(jnp.bfloat16)
    outgoing = outgoing.reshape(experts, capacity, width)
    arrived = lax.all_to_all(outgoing, "exp", split_axis=0, concat_axis=0, tiled=True)
    piece = lax.all_gather(arrived.reshape(slots, width), "ctx", axis=0, tiled=True)
    gate = times_rows(piece, gate_w)
    upper = times_rows(piece, up_w)
    hidden_units = (jax.nn.silu(gate) * upper).astype(jnp.bfloat16)
    projected = times_rows(lax.all_gather(hidden_units, "ctx", axis=1, tiled=True), down_w)
    columns = projected.astype(jnp.bfloat16).reshape(groups, experts, capacity, down_w.shape[0])
    by_block = lax.all_to_all(columns, "ctx", split_axis=0, concat_axis=3, tiled=True)
    returned = lax.all_to_all(by_block, "exp", split_axis=1, concat_axis=1, tiled=True)
    combine_matrix = jnp.dot(
        slot_hot.T, tok_hot * pick_weight[:, None], precision=lax.Precision.HIGHEST
    )
    back_rows = returned.reshape(slots, width).astype(jnp.float32)
    mixed = jnp.dot(combine_matrix.T, back_rows, precision=lax.Precision.HIGHEST).astype(
        jnp.bfloat16
    )
    return (attended, mixed[None])


def solution(mesh):
    experts, groups = mesh.shape["exp"], mesh.shape["ctx"]
    whole = groups == 2 and experts % 4 == 0 and experts <= 16
    on_device = on_device_gathered if whole else on_device_slots
    placed = (
        P("exp", "ctx", None),
        P("ctx", "exp"),
        P("ctx", None),
        P("exp", "ctx", None),
        P("exp", "ctx", None),
        P("exp", "ctx", None),
        P("exp", "ctx", None),
        P("exp", "ctx", None),
    )
    return jax.shard_map(
        on_device,
        mesh=mesh,
        in_specs=placed,
        out_specs=(P("ctx", "exp"), P("exp", "ctx", None)),
        check_vma=False,
    )
```

```python
import jax
import jax.numpy as jnp
from jax import lax
from jax.experimental import pallas as pl
from jax.experimental.pallas import tpu as pltpu
from jax.sharding import PartitionSpec as P

LATENT = 512
ROPE = 64


SCALE = 0.07216878364870322


def shifted(block, axis, distance):
    devices = range(lax.axis_size(axis))
    route = [(i - distance, i) for i in devices if i - distance in devices]
    return lax.ppermute(block, axis, route)


def place_picks(picks, experts, capacity):
    flat = picks.reshape(-1)
    onehot = (flat[:, None] == jnp.arange(experts, dtype=jnp.int32)[None, :]).astype(jnp.int32)
    earlier = jnp.cumsum(onehot, axis=0) - onehot
    rank = jnp.sum(earlier * onehot, axis=1)
    target = flat * capacity + rank
    return (target[:, None] == jnp.arange(experts * capacity, dtype=jnp.int32)[None, :]).astype(
        jnp.float32
    )


def token_table(tok_count, topk):
    owner = jnp.arange(tok_count * topk, dtype=jnp.int32) // topk
    return (owner[:, None] == jnp.arange(tok_count, dtype=jnp.int32)[None, :]).astype(jnp.float32)


def times_rows(left, right):
    return lax.dot_general(
        left, right, (((1,), (1,)), ((), ())), preferred_element_type=jnp.float32
    )


def swapped(block, axis, bit):
    return lax.ppermute(block, axis, [(i, i ^ bit) for i in range(lax.axis_size(axis))])


def along_line(block, steps):
    return lax.ppermute(
        block, "exp", [(i, i ^ (4 * steps)) for i in range(lax.axis_size("exp"))]
    )


def paired(block, partner):
    count = lax.axis_size("exp")
    both = lax.axis_size("ctx") * count
    route = []
    for i in range(both):
        ctx, exp = partner(i // count, i % count)
        route.append((i, ctx * count + exp))
    return lax.ppermute(block, ("ctx", "exp"), route)


def over_y(ctx, exp):
    return ctx, exp ^ 2


def over_x(ctx, exp):
    return 1 - ctx, exp


def y_then_x(ctx, exp):
    return over_x(ctx, exp) if exp % 2 else over_y(ctx, exp)


def x_then_y(ctx, exp):
    return over_y(ctx, exp) if exp % 2 else over_x(ctx, exp)


def times_rows_in(left, right):
    return lax.dot_general(
        left, right, (((1,), (1,)), ((), ())), preferred_element_type=jnp.float32
    )


def in_vmem(array):
    return pltpu.with_memory_space_constraint(array, pltpu.VMEM)


def in_hbm(array):
    return pltpu.with_memory_space_constraint(array, pltpu.HBM)


def local_kernel(body, ins, outs, scratch, name):
    kinds = {"vmem": pltpu.VMEM, "hbm": pl.ANY, "result": pltpu.VMEM}
    place = {"vmem": in_vmem, "hbm": in_hbm}
    made = [
        pltpu.VMEM(shape, dtype) if kind == "vmem" else jax.ShapeDtypeStruct(shape, dtype)
        for shape, dtype, kind in outs
    ]
    return pl.pallas_call(
        body,
        in_specs=[pl.BlockSpec(memory_space=kinds[kind]) for _, kind in ins],
        out_specs=[pl.BlockSpec(memory_space=kinds[kind]) for _, _, kind in outs],
        out_shape=made,
        scratch_shapes=scratch,
        compiler_params=pltpu.CompilerParams(vmem_limit_bytes=20 * 1024 * 1024),
        cost_estimate=pl.CostEstimate(flops=0, bytes_accessed=0, transcendentals=0),
        name=name,
    )(*[place[kind](array) for array, kind in ins])


def start_copies(pairs, sems, pieces):
    copies = []
    for number, (source, target) in enumerate(pairs):
        step = target.shape[0] // pieces
        for piece in range(pieces):
            span = pl.ds(piece * step, step)
            copy = pltpu.make_async_copy(
                source.at[span, :], target.at[span, :], sems.at[number * pieces + piece]
            )
            copy.start()
            copies.append(copy)
    return copies


PIECES = 4


def rows_kernel(tokens_in, names_in, weights_in, out, tokens, names, weights, sems, *, half, topk):
    copies = [
        pltpu.make_async_copy(source, target, sems.at[number])
        for number, (source, target) in enumerate(
            ((tokens_in, tokens), (names_in, names), (weights_in, weights))
        )
    ]
    for copy in copies:
        copy.start()
    for copy in copies:
        copy.wait()
    count = tokens.shape[0]
    width = tokens.shape[1]
    out[:, :half] = tokens[:, :half]
    out[:, half + 128 :] = tokens[:, half:width]
    lane = lax.broadcasted_iota(jnp.int32, (count, 128), 1)
    same = lax.broadcasted_iota(jnp.int32, (count, count), 0) == lax.broadcasted_iota(
        jnp.int32, (count, count), 1
    )

    def column(row):
        return jnp.sum(
            jnp.where(same, jnp.broadcast_to(row, same.shape), 0.0), axis=1, keepdims=True
        )

    note = jnp.zeros((count, 128), jnp.float32)
    for k in range(topk):
        name = column(names[k].astype(jnp.float32))
        weight = column(weights[k])
        low = weight - weight.astype(jnp.bfloat16).astype(jnp.float32)
        for value, at in ((name, k), (weight, topk + k), (low, 2 * topk + k)):
            note = jnp.where(lane == at, value, note)
    out[:, half : half + 128] = note.astype(jnp.bfloat16)


def fetch_kernel(after, *refs, start):
    count = len(refs) // 2
    ins, outs, sems = refs[:count], refs[count:-1], refs[-1]
    pairs = [(a.at[:, start : start + b.shape[1]], b) for a, b in zip(ins[:2], outs[:2])]
    if count > 2:
        width = outs[2].shape[1]
        own_at = pl.multiple_of(lax.axis_index("ctx") * width, 128)
        pairs.append((ins[2].at[:, pl.ds(own_at, width)], outs[2]))
    for copy in start_copies(pairs, sems, PIECES):
        copy.wait()


def stack_kernel(*refs, cuts):
    ins, outs = refs[: len(refs) - len(cuts)], refs[len(refs) - len(cuts) :]
    for out, (low, high) in zip(outs, cuts):
        if ins[0].shape[0] % 16 == 0:
            at = 0
            for ref in ins:
                out[at : at + ref.shape[0], :] = ref[:, low:high]
                at += ref.shape[0]
        else:
            rows = [ref[:, low:high].astype(jnp.float32) for ref in ins]
            out[...] = jnp.concatenate(rows, axis=0).astype(out.dtype)


def attention_kernel(
    after, earlier, queries_in, latents_in, attended, queries, latents, even, odd, mixed, sems
):
    width, rows = latents.shape
    pad = even.shape[0] - width
    loads = [
        pltpu.make_async_copy(queries_in, queries, sems.at[0]),
        pltpu.make_async_copy(latents_in, latents, sems.at[1]),
    ]
    for copy in loads:
        copy.start()
    for copy in loads:
        copy.wait()
    even[width:, :] = jnp.zeros((pad, 2 * rows), jnp.bfloat16)
    odd[:pad, :] = jnp.zeros((pad, 2 * rows), jnp.bfloat16)
    even[:width, :rows] = earlier[...]
    even[:width, rows:] = latents[...]
    odd[pad:, :rows] = earlier[...]
    odd[pad:, rows:] = latents[...]
    row = lax.broadcasted_iota(jnp.int32, (rows, 2 * rows), 0)
    key = lax.broadcasted_iota(jnp.int32, (rows, 2 * rows), 1)
    nearest = jnp.where(lax.axis_index("ctx") > 0, 0, rows)
    seen = (key >= nearest) & (key <= row + rows)
    heads = attended.shape[1] // LATENT
    writes = []
    for head in range(heads):
        start = head * width
        keys, start = (even, start) if start % 128 == 0 else (odd, start - pad)
        scores = jnp.dot(
            queries[:, start : start + width + pad], keys[...], preferred_element_type=jnp.float32
        )
        scores = jnp.where(seen, scores * SCALE, jnp.float32(-1e30))
        expo = jnp.exp(scores - jnp.max(scores, axis=-1, keepdims=True))
        probs = (expo / jnp.sum(expo, axis=-1, keepdims=True)).astype(jnp.bfloat16)
        span = slice(head * LATENT, (head + 1) * LATENT)
        mixed[:, span] = times_rows_in(probs, even[:LATENT, :]).astype(jnp.bfloat16)
        write = pltpu.make_async_copy(mixed.at[:, span], attended.at[:, span], sems.at[2 + head])
        write.start()
        writes.append(write)
    for copy in writes:
        copy.wait()


def assemble(place, core, two_ref, far_ref, two_other_ref, far_other_ref, unit, start=0):
    span = slice(start, start + place.shape[1])
    for lane, two, far in ((0, two_ref, far_ref), (1, two_other_ref, far_other_ref)):
        went_x = core if lane == 0 else 1 - core
        base = lane * 4 * unit
        near = pl.multiple_of(base + (2 - went_x) * unit, unit)
        next_ = pl.multiple_of(base + (1 + went_x) * unit, unit)
        place[base : base + unit, :] = two[:unit, span]
        place[pl.ds(near, unit), :] = two[unit:, span]
        place[pl.ds(next_, unit), :] = far[:unit, span]
        place[base + 3 * unit : base + 4 * unit, :] = far[unit:, span]


def first_kernel(
    two, far, two_other, far_other, gate_w, up_w,
    gate_out, up_out, pick_out, pick_far_out, coef_out,
    tokens, notes, *, unit, tok_dev, capacity, topk,
):
    width = tokens.shape[1]
    rows = tokens.shape[0]
    slots = pick_out.shape[1]
    expert = lax.axis_index("exp")
    assemble(tokens, expert % 2, two, far, two_other, far_other, unit)
    gate_out[...] = times_rows_in(tokens[...], gate_w[...])
    up_out[...] = times_rows_in(tokens[...], up_w[...])

    assemble(notes, expert % 2, two, far, two_other, far_other, unit, width)
    note = notes[...].astype(jnp.float32)
    lane = lax.broadcasted_iota(jnp.int32, note.shape, 1)
    mine = (note == expert.astype(jnp.float32)) & (lane < topk)
    weight = pltpu.roll(note, 128 - topk, 1) + pltpu.roll(note, 128 - 2 * topk, 1)
    coef = jnp.sum(jnp.where(mine, weight, 0.0), axis=1, keepdims=True)
    hit = jnp.sum(mine.astype(jnp.float32), axis=1, keepdims=True)
    shift = tok_dev.bit_length() - 1
    at = lax.broadcasted_iota(jnp.int32, (rows, rows), 0)
    before = lax.broadcasted_iota(jnp.int32, (rows, rows), 1)
    earlier = ((at >> shift) == (before >> shift)) & (before < at)
    hits = jnp.broadcast_to(hit, (rows, slots))
    rank = jnp.dot(
        earlier.astype(jnp.float32).astype(jnp.bfloat16),
        hits.astype(jnp.bfloat16),
        preferred_element_type=jnp.float32,
    ).astype(jnp.int32)
    row = lax.broadcasted_iota(jnp.int32, (rows, slots), 0)
    slot = (row >> shift) * capacity + rank
    group = unit // tok_dev * capacity
    away = ((row >> (unit.bit_length() - 1)) & 1) == 0
    slot_far = slot + jnp.where(away, group, -group)
    column = lax.broadcasted_iota(jnp.int32, (rows, slots), 1)
    pick_out[...] = jnp.where(slot == column, hits, 0.0).astype(jnp.bfloat16)
    pick_far_out[...] = jnp.where(slot_far == column, hits, 0.0).astype(jnp.bfloat16)
    coef_out[...] = jnp.broadcast_to(coef, coef_out.shape)


def finish_units(tokens, gate_w, up_w, gate_in, up_in, pick, act_out, packed_out, start):
    span = slice(start, start + act_out.shape[1])
    gate = gate_in[:, span] + times_rows_in(tokens[...], gate_w[span, :])
    upper = up_in[:, span] + times_rows_in(tokens[...], up_w[span, :])
    act = (gate / (1.0 + jnp.exp(-gate)) * upper).astype(jnp.bfloat16)
    act_out[...] = act
    packed_out[...] = lax.dot_general(
        pick[...], act, (((0,), (0,)), ((), ())), preferred_element_type=jnp.float32
    ).astype(jnp.bfloat16)


def second_kernel(
    two, far, two_other, far_other, gate_w, up_w, gate_in, up_in, pick,
    act_out, packed_out, tokens, *, unit,
):
    assemble(tokens, lax.axis_index("exp") % 2, two, far, two_other, far_other, unit)
    finish_units(tokens, gate_w, up_w, gate_in, up_in, pick, act_out, packed_out, 0)


def third_kernel(tokens, gate_w, up_w, gate_in, up_in, pick, act_out, packed_out, *, start):
    finish_units(tokens, gate_w, up_w, gate_in, up_in, pick, act_out, packed_out, start)


def own_kernel(act_a, act_b, down_own, down_w, out, down_other, sems):
    units = down_own.shape[1]
    few = act_a.shape[1]
    other_at = pl.multiple_of((1 - lax.axis_index("ctx")) * units, 128)
    copies = start_copies([(down_w.at[:, pl.ds(other_at, units)], down_other)], sems, PIECES)
    tall = out.shape[1] // 5 if out.shape[1] % 640 == 0 else out.shape[1]
    for n in range(0, out.shape[1], tall):
        span = slice(n, n + tall)
        out[:, span] = times_rows_in(act_a[...], down_own[span, :few]) + times_rows_in(
            act_b[...], down_own[span, few:]
        )
    for copy in copies:
        copy.wait()


def other_kernel(packed_a, packed_b, pick, coef, down_w, own, keep, give, act, *, start):
    few = packed_a.shape[1]
    for packed, span in ((packed_a, slice(0, few)), (packed_b, slice(few, act.shape[1]))):
        act[:, span] = jnp.dot(
            pick[...], packed[...], preferred_element_type=jnp.float32
        ).astype(jnp.bfloat16)
    half, part = keep.shape
    tall = part // 5 if part % 5 == 0 else part
    for n in range(0, part, tall):
        span = slice(start + n, start + n + tall)
        projected = own[:, span] + times_rows_in(act[...], down_w[span, :])
        projected = projected * coef[:, :1]
        keep[:, n : n + tall] = projected[:half].astype(jnp.bfloat16)
        give[:, n : n + tall] = projected[half:].astype(jnp.bfloat16)


def spread_kernel(keep, got, send, stay):
    core = lax.axis_index("exp") % 2
    unit = keep.shape[0] // 4

    def total(block):
        span = slice(block * unit, (block + 1) * unit)
        return keep[span, :].astype(jnp.float32) + got[span, :].astype(jnp.float32)

    for this, (stays, sends) in enumerate((((0, 1), (2, 3)), ((0, 2), (1, 3)))):

        @pl.when(core == this)
        def _():
            for number in range(2):
                span = slice(number * unit, (number + 1) * unit)
                stay[span, :] = total(stays[number])
                send[span, :] = total(sends[number]).astype(jnp.bfloat16)


def cross_kernel(stay, got, send, left):
    core = lax.axis_index("exp") % 2
    unit, part = send.shape[0], send.shape[1] // 2

    @pl.when(core == 0)
    def _():
        left[:, :part] = stay[:unit, :] + got[:unit, :].astype(jnp.float32)
        left[:, part:] = jnp.zeros((unit, part), jnp.float32)
        send[:, :part] = (stay[unit:, :] + got[unit:, :].astype(jnp.float32)).astype(jnp.bfloat16)
        send[:, part:] = jnp.zeros((unit, part), jnp.bfloat16)

    @pl.when(core == 1)
    def _():
        left[:, :part] = stay[:unit, :]
        left[:, part:] = got[:unit, :].astype(jnp.float32)
        send[:, :part] = stay[unit:, :].astype(jnp.bfloat16)
        send[:, part:] = got[unit:, :]


def line_kernel(*refs, line):
    ins, outs = refs[:4], refs[4:]
    core = lax.axis_index("exp") % 2
    ctx = lax.axis_index("ctx")
    count = outs[0].shape[0]
    part = ins[0].shape[1] // 2
    for number in range(2):
        left, got = ins[2 * number], ins[2 * number + 1]
        arrived = got[...].astype(jnp.float32)
        own = left[:, :part] + jnp.where(core == 1, arrived[:, :part], 0.0)
        other = left[:, part:] + jnp.where(core == 1, arrived[:, part:], arrived[:, :part])
        for value, side in ((own, ctx), (other, 1 - ctx)):
            at = pl.multiple_of(side * 2 * part + number * part, 128)
            for place, out in enumerate(outs):
                rows = value[place * count : (place + 1) * count]
                out[:, pl.ds(at, part)] = rows.astype(out.dtype)


def sum_kernel(first, *refs):
    total = first[...]
    for ref in refs[:-1]:
        total = total + ref[...].astype(jnp.float32)
    refs[-1][...] = total.astype(refs[-1].dtype)


def on_device_gathered(
    hidden, queries, latents, expert_ids, route_weight, w_gate, w_up, w_down
):
    tok_dev = hidden.shape[1]
    width = hidden.shape[2]
    topk = expert_ids.shape[2]
    units = w_gate.shape[1]
    columns = w_down.shape[1]
    tok_att, key_width = latents.shape
    heads_dev = queries.shape[1] // key_width
    experts = lax.axis_size("exp")
    line = experts // 4
    capacity = min(tok_dev, max(2, 3 * topk * tok_dev // (2 * experts)))
    half = width // 2
    unit = line * tok_dev
    count = 8 * unit
    slots = count // tok_dev * capacity
    bf16, f32 = jnp.bfloat16, jnp.float32
    copy_sems = pltpu.SemaphoreType.DMA((2 * PIECES,))

    (rows,) = local_kernel(
        lambda *refs: rows_kernel(*refs, half=half, topk=topk),
        [
            (hidden[0], "hbm"),
            (jnp.transpose(expert_ids, (2, 0, 1)), "hbm"),
            (jnp.transpose(route_weight, (2, 0, 1)), "hbm"),
        ],
        [((tok_dev, width + 128), bf16, "vmem")],
        [
            pltpu.VMEM((tok_dev, width), bf16),
            pltpu.VMEM((topk, 1, tok_dev), jnp.int32),
            pltpu.VMEM((topk, 1, tok_dev), f32),
            pltpu.SemaphoreType.DMA((3,)),
        ],
        "rows",
    )
    places = range(line - 1, 0, -1)
    along = [rows] + [along_line(rows, d) for d in places]
    latents_t, _ = lax.optimization_barrier((latents.T, rows))
    earlier_kv = swapped(latents_t, "ctx", 1)
    gate_1, up_1 = local_kernel(
        lambda *refs: fetch_kernel(*refs, start=0),
        [(rows, "vmem"), (w_gate[0], "hbm"), (w_up[0], "hbm")],
        [((units, half), bf16, "vmem")] * 2,
        [copy_sems],
        "fetch",
    )
    *along, earlier_kv, gate_1, up_1 = lax.optimization_barrier((*along, earlier_kv, gate_1, up_1))
    cuts = ((0, half + 128), (half + 128, width + 128))
    nears = local_kernel(
        lambda *refs: stack_kernel(*refs, cuts=cuts),
        [(row, "vmem") for row in along],
        [((unit, high - low), bf16, "vmem") for low, high in cuts],
        [],
        "stack_line",
    )
    pieces = []
    for near in nears:
        got = paired(near, y_then_x)
        (two,) = local_kernel(
            lambda *refs, cut=near.shape[1]: stack_kernel(*refs, cuts=((0, cut),)),
            [(near, "vmem"), (got, "vmem")],
            [((2 * unit, near.shape[1]), bf16, "vmem")],
            [],
            "stack_two",
        )
        pieces.append([two, paired(two, x_then_y)])
    gate_2, up_2, down_mine = local_kernel(
        lambda *refs: fetch_kernel(*refs, start=half),
        [(pieces[1][0], "vmem"), (w_gate[0], "hbm"), (w_up[0], "hbm"), (w_down[0], "hbm")],
        [((units, half), bf16, "vmem")] * 2 + [((columns, units), bf16, "vmem")],
        [pltpu.SemaphoreType.DMA((3 * PIECES,))],
        "fetch",
    )
    pieces[0][1], gate_2, up_2, down_mine = lax.optimization_barrier(
        (pieces[0][1], gate_2, up_2, down_mine)
    )
    for number, (two, far) in enumerate(pieces):
        group = (two, far, swapped(two, "exp", 1), swapped(far, "exp", 1))
        pieces[number] = [(piece, "vmem") for piece in group]

    gate, up, pick, pick_far, coef = local_kernel(
        lambda *refs: first_kernel(
            *refs, unit=unit, tok_dev=tok_dev, capacity=capacity, topk=topk
        ),
        [*pieces[0], (gate_1, "vmem"), (up_1, "vmem")],
        [((count, units), f32, "vmem")] * 2
        + [((count, slots), bf16, "vmem")] * 2
        + [((count, 128), f32, "vmem")],
        [pltpu.VMEM((count, half), bf16), pltpu.VMEM((count, 128), bf16)],
        "gate_up_first",
    )
    few = 2 * units // 3 if units % 384 == 0 else units // 2
    sums_in = [(gate_2, "vmem"), (up_2, "vmem"), (gate, "vmem"), (up, "vmem"), (pick, "vmem")]
    act_a, packed_a, tokens = local_kernel(
        lambda *refs: second_kernel(*refs, unit=unit),
        [*pieces[1], *sums_in],
        [
            ((count, few), bf16, "vmem"),
            ((slots, few), bf16, "vmem"),
            ((count, half), bf16, "vmem"),
        ],
        [],
        "gate_up_second",
    )
    other_a = swapped(packed_a, "ctx", 1)
    act_b, packed_b = local_kernel(
        lambda *refs: third_kernel(*refs, start=few),
        [(tokens, "vmem"), *sums_in],
        [((count, units - few), bf16, "vmem"), ((slots, units - few), bf16, "vmem")],
        [],
        "gate_up_third",
    )
    other_b = swapped(packed_b, "ctx", 1)
    own, down_other = local_kernel(
        own_kernel,
        [(act_a, "vmem"), (act_b, "vmem"), (down_mine, "vmem"), (w_down[0], "hbm")],
        [((count, columns), f32, "vmem"), ((columns, units), bf16, "vmem")],
        [pltpu.SemaphoreType.DMA((PIECES,))],
        "down_own",
    )
    part = columns // 2
    crossing = []
    for start in (0, part):
        keep, give = local_kernel(
            lambda *refs, start=start: other_kernel(*refs, start=start),
            [
                (other_a, "vmem"), (other_b, "vmem"), (pick_far, "vmem"), (coef, "vmem"),
                (down_other, "vmem"), (own, "vmem"),
            ],
            [((count // 2, part), bf16, "vmem")] * 2,
            [pltpu.VMEM((count, units), bf16)],
            "down_other",
        )
        send, stay = local_kernel(
            spread_kernel,
            [(keep, "vmem"), (swapped(give, "exp", 1), "vmem")],
            [((2 * unit, part), bf16, "vmem"), ((2 * unit, part), f32, "vmem")],
            [],
            "spread",
        )
        crossing.append((stay, paired(send, y_then_x)))
    lines = []
    for stay, got in crossing:
        send, left = local_kernel(
            cross_kernel,
            [(stay, "vmem"), (got, "vmem")],
            [((unit, 2 * part), bf16, "vmem"), ((unit, 2 * part), f32, "vmem")],
            [],
            "cross",
        )
        lines += [left, paired(send, x_then_y)]
    pad = -key_width % 128
    (attended,) = local_kernel(
        attention_kernel,
        [(send, "vmem"), (earlier_kv, "vmem"), (queries, "hbm"), (latents.T, "hbm")],
        [((tok_att, heads_dev * LATENT), bf16, "hbm")],
        [
            pltpu.VMEM((tok_att, heads_dev * key_width), bf16),
            pltpu.VMEM((key_width, tok_att), bf16),
            pltpu.VMEM((key_width + pad, 2 * tok_att), bf16),
            pltpu.VMEM((key_width + pad, 2 * tok_att), bf16),
            pltpu.VMEM((tok_att, heads_dev * LATENT), bf16),
            pltpu.SemaphoreType.DMA((2 + heads_dev,)),
        ],
        "attention",
    )
    lines[1], attended = lax.optimization_barrier((lines[1], attended))
    keep, *sends = local_kernel(
        lambda *refs: line_kernel(*refs, line=line),
        [(block, "vmem") for block in lines],
        [((tok_dev, 2 * columns), f32, "vmem")]
        + [((tok_dev, 2 * columns), bf16, "vmem")] * (line - 1),
        [],
        "line",
    )
    got = [along_line(block, d) for block, d in zip(sends, places)]
    (mixed,) = local_kernel(
        sum_kernel,
        [(block, "vmem") for block in (keep, *got)],
        [((tok_dev, 2 * columns), bf16, "result")],
        [],
        "sum",
    )
    return (attended, mixed[None])


def on_device_slots(hidden, queries, latents, expert_ids, route_weight, w_gate, w_up, w_down):
    tok_att = latents.shape[0]
    heads_dev = queries.shape[1] // (LATENT + ROPE)
    tok_dev = hidden.shape[1]
    width = hidden.shape[2]
    topk = expert_ids.shape[2]
    experts = lax.axis_size("exp")
    groups = lax.axis_size("ctx")
    capacity = min(tok_dev, max(2, 3 * topk * tok_dev // (2 * experts)))
    slots = experts * capacity
    earlier_kv = shifted(latents, "ctx", 1)
    keys = jnp.concatenate([earlier_kv, latents], axis=0)
    query_rows = queries.reshape(tok_att, heads_dev, LATENT + ROPE)
    scores = jnp.einsum("thc,kc->htk", query_rows, keys, preferred_element_type=jnp.float32) * SCALE
    row_pos = jnp.arange(tok_att, dtype=jnp.int32)
    key_pos = jnp.arange(2 * tok_att, dtype=jnp.int32)
    seen_own = (key_pos[None, :] >= tok_att) & (key_pos[None, :] - tok_att <= row_pos[:, None])
    seen_prev = (key_pos[None, :] < tok_att) & (lax.axis_index("ctx") > 0)
    scores = jnp.where((seen_own | seen_prev)[None, :, :], scores, jnp.float32(-1e30))
    top = jnp.max(scores, axis=-1, keepdims=True)
    expo = jnp.exp(scores - top)
    probs = (expo / jnp.sum(expo, axis=-1, keepdims=True)).astype(jnp.bfloat16)
    mixed_heads = jnp.einsum(
        "htk,kc->thc", probs, keys[:, :LATENT], preferred_element_type=jnp.float32
    )
    attended = mixed_heads.astype(jnp.bfloat16).reshape(tok_att, heads_dev * LATENT)
    tokens = hidden[0]
    picks = expert_ids[0]
    pick_weight = route_weight[0].reshape(-1)
    tok_hot = token_table(tok_dev, topk)
    slot_hot = place_picks(picks, experts, capacity)
    gate_w = w_gate[0]
    up_w = w_up[0]
    down_w = w_down[0]
    send_matrix = jnp.dot(slot_hot.T, tok_hot).astype(jnp.bfloat16)
    outgoing = jnp.dot(send_matrix, tokens, preferred_element_type=jnp.float32).astype(jnp.bfloat16)
    outgoing = outgoing.reshape(experts, capacity, width)
    arrived = lax.all_to_all(outgoing, "exp", split_axis=0, concat_axis=0, tiled=True)
    piece = lax.all_gather(arrived.reshape(slots, width), "ctx", axis=0, tiled=True)
    gate = times_rows(piece, gate_w)
    upper = times_rows(piece, up_w)
    hidden_units = (jax.nn.silu(gate) * upper).astype(jnp.bfloat16)
    projected = times_rows(lax.all_gather(hidden_units, "ctx", axis=1, tiled=True), down_w)
    columns = projected.astype(jnp.bfloat16).reshape(groups, experts, capacity, down_w.shape[0])
    by_block = lax.all_to_all(columns, "ctx", split_axis=0, concat_axis=3, tiled=True)
    returned = lax.all_to_all(by_block, "exp", split_axis=1, concat_axis=1, tiled=True)
    combine_matrix = jnp.dot(
        slot_hot.T, tok_hot * pick_weight[:, None], precision=lax.Precision.HIGHEST
    )
    back_rows = returned.reshape(slots, width).astype(jnp.float32)
    mixed = jnp.dot(combine_matrix.T, back_rows, precision=lax.Precision.HIGHEST).astype(
        jnp.bfloat16
    )
    return (attended, mixed[None])


def solution(mesh):
    experts, groups = mesh.shape["exp"], mesh.shape["ctx"]
    whole = groups == 2 and experts == 16
    on_device = on_device_gathered if whole else on_device_slots
    placed = (
        P("exp", "ctx", None),
        P("ctx", "exp"),
        P("ctx", None),
        P("exp", "ctx", None),
        P("exp", "ctx", None),
        P("exp", "ctx", None),
        P("exp", "ctx", None),
        P("exp", "ctx", None),
    )
    return jax.shard_map(
        on_device,
        mesh=mesh,
        in_specs=placed,
        out_specs=(P("ctx", "exp"), P("exp", "ctx", None)),
        check_vma=False,
    )
```

```python
import jax
import jax.numpy as jnp
from jax import lax
from jax.experimental import pallas as pl
from jax.experimental.pallas import tpu as pltpu
from jax.sharding import PartitionSpec as P

LATENT = 512
ROPE = 64


SCALE = 0.07216878364870322


def shifted(block, axis, distance):
    devices = range(lax.axis_size(axis))
    route = [(i - distance, i) for i in devices if i - distance in devices]
    return lax.ppermute(block, axis, route)


def place_picks(picks, experts, capacity):
    flat = picks.reshape(-1)
    onehot = (flat[:, None] == jnp.arange(experts, dtype=jnp.int32)[None, :]).astype(jnp.int32)
    earlier = jnp.cumsum(onehot, axis=0) - onehot
    rank = jnp.sum(earlier * onehot, axis=1)
    target = flat * capacity + rank
    return (target[:, None] == jnp.arange(experts * capacity, dtype=jnp.int32)[None, :]).astype(
        jnp.float32
    )


def token_table(tok_count, topk):
    owner = jnp.arange(tok_count * topk, dtype=jnp.int32) // topk
    return (owner[:, None] == jnp.arange(tok_count, dtype=jnp.int32)[None, :]).astype(jnp.float32)


def times_rows(left, right):
    return lax.dot_general(
        left, right, (((1,), (1,)), ((), ())), preferred_element_type=jnp.float32
    )


def swapped(block, axis, bit):
    return lax.ppermute(block, axis, [(i, i ^ bit) for i in range(lax.axis_size(axis))])


def along_line(block, steps):
    return lax.ppermute(
        block, "exp", [(i, i ^ (4 * steps)) for i in range(lax.axis_size("exp"))]
    )


def paired(block, partner):
    count = lax.axis_size("exp")
    both = lax.axis_size("ctx") * count
    route = []
    for i in range(both):
        ctx, exp = partner(i // count, i % count)
        route.append((i, ctx * count + exp))
    return lax.ppermute(block, ("ctx", "exp"), route)


def over_y(ctx, exp):
    return ctx, exp ^ 2


def over_x(ctx, exp):
    return 1 - ctx, exp


def times_rows_in(left, right):
    return lax.dot_general(
        left, right, (((1,), (1,)), ((), ())), preferred_element_type=jnp.float32
    )


def in_vmem(array):
    return pltpu.with_memory_space_constraint(array, pltpu.VMEM)


def in_hbm(array):
    return pltpu.with_memory_space_constraint(array, pltpu.HBM)


def local_kernel(body, ins, outs, scratch, name):
    kinds = {"vmem": pltpu.VMEM, "hbm": pl.ANY, "result": pltpu.VMEM}
    place = {"vmem": in_vmem, "hbm": in_hbm}
    made = [
        pltpu.VMEM(shape, dtype) if kind == "vmem" else jax.ShapeDtypeStruct(shape, dtype)
        for shape, dtype, kind in outs
    ]
    return pl.pallas_call(
        body,
        in_specs=[pl.BlockSpec(memory_space=kinds[kind]) for _, kind in ins],
        out_specs=[pl.BlockSpec(memory_space=kinds[kind]) for _, _, kind in outs],
        out_shape=made,
        scratch_shapes=scratch,
        compiler_params=pltpu.CompilerParams(vmem_limit_bytes=20 * 1024 * 1024),
        cost_estimate=pl.CostEstimate(flops=0, bytes_accessed=0, transcendentals=0),
        name=name,
    )(*[place[kind](array) for array, kind in ins])


def start_copies(pairs, sems, pieces):
    copies = []
    for number, (source, target) in enumerate(pairs):
        step = target.shape[0] // pieces
        for piece in range(pieces):
            span = pl.ds(piece * step, step)
            copy = pltpu.make_async_copy(
                source.at[span, :], target.at[span, :], sems.at[number * pieces + piece]
            )
            copy.start()
            copies.append(copy)
    return copies


PIECES = 4


def rows_kernel(tokens_in, names_in, weights_in, out, tokens, names, weights, sems, *, half, topk):
    copies = [
        pltpu.make_async_copy(source, target, sems.at[number])
        for number, (source, target) in enumerate(
            ((tokens_in, tokens), (names_in, names), (weights_in, weights))
        )
    ]
    for copy in copies:
        copy.start()
    for copy in copies:
        copy.wait()
    count = tokens.shape[0]
    width = tokens.shape[1]
    out[:, :half] = tokens[:, :half]
    out[:, half + 128 :] = tokens[:, half:width]
    lane = lax.broadcasted_iota(jnp.int32, (count, 128), 1)
    same = lax.broadcasted_iota(jnp.int32, (count, count), 0) == lax.broadcasted_iota(
        jnp.int32, (count, count), 1
    )

    def column(row):
        return jnp.sum(
            jnp.where(same, jnp.broadcast_to(row, same.shape), 0.0), axis=1, keepdims=True
        )

    note = jnp.zeros((count, 128), jnp.float32)
    for k in range(topk):
        name = column(names[k].astype(jnp.float32))
        weight = column(weights[k])
        low = weight - weight.astype(jnp.bfloat16).astype(jnp.float32)
        for value, at in ((name, k), (weight, topk + k), (low, 2 * topk + k)):
            note = jnp.where(lane == at, value, note)
    out[:, half : half + 128] = note.astype(jnp.bfloat16)


def fetch_kernel(after, *refs, start):
    count = len(refs) // 2
    ins, outs, sems = refs[:count], refs[count:-1], refs[-1]
    pairs = [(a.at[:, start : start + b.shape[1]], b) for a, b in zip(ins[:2], outs[:2])]
    if count > 2:
        width = outs[2].shape[1]
        own_at = pl.multiple_of(lax.axis_index("ctx") * width, 128)
        pairs.append((ins[2].at[:, pl.ds(own_at, width)], outs[2]))
    for copy in start_copies(pairs, sems, PIECES):
        copy.wait()


def stack_kernel(*refs, cuts):
    ins, outs = refs[: len(refs) - len(cuts)], refs[len(refs) - len(cuts) :]
    for out, (low, high) in zip(outs, cuts):
        if ins[0].shape[0] % 16 == 0:
            at = 0
            for ref in ins:
                out[at : at + ref.shape[0], :] = ref[:, low:high]
                at += ref.shape[0]
        else:
            rows = [ref[:, low:high].astype(jnp.float32) for ref in ins]
            out[...] = jnp.concatenate(rows, axis=0).astype(out.dtype)


def attention_kernel(
    after, earlier, queries_in, latents_in, attended, queries, latents, even, odd, mixed, sems
):
    width, rows = latents.shape
    pad = even.shape[0] - width
    loads = [
        pltpu.make_async_copy(queries_in, queries, sems.at[0]),
        pltpu.make_async_copy(latents_in, latents, sems.at[1]),
    ]
    for copy in loads:
        copy.start()
    for copy in loads:
        copy.wait()
    even[width:, :] = jnp.zeros((pad, 2 * rows), jnp.bfloat16)
    odd[:pad, :] = jnp.zeros((pad, 2 * rows), jnp.bfloat16)
    even[:width, :rows] = earlier[...]
    even[:width, rows:] = latents[...]
    odd[pad:, :rows] = earlier[...]
    odd[pad:, rows:] = latents[...]
    row = lax.broadcasted_iota(jnp.int32, (rows, 2 * rows), 0)
    key = lax.broadcasted_iota(jnp.int32, (rows, 2 * rows), 1)
    nearest = jnp.where(lax.axis_index("ctx") > 0, 0, rows)
    seen = (key >= nearest) & (key <= row + rows)
    heads = attended.shape[1] // LATENT
    writes = []
    for head in range(heads):
        start = head * width
        keys, start = (even, start) if start % 128 == 0 else (odd, start - pad)
        scores = jnp.dot(
            queries[:, start : start + width + pad], keys[...], preferred_element_type=jnp.float32
        )
        scores = jnp.where(seen, scores * SCALE, jnp.float32(-1e30))
        expo = jnp.exp(scores - jnp.max(scores, axis=-1, keepdims=True))
        probs = (expo / jnp.sum(expo, axis=-1, keepdims=True)).astype(jnp.bfloat16)
        span = slice(head * LATENT, (head + 1) * LATENT)
        mixed[:, span] = times_rows_in(probs, even[:LATENT, :]).astype(jnp.bfloat16)
        write = pltpu.make_async_copy(mixed.at[:, span], attended.at[:, span], sems.at[2 + head])
        write.start()
        writes.append(write)
    for copy in writes:
        copy.wait()


def assemble(place, two_ref, far_ref, two_other_ref, far_other_ref, unit, y_first, start=0):
    span = slice(start, start + place.shape[1])
    order = (0, 2, 1, 3) if y_first else (0, 1, 2, 3)
    for lane, two, far in ((0, two_ref, far_ref), (1, two_other_ref, far_other_ref)):
        for number, block in enumerate(order):
            ref = (two, far)[number // 2]
            rows = slice(number % 2 * unit, (number % 2 + 1) * unit)
            base = (lane * 4 + block) * unit
            place[base : base + unit, :] = ref[rows, span]


def first_kernel(
    two, far, two_other, far_other, gate_w, up_w,
    gate_out, up_out, pick_out, pick_far_out, coef_out,
    tokens, notes, *, unit, tok_dev, capacity, topk,
):
    width = tokens.shape[1]
    rows = tokens.shape[0]
    slots = pick_out.shape[1]
    expert = lax.axis_index("exp")
    assemble(tokens, two, far, two_other, far_other, unit, True)
    gate_out[...] = times_rows_in(tokens[...], gate_w[...])
    up_out[...] = times_rows_in(tokens[...], up_w[...])

    assemble(notes, two, far, two_other, far_other, unit, True, width)
    note = notes[...].astype(jnp.float32)
    lane = lax.broadcasted_iota(jnp.int32, note.shape, 1)
    mine = (note == expert.astype(jnp.float32)) & (lane < topk)
    weight = pltpu.roll(note, 128 - topk, 1) + pltpu.roll(note, 128 - 2 * topk, 1)
    coef = jnp.sum(jnp.where(mine, weight, 0.0), axis=1, keepdims=True)
    hit = jnp.sum(mine.astype(jnp.float32), axis=1, keepdims=True)
    shift = tok_dev.bit_length() - 1
    at = lax.broadcasted_iota(jnp.int32, (rows, rows), 0)
    before = lax.broadcasted_iota(jnp.int32, (rows, rows), 1)
    earlier = ((at >> shift) == (before >> shift)) & (before < at)
    hits = jnp.broadcast_to(hit, (rows, slots))
    rank = jnp.dot(
        earlier.astype(jnp.float32).astype(jnp.bfloat16),
        hits.astype(jnp.bfloat16),
        preferred_element_type=jnp.float32,
    ).astype(jnp.int32)
    row = lax.broadcasted_iota(jnp.int32, (rows, slots), 0)
    slot = (row >> shift) * capacity + rank
    group = unit // tok_dev * capacity
    away = ((row >> (unit.bit_length() - 1)) & 1) == 0
    slot_far = slot + jnp.where(away, group, -group)
    column = lax.broadcasted_iota(jnp.int32, (rows, slots), 1)
    pick_out[...] = jnp.where(slot == column, hits, 0.0).astype(jnp.bfloat16)
    pick_far_out[...] = jnp.where(slot_far == column, hits, 0.0).astype(jnp.bfloat16)
    coef_out[...] = jnp.broadcast_to(coef, coef_out.shape)


def finish_units(tokens, gate_w, up_w, gate_in, up_in, pick, act_out, packed_out, start):
    span = slice(start, start + act_out.shape[1])
    gate = gate_in[:, span] + times_rows_in(tokens[...], gate_w[span, :])
    upper = up_in[:, span] + times_rows_in(tokens[...], up_w[span, :])
    act = (gate / (1.0 + jnp.exp(-gate)) * upper).astype(jnp.bfloat16)
    act_out[...] = act
    packed_out[...] = lax.dot_general(
        pick[...], act, (((0,), (0,)), ((), ())), preferred_element_type=jnp.float32
    ).astype(jnp.bfloat16)


def second_kernel(
    two, far, two_other, far_other, gate_w, up_w, gate_in, up_in, pick,
    act_out, packed_out, tokens, *, unit,
):
    assemble(tokens, two, far, two_other, far_other, unit, False)
    finish_units(tokens, gate_w, up_w, gate_in, up_in, pick, act_out, packed_out, 0)


def third_kernel(tokens, gate_w, up_w, gate_in, up_in, pick, act_out, packed_out, *, start):
    finish_units(tokens, gate_w, up_w, gate_in, up_in, pick, act_out, packed_out, start)


def own_kernel(act_a, act_b, down_own, down_w, out, down_other, sems):
    units = down_own.shape[1]
    few = act_a.shape[1]
    other_at = pl.multiple_of((1 - lax.axis_index("ctx")) * units, 128)
    copies = start_copies([(down_w.at[:, pl.ds(other_at, units)], down_other)], sems, PIECES)
    tall = out.shape[1] // 5 if out.shape[1] % 640 == 0 else out.shape[1]
    for n in range(0, out.shape[1], tall):
        span = slice(n, n + tall)
        out[:, span] = times_rows_in(act_a[...], down_own[span, :few]) + times_rows_in(
            act_b[...], down_own[span, few:]
        )
    for copy in copies:
        copy.wait()


def other_kernel(packed_a, packed_b, pick, coef, down_w, own, keep, give, act, *, start):
    few = packed_a.shape[1]
    for packed, span in ((packed_a, slice(0, few)), (packed_b, slice(few, act.shape[1]))):
        act[:, span] = jnp.dot(
            pick[...], packed[...], preferred_element_type=jnp.float32
        ).astype(jnp.bfloat16)
    half, part = keep.shape
    tall = part // 5 if part % 5 == 0 else part
    for n in range(0, part, tall):
        span = slice(start + n, start + n + tall)
        projected = own[:, span] + times_rows_in(act[...], down_w[span, :])
        projected = projected * coef[:, :1]
        keep[:, n : n + tall] = projected[:half].astype(jnp.bfloat16)
        give[:, n : n + tall] = projected[half:].astype(jnp.bfloat16)


def spread_kernel(keep, got, send, stay, *, y_first):
    unit = keep.shape[0] // 4
    stays, sends = ((0, 1), (2, 3)) if y_first else ((0, 2), (1, 3))
    for out, blocks in ((stay, stays), (send, sends)):
        for number, block in enumerate(blocks):
            span = slice(block * unit, (block + 1) * unit)
            total = keep[span, :].astype(jnp.float32) + got[span, :].astype(jnp.float32)
            out[number * unit : (number + 1) * unit, :] = total.astype(out.dtype)


def cross_kernel(stay, got, send, left, *, y_first):
    unit, part = send.shape[0], stay.shape[1]
    if y_first:
        left[...] = stay[:unit, :] + got[:unit, :].astype(jnp.float32)
        send[...] = (stay[unit:, :] + got[unit:, :].astype(jnp.float32)).astype(jnp.bfloat16)
    else:
        left[:, :part] = stay[:unit, :]
        left[:, part:] = got[:unit, :].astype(jnp.float32)
        send[:, :part] = stay[unit:, :].astype(jnp.bfloat16)
        send[:, part:] = got[unit:, :]


def line_kernel(left_y, got_x, left_x, got_y, *outs):
    ctx = lax.axis_index("ctx")
    count, part = outs[0].shape[0], left_y.shape[1]
    whole = left_x[...] + got_y[...].astype(jnp.float32)
    blocks = (
        (left_y[...], ctx, 0),
        (got_x[...].astype(jnp.float32), 1 - ctx, 0),
        (whole[:, :part], ctx, 1),
        (whole[:, part:], 1 - ctx, 1),
    )
    for value, side, number in blocks:
        at = pl.multiple_of(side * 2 * part + number * part, 128)
        for place, out in enumerate(outs):
            rows = value[place * count : (place + 1) * count]
            out[:, pl.ds(at, part)] = rows.astype(out.dtype)


def sum_kernel(first, *refs):
    total = first[...]
    for ref in refs[:-1]:
        total = total + ref[...].astype(jnp.float32)
    refs[-1][...] = total.astype(refs[-1].dtype)


def on_device_gathered(
    hidden, queries, latents, expert_ids, route_weight, w_gate, w_up, w_down
):
    tok_dev = hidden.shape[1]
    width = hidden.shape[2]
    topk = expert_ids.shape[2]
    units = w_gate.shape[1]
    columns = w_down.shape[1]
    tok_att, key_width = latents.shape
    heads_dev = queries.shape[1] // key_width
    experts = lax.axis_size("exp")
    line = experts // 4
    capacity = min(tok_dev, max(2, 3 * topk * tok_dev // (2 * experts)))
    half = width // 2
    unit = line * tok_dev
    count = 8 * unit
    slots = count // tok_dev * capacity
    bf16, f32 = jnp.bfloat16, jnp.float32
    copy_sems = pltpu.SemaphoreType.DMA((2 * PIECES,))

    (rows,) = local_kernel(
        lambda *refs: rows_kernel(*refs, half=half, topk=topk),
        [
            (hidden[0], "hbm"),
            (jnp.transpose(expert_ids, (2, 0, 1)), "hbm"),
            (jnp.transpose(route_weight, (2, 0, 1)), "hbm"),
        ],
        [((tok_dev, width + 128), bf16, "vmem")],
        [
            pltpu.VMEM((tok_dev, width), bf16),
            pltpu.VMEM((topk, 1, tok_dev), jnp.int32),
            pltpu.VMEM((topk, 1, tok_dev), f32),
            pltpu.SemaphoreType.DMA((3,)),
        ],
        "rows",
    )
    places = range(line - 1, 0, -1)
    along = [rows] + [along_line(rows, d) for d in places]
    latents_t, _ = lax.optimization_barrier((latents.T, rows))
    earlier_kv = swapped(latents_t, "ctx", 1)
    gate_1, up_1 = local_kernel(
        lambda *refs: fetch_kernel(*refs, start=0),
        [(rows, "vmem"), (w_gate[0], "hbm"), (w_up[0], "hbm")],
        [((units, half), bf16, "vmem")] * 2,
        [copy_sems],
        "fetch",
    )
    *along, earlier_kv, gate_1, up_1 = lax.optimization_barrier((*along, earlier_kv, gate_1, up_1))
    cuts = ((0, half + 128), (half + 128, width + 128))
    nears = local_kernel(
        lambda *refs: stack_kernel(*refs, cuts=cuts),
        [(row, "vmem") for row in along],
        [((unit, high - low), bf16, "vmem") for low, high in cuts],
        [],
        "stack_line",
    )
    pieces = []
    for near, first, then in zip(nears, (over_y, over_x), (over_x, over_y)):
        got = paired(near, first)
        (two,) = local_kernel(
            lambda *refs, cut=near.shape[1]: stack_kernel(*refs, cuts=((0, cut),)),
            [(near, "vmem"), (got, "vmem")],
            [((2 * unit, near.shape[1]), bf16, "vmem")],
            [],
            "stack_two",
        )
        pieces.append([two, paired(two, then)])
    gate_2, up_2, down_mine = local_kernel(
        lambda *refs: fetch_kernel(*refs, start=half),
        [(pieces[1][0], "vmem"), (w_gate[0], "hbm"), (w_up[0], "hbm"), (w_down[0], "hbm")],
        [((units, half), bf16, "vmem")] * 2 + [((columns, units), bf16, "vmem")],
        [pltpu.SemaphoreType.DMA((3 * PIECES,))],
        "fetch",
    )
    pieces[0][1], gate_2, up_2, down_mine = lax.optimization_barrier(
        (pieces[0][1], gate_2, up_2, down_mine)
    )
    for number, (two, far) in enumerate(pieces):
        group = (two, far, swapped(two, "exp", 1), swapped(far, "exp", 1))
        pieces[number] = [(piece, "vmem") for piece in group]

    gate, up, pick, pick_far, coef = local_kernel(
        lambda *refs: first_kernel(
            *refs, unit=unit, tok_dev=tok_dev, capacity=capacity, topk=topk
        ),
        [*pieces[0], (gate_1, "vmem"), (up_1, "vmem")],
        [((count, units), f32, "vmem")] * 2
        + [((count, slots), bf16, "vmem")] * 2
        + [((count, 128), f32, "vmem")],
        [pltpu.VMEM((count, half), bf16), pltpu.VMEM((count, 128), bf16)],
        "gate_up_first",
    )
    few = 2 * units // 3 if units % 384 == 0 else units // 2
    sums_in = [(gate_2, "vmem"), (up_2, "vmem"), (gate, "vmem"), (up, "vmem"), (pick, "vmem")]
    act_a, packed_a, tokens = local_kernel(
        lambda *refs: second_kernel(*refs, unit=unit),
        [*pieces[1], *sums_in],
        [
            ((count, few), bf16, "vmem"),
            ((slots, few), bf16, "vmem"),
            ((count, half), bf16, "vmem"),
        ],
        [],
        "gate_up_second",
    )
    other_a = swapped(packed_a, "ctx", 1)
    act_b, packed_b = local_kernel(
        lambda *refs: third_kernel(*refs, start=few),
        [(tokens, "vmem"), *sums_in],
        [((count, units - few), bf16, "vmem"), ((slots, units - few), bf16, "vmem")],
        [],
        "gate_up_third",
    )
    other_b = swapped(packed_b, "ctx", 1)
    own, down_other = local_kernel(
        own_kernel,
        [(act_a, "vmem"), (act_b, "vmem"), (down_mine, "vmem"), (w_down[0], "hbm")],
        [((count, columns), f32, "vmem"), ((columns, units), bf16, "vmem")],
        [pltpu.SemaphoreType.DMA((PIECES,))],
        "down_own",
    )
    part = columns // 2
    crossing = []
    for start, y_first in ((0, True), (part, False)):
        keep, give = local_kernel(
            lambda *refs, start=start: other_kernel(*refs, start=start),
            [
                (other_a, "vmem"), (other_b, "vmem"), (pick_far, "vmem"), (coef, "vmem"),
                (down_other, "vmem"), (own, "vmem"),
            ],
            [((count // 2, part), bf16, "vmem")] * 2,
            [pltpu.VMEM((count, units), bf16)],
            "down_other",
        )
        send, stay = local_kernel(
            lambda *refs, y_first=y_first: spread_kernel(*refs, y_first=y_first),
            [(keep, "vmem"), (swapped(give, "exp", 1), "vmem")],
            [((2 * unit, part), bf16, "vmem"), ((2 * unit, part), f32, "vmem")],
            [],
            "spread",
        )
        crossing.append((y_first, stay, paired(send, over_y if y_first else over_x)))
    lines = []
    for y_first, stay, got in crossing:
        wide = part if y_first else 2 * part
        send, left = local_kernel(
            lambda *refs, y_first=y_first: cross_kernel(*refs, y_first=y_first),
            [(stay, "vmem"), (got, "vmem")],
            [((unit, wide), bf16, "vmem"), ((unit, wide), f32, "vmem")],
            [],
            "cross",
        )
        lines += [left, paired(send, over_x if y_first else over_y)]
    pad = -key_width % 128
    (attended,) = local_kernel(
        attention_kernel,
        [(send, "vmem"), (earlier_kv, "vmem"), (queries, "hbm"), (latents.T, "hbm")],
        [((tok_att, heads_dev * LATENT), bf16, "hbm")],
        [
            pltpu.VMEM((tok_att, heads_dev * key_width), bf16),
            pltpu.VMEM((key_width, tok_att), bf16),
            pltpu.VMEM((key_width + pad, 2 * tok_att), bf16),
            pltpu.VMEM((key_width + pad, 2 * tok_att), bf16),
            pltpu.VMEM((tok_att, heads_dev * LATENT), bf16),
            pltpu.SemaphoreType.DMA((2 + heads_dev,)),
        ],
        "attention",
    )
    lines[1], attended = lax.optimization_barrier((lines[1], attended))
    keep, *sends = local_kernel(
        line_kernel,
        [(block, "vmem") for block in lines],
        [((tok_dev, 2 * columns), f32, "vmem")]
        + [((tok_dev, 2 * columns), bf16, "vmem")] * (line - 1),
        [],
        "line",
    )
    got = [along_line(block, d) for block, d in zip(sends, places)]
    (mixed,) = local_kernel(
        sum_kernel,
        [(block, "vmem") for block in (keep, *got)],
        [((tok_dev, 2 * columns), bf16, "result")],
        [],
        "sum",
    )
    return (attended, mixed[None])


def on_device_slots(hidden, queries, latents, expert_ids, route_weight, w_gate, w_up, w_down):
    tok_att = latents.shape[0]
    heads_dev = queries.shape[1] // (LATENT + ROPE)
    tok_dev = hidden.shape[1]
    width = hidden.shape[2]
    topk = expert_ids.shape[2]
    experts = lax.axis_size("exp")
    groups = lax.axis_size("ctx")
    capacity = min(tok_dev, max(2, 3 * topk * tok_dev // (2 * experts)))
    slots = experts * capacity
    earlier_kv = shifted(latents, "ctx", 1)
    keys = jnp.concatenate([earlier_kv, latents], axis=0)
    query_rows = queries.reshape(tok_att, heads_dev, LATENT + ROPE)
    scores = jnp.einsum("thc,kc->htk", query_rows, keys, preferred_element_type=jnp.float32) * SCALE
    row_pos = jnp.arange(tok_att, dtype=jnp.int32)
    key_pos = jnp.arange(2 * tok_att, dtype=jnp.int32)
    seen_own = (key_pos[None, :] >= tok_att) & (key_pos[None, :] - tok_att <= row_pos[:, None])
    seen_prev = (key_pos[None, :] < tok_att) & (lax.axis_index("ctx") > 0)
    scores = jnp.where((seen_own | seen_prev)[None, :, :], scores, jnp.float32(-1e30))
    top = jnp.max(scores, axis=-1, keepdims=True)
    expo = jnp.exp(scores - top)
    probs = (expo / jnp.sum(expo, axis=-1, keepdims=True)).astype(jnp.bfloat16)
    mixed_heads = jnp.einsum(
        "htk,kc->thc", probs, keys[:, :LATENT], preferred_element_type=jnp.float32
    )
    attended = mixed_heads.astype(jnp.bfloat16).reshape(tok_att, heads_dev * LATENT)
    tokens = hidden[0]
    picks = expert_ids[0]
    pick_weight = route_weight[0].reshape(-1)
    tok_hot = token_table(tok_dev, topk)
    slot_hot = place_picks(picks, experts, capacity)
    gate_w = w_gate[0]
    up_w = w_up[0]
    down_w = w_down[0]
    send_matrix = jnp.dot(slot_hot.T, tok_hot).astype(jnp.bfloat16)
    outgoing = jnp.dot(send_matrix, tokens, preferred_element_type=jnp.float32).astype(jnp.bfloat16)
    outgoing = outgoing.reshape(experts, capacity, width)
    arrived = lax.all_to_all(outgoing, "exp", split_axis=0, concat_axis=0, tiled=True)
    piece = lax.all_gather(arrived.reshape(slots, width), "ctx", axis=0, tiled=True)
    gate = times_rows(piece, gate_w)
    upper = times_rows(piece, up_w)
    hidden_units = (jax.nn.silu(gate) * upper).astype(jnp.bfloat16)
    projected = times_rows(lax.all_gather(hidden_units, "ctx", axis=1, tiled=True), down_w)
    columns = projected.astype(jnp.bfloat16).reshape(groups, experts, capacity, down_w.shape[0])
    by_block = lax.all_to_all(columns, "ctx", split_axis=0, concat_axis=3, tiled=True)
    returned = lax.all_to_all(by_block, "exp", split_axis=1, concat_axis=1, tiled=True)
    combine_matrix = jnp.dot(
        slot_hot.T, tok_hot * pick_weight[:, None], precision=lax.Precision.HIGHEST
    )
    back_rows = returned.reshape(slots, width).astype(jnp.float32)
    mixed = jnp.dot(combine_matrix.T, back_rows, precision=lax.Precision.HIGHEST).astype(
        jnp.bfloat16
    )
    return (attended, mixed[None])


def solution(mesh):
    experts, groups = mesh.shape["exp"], mesh.shape["ctx"]
    whole = groups == 2 and experts == 16
    on_device = on_device_gathered if whole else on_device_slots
    placed = (
        P("exp", "ctx", None),
        P("ctx", "exp"),
        P("ctx", None),
        P("exp", "ctx", None),
        P("exp", "ctx", None),
        P("exp", "ctx", None),
        P("exp", "ctx", None),
        P("exp", "ctx", None),
    )
    return jax.shard_map(
        on_device,
        mesh=mesh,
        in_specs=placed,
        out_specs=(P("ctx", "exp"), P("exp", "ctx", None)),
        check_vma=False,
    )
```

```python
import jax
import jax.numpy as jnp
from jax import lax
from jax.experimental import pallas as pl
from jax.experimental.pallas import tpu as pltpu
from jax.sharding import PartitionSpec as P

LATENT = 512
ROPE = 64


SCALE = 0.07216878364870322


def shifted(block, axis, distance):
    devices = range(lax.axis_size(axis))
    route = [(i - distance, i) for i in devices if i - distance in devices]
    return lax.ppermute(block, axis, route)


def place_picks(picks, experts, capacity):
    flat = picks.reshape(-1)
    onehot = (flat[:, None] == jnp.arange(experts, dtype=jnp.int32)[None, :]).astype(jnp.int32)
    earlier = jnp.cumsum(onehot, axis=0) - onehot
    rank = jnp.sum(earlier * onehot, axis=1)
    target = flat * capacity + rank
    return (target[:, None] == jnp.arange(experts * capacity, dtype=jnp.int32)[None, :]).astype(
        jnp.float32
    )


def token_table(tok_count, topk):
    owner = jnp.arange(tok_count * topk, dtype=jnp.int32) // topk
    return (owner[:, None] == jnp.arange(tok_count, dtype=jnp.int32)[None, :]).astype(jnp.float32)


def times_rows(left, right):
    return lax.dot_general(
        left, right, (((1,), (1,)), ((), ())), preferred_element_type=jnp.float32
    )


def swapped(block, axis, bit):
    return lax.ppermute(block, axis, [(i, i ^ bit) for i in range(lax.axis_size(axis))])


def along_line(block, steps):
    return lax.ppermute(
        block, "exp", [(i, i ^ (4 * steps)) for i in range(lax.axis_size("exp"))]
    )


def paired(block, partner):
    count = lax.axis_size("exp")
    both = lax.axis_size("ctx") * count
    route = []
    for i in range(both):
        ctx, exp = partner(i // count, i % count)
        route.append((i, ctx * count + exp))
    return lax.ppermute(block, ("ctx", "exp"), route)


def over_y(ctx, exp):
    return ctx, exp ^ 2


def over_x(ctx, exp):
    return 1 - ctx, exp


def times_rows_in(left, right):
    return lax.dot_general(
        left, right, (((1,), (1,)), ((), ())), preferred_element_type=jnp.float32
    )


def in_vmem(array):
    return pltpu.with_memory_space_constraint(array, pltpu.VMEM)


def in_hbm(array):
    return pltpu.with_memory_space_constraint(array, pltpu.HBM)


def local_kernel(body, ins, outs, scratch, name):
    kinds = {"vmem": pltpu.VMEM, "hbm": pl.ANY, "result": pltpu.VMEM}
    place = {"vmem": in_vmem, "hbm": in_hbm}
    made = [
        pltpu.VMEM(shape, dtype) if kind == "vmem" else jax.ShapeDtypeStruct(shape, dtype)
        for shape, dtype, kind in outs
    ]
    return pl.pallas_call(
        body,
        in_specs=[pl.BlockSpec(memory_space=kinds[kind]) for _, kind in ins],
        out_specs=[pl.BlockSpec(memory_space=kinds[kind]) for _, _, kind in outs],
        out_shape=made,
        scratch_shapes=scratch,
        compiler_params=pltpu.CompilerParams(vmem_limit_bytes=20 * 1024 * 1024),
        cost_estimate=pl.CostEstimate(flops=0, bytes_accessed=0, transcendentals=0),
        name=name,
    )(*[place[kind](array) for array, kind in ins])


def start_copies(pairs, sems, pieces):
    copies = []
    for number, (source, target) in enumerate(pairs):
        step = target.shape[0] // pieces
        for piece in range(pieces):
            span = pl.ds(piece * step, step)
            copy = pltpu.make_async_copy(
                source.at[span, :], target.at[span, :], sems.at[number * pieces + piece]
            )
            copy.start()
            copies.append(copy)
    return copies


PIECES = 4


def rows_kernel(
    tokens_in, names_in, weights_in, latents_in, out, latents, tokens, names, weights, sems, *, half, topk
):
    share = latents.shape[0]
    at = pl.multiple_of(lax.axis_index("exp") % 2 * share, 16)
    copies = [
        pltpu.make_async_copy(source, target, sems.at[number])
        for number, (source, target) in enumerate(
            (
                (tokens_in, tokens),
                (names_in, names),
                (weights_in, weights),
                (latents_in.at[pl.ds(at, share), :], latents),
            )
        )
    ]
    for copy in copies:
        copy.start()
    for copy in copies:
        copy.wait()
    count = tokens.shape[0]
    width = tokens.shape[1]
    out[:, :half] = tokens[:, :half]
    out[:, half + 128 :] = tokens[:, half:width]
    lane = lax.broadcasted_iota(jnp.int32, (count, 128), 1)
    same = lax.broadcasted_iota(jnp.int32, (count, count), 0) == lax.broadcasted_iota(
        jnp.int32, (count, count), 1
    )

    def column(row):
        return jnp.sum(
            jnp.where(same, jnp.broadcast_to(row, same.shape), 0.0), axis=1, keepdims=True
        )

    note = jnp.zeros((count, 128), jnp.float32)
    for k in range(topk):
        name = column(names[k].astype(jnp.float32))
        weight = column(weights[k])
        low = weight - weight.astype(jnp.bfloat16).astype(jnp.float32)
        for value, at in ((name, k), (weight, topk + k), (low, 2 * topk + k)):
            note = jnp.where(lane == at, value, note)
    out[:, half : half + 128] = note.astype(jnp.bfloat16)


def fetch_kernel(after, *refs, start):
    count = len(refs) // 2
    ins, outs, sems = refs[:count], refs[count:-1], refs[-1]
    pairs = [(a.at[:, start : start + b.shape[1]], b) for a, b in zip(ins[:2], outs[:2])]
    for source, target in zip(ins[2:], outs[2:]):
        width = target.shape[1]
        if source.shape[1] != width:
            own_at = pl.multiple_of(lax.axis_index("ctx") * width, 128)
            source = source.at[:, pl.ds(own_at, width)]
        pairs.append((source, target))
    for copy in start_copies(pairs, sems, PIECES):
        copy.wait()


def stack_kernel(*refs, cuts):
    ins, outs = refs[: len(refs) - len(cuts)], refs[len(refs) - len(cuts) :]
    for out, (low, high) in zip(outs, cuts):
        if ins[0].shape[0] % 16 == 0:
            at = 0
            for ref in ins:
                out[at : at + ref.shape[0], :] = ref[:, low:high]
                at += ref.shape[0]
        else:
            rows = [ref[:, low:high].astype(jnp.float32) for ref in ins]
            out[...] = jnp.concatenate(rows, axis=0).astype(out.dtype)


def attention_kernel(
    after, earlier, earlier_other, queries, latents, attended, even, odd, mixed, sems
):
    width, rows = latents.shape
    pad = even.shape[0] - width
    even[width:, :] = jnp.zeros((pad, 2 * rows), jnp.bfloat16)
    odd[:pad, :] = jnp.zeros((pad, 2 * rows), jnp.bfloat16)
    share = width // 2
    core = lax.axis_index("exp") % 2
    for side, ref in ((core, earlier), (1 - core, earlier_other)):
        even[pl.ds(pl.multiple_of(side * share, 16), share), :rows] = ref[...]
        odd[pl.ds(pl.multiple_of(side * share + pad, 16), share), :rows] = ref[...]
    even[:width, rows:] = latents[...]
    odd[pad:, rows:] = latents[...]
    row = lax.broadcasted_iota(jnp.int32, (rows, 2 * rows), 0)
    key = lax.broadcasted_iota(jnp.int32, (rows, 2 * rows), 1)
    nearest = jnp.where(lax.axis_index("ctx") > 0, 0, rows)
    seen = (key >= nearest) & (key <= row + rows)
    heads = attended.shape[1] // LATENT
    writes = []
    for head in range(heads):
        start = head * width
        keys, start = (even, start) if start % 128 == 0 else (odd, start - pad)
        scores = jnp.dot(
            queries[:, start : start + width + pad], keys[...], preferred_element_type=jnp.float32
        )
        scores = jnp.where(seen, scores * SCALE, jnp.float32(-1e30))
        expo = jnp.exp(scores - jnp.max(scores, axis=-1, keepdims=True))
        probs = (expo / jnp.sum(expo, axis=-1, keepdims=True)).astype(jnp.bfloat16)
        span = slice(head * LATENT, (head + 1) * LATENT)
        mixed[:, span] = times_rows_in(probs, even[:LATENT, :]).astype(jnp.bfloat16)
        write = pltpu.make_async_copy(mixed.at[:, span], attended.at[:, span], sems.at[head])
        write.start()
        writes.append(write)
    for copy in writes:
        copy.wait()


def assemble(place, two_ref, far_ref, two_other_ref, far_other_ref, unit, y_first, start=0):
    span = slice(start, start + place.shape[1])
    order = (0, 2, 1, 3) if y_first else (0, 1, 2, 3)
    for lane, two, far in ((0, two_ref, far_ref), (1, two_other_ref, far_other_ref)):
        for number, block in enumerate(order):
            ref = (two, far)[number // 2]
            rows = slice(number % 2 * unit, (number % 2 + 1) * unit)
            base = (lane * 4 + block) * unit
            place[base : base + unit, :] = ref[rows, span]


def first_kernel(
    two, far, two_other, far_other, gate_w, up_w,
    gate_out, up_out, pick_out, pick_far_out, coef_out,
    tokens, notes, *, unit, tok_dev, capacity, topk,
):
    width = tokens.shape[1]
    rows = tokens.shape[0]
    slots = pick_out.shape[1]
    expert = lax.axis_index("exp")
    assemble(tokens, two, far, two_other, far_other, unit, True)
    gate_out[...] = times_rows_in(tokens[...], gate_w[...])
    up_out[...] = times_rows_in(tokens[...], up_w[...])

    assemble(notes, two, far, two_other, far_other, unit, True, width)
    note = notes[...].astype(jnp.float32)
    lane = lax.broadcasted_iota(jnp.int32, note.shape, 1)
    mine = (note == expert.astype(jnp.float32)) & (lane < topk)
    weight = pltpu.roll(note, 128 - topk, 1) + pltpu.roll(note, 128 - 2 * topk, 1)
    coef = jnp.sum(jnp.where(mine, weight, 0.0), axis=1, keepdims=True)
    hit = jnp.sum(mine.astype(jnp.float32), axis=1, keepdims=True)
    shift = tok_dev.bit_length() - 1
    at = lax.broadcasted_iota(jnp.int32, (rows, rows), 0)
    before = lax.broadcasted_iota(jnp.int32, (rows, rows), 1)
    earlier = ((at >> shift) == (before >> shift)) & (before < at)
    hits = jnp.broadcast_to(hit, (rows, slots))
    rank = jnp.dot(
        earlier.astype(jnp.float32).astype(jnp.bfloat16),
        hits.astype(jnp.bfloat16),
        preferred_element_type=jnp.float32,
    ).astype(jnp.int32)
    row = lax.broadcasted_iota(jnp.int32, (rows, slots), 0)
    slot = (row >> shift) * capacity + rank
    group = unit // tok_dev * capacity
    away = ((row >> (unit.bit_length() - 1)) & 1) == 0
    slot_far = slot + jnp.where(away, group, -group)
    column = lax.broadcasted_iota(jnp.int32, (rows, slots), 1)
    pick_out[...] = jnp.where(slot == column, hits, 0.0).astype(jnp.bfloat16)
    pick_far_out[...] = jnp.where(slot_far == column, hits, 0.0).astype(jnp.bfloat16)
    coef_out[...] = jnp.broadcast_to(coef, coef_out.shape)


def finish_units(tokens, gate_w, up_w, gate_in, up_in, pick, act_out, packed_out, start):
    span = slice(start, start + act_out.shape[1])
    gate = gate_in[:, span] + times_rows_in(tokens[...], gate_w[span, :])
    upper = up_in[:, span] + times_rows_in(tokens[...], up_w[span, :])
    act = (gate / (1.0 + jnp.exp(-gate)) * upper).astype(jnp.bfloat16)
    act_out[...] = act
    packed_out[...] = lax.dot_general(
        pick[...], act, (((0,), (0,)), ((), ())), preferred_element_type=jnp.float32
    ).astype(jnp.bfloat16)


def second_kernel(
    two, far, two_other, far_other, gate_w, up_w, gate_in, up_in, pick,
    act_out, packed_out, tokens, *, unit,
):
    assemble(tokens, two, far, two_other, far_other, unit, False)
    finish_units(tokens, gate_w, up_w, gate_in, up_in, pick, act_out, packed_out, 0)


def third_kernel(tokens, gate_w, up_w, gate_in, up_in, pick, act_out, packed_out, *, start):
    finish_units(tokens, gate_w, up_w, gate_in, up_in, pick, act_out, packed_out, start)


def own_kernel(act_a, act_b, down_own, down_w, out, down_other, sems):
    units = down_own.shape[1]
    few = act_a.shape[1]
    other_at = pl.multiple_of((1 - lax.axis_index("ctx")) * units, 128)
    copies = start_copies([(down_w.at[:, pl.ds(other_at, units)], down_other)], sems, PIECES)
    tall = out.shape[1] // 5 if out.shape[1] % 640 == 0 else out.shape[1]
    for n in range(0, out.shape[1], tall):
        span = slice(n, n + tall)
        out[:, span] = times_rows_in(act_a[...], down_own[span, :few]) + times_rows_in(
            act_b[...], down_own[span, few:]
        )
    for copy in copies:
        copy.wait()


def other_kernel(packed_a, packed_b, pick, coef, down_w, own, keep, give, act, *, start):
    few = packed_a.shape[1]
    for packed, span in ((packed_a, slice(0, few)), (packed_b, slice(few, act.shape[1]))):
        act[:, span] = jnp.dot(
            pick[...], packed[...], preferred_element_type=jnp.float32
        ).astype(jnp.bfloat16)
    half, part = keep.shape
    tall = part // 5 if part % 5 == 0 else part
    for n in range(0, part, tall):
        span = slice(start + n, start + n + tall)
        projected = own[:, span] + times_rows_in(act[...], down_w[span, :])
        projected = projected * coef[:, :1]
        keep[:, n : n + tall] = projected[:half].astype(jnp.bfloat16)
        give[:, n : n + tall] = projected[half:].astype(jnp.bfloat16)


def spread_kernel(keep, got, send, stay, *, y_first):
    unit = keep.shape[0] // 4
    stays, sends = ((0, 1), (2, 3)) if y_first else ((0, 2), (1, 3))
    for out, blocks in ((stay, stays), (send, sends)):
        for number, block in enumerate(blocks):
            span = slice(block * unit, (block + 1) * unit)
            total = keep[span, :].astype(jnp.float32) + got[span, :].astype(jnp.float32)
            out[number * unit : (number + 1) * unit, :] = total.astype(out.dtype)


def cross_kernel(stay, got, send, left, *, y_first):
    unit, part = send.shape[0], stay.shape[1]
    if y_first:
        left[...] = stay[:unit, :] + got[:unit, :].astype(jnp.float32)
        send[...] = (stay[unit:, :] + got[unit:, :].astype(jnp.float32)).astype(jnp.bfloat16)
    else:
        left[:, :part] = stay[:unit, :]
        left[:, part:] = got[:unit, :].astype(jnp.float32)
        send[:, :part] = stay[unit:, :].astype(jnp.bfloat16)
        send[:, part:] = got[unit:, :]


def line_kernel(left_y, got_x, left_x, got_y, *outs):
    ctx = lax.axis_index("ctx")
    count, part = outs[0].shape[0], left_y.shape[1]
    whole = left_x[...] + got_y[...].astype(jnp.float32)
    blocks = (
        (left_y[...], ctx, 0),
        (got_x[...].astype(jnp.float32), 1 - ctx, 0),
        (whole[:, :part], ctx, 1),
        (whole[:, part:], 1 - ctx, 1),
    )
    for value, side, number in blocks:
        at = pl.multiple_of(side * 2 * part + number * part, 128)
        for place, out in enumerate(outs):
            rows = value[place * count : (place + 1) * count]
            out[:, pl.ds(at, part)] = rows.astype(out.dtype)


def sum_kernel(first, *refs):
    total = first[...]
    for ref in refs[:-1]:
        total = total + ref[...].astype(jnp.float32)
    refs[-1][...] = total.astype(refs[-1].dtype)


def on_device_gathered(
    hidden, queries, latents, expert_ids, route_weight, w_gate, w_up, w_down
):
    tok_dev = hidden.shape[1]
    width = hidden.shape[2]
    topk = expert_ids.shape[2]
    units = w_gate.shape[1]
    columns = w_down.shape[1]
    tok_att, key_width = latents.shape
    heads_dev = queries.shape[1] // key_width
    experts = lax.axis_size("exp")
    line = experts // 4
    capacity = min(tok_dev, max(2, 3 * topk * tok_dev // (2 * experts)))
    half = width // 2
    unit = line * tok_dev
    count = 8 * unit
    slots = count // tok_dev * capacity
    bf16, f32 = jnp.bfloat16, jnp.float32

    rows, latents_half = local_kernel(
        lambda *refs: rows_kernel(*refs, half=half, topk=topk),
        [
            (hidden[0], "hbm"),
            (jnp.transpose(expert_ids, (2, 0, 1)), "hbm"),
            (jnp.transpose(route_weight, (2, 0, 1)), "hbm"),
            (latents.T, "hbm"),
        ],
        [((tok_dev, width + 128), bf16, "vmem"), ((key_width // 2, tok_att), bf16, "vmem")],
        [
            pltpu.VMEM((tok_dev, width), bf16),
            pltpu.VMEM((topk, 1, tok_dev), jnp.int32),
            pltpu.VMEM((topk, 1, tok_dev), f32),
            pltpu.SemaphoreType.DMA((4,)),
        ],
        "rows",
    )
    places = (3, 2, 1)
    along = [rows] + [along_line(rows, d) for d in places]
    earlier_kv = swapped(latents_half, "ctx", 1)
    gate_1, up_1, queries_here, latents_here = local_kernel(
        lambda *refs: fetch_kernel(*refs, start=0),
        [
            (rows, "vmem"), (w_gate[0], "hbm"), (w_up[0], "hbm"),
            (queries, "hbm"), (latents.T, "hbm"),
        ],
        [((units, half), bf16, "vmem")] * 2
        + [(queries.shape, bf16, "vmem"), ((key_width, tok_att), bf16, "vmem")],
        [pltpu.SemaphoreType.DMA((4 * PIECES,))],
        "fetch",
    )
    *along, earlier_kv, gate_1, up_1 = lax.optimization_barrier((*along, earlier_kv, gate_1, up_1))
    cuts = ((0, half + 128), (half + 128, width + 128))
    nears = local_kernel(
        lambda *refs: stack_kernel(*refs, cuts=cuts),
        [(row, "vmem") for row in along],
        [((unit, high - low), bf16, "vmem") for low, high in cuts],
        [],
        "stack_line",
    )
    pieces = []
    for near, first, then in zip(nears, (over_y, over_x), (over_x, over_y)):
        got = paired(near, first)
        (two,) = local_kernel(
            lambda *refs, cut=near.shape[1]: stack_kernel(*refs, cuts=((0, cut),)),
            [(near, "vmem"), (got, "vmem")],
            [((2 * unit, near.shape[1]), bf16, "vmem")],
            [],
            "stack_two",
        )
        pieces.append([two, paired(two, then)])
    gate_2, up_2, down_mine = local_kernel(
        lambda *refs: fetch_kernel(*refs, start=half),
        [(pieces[1][0], "vmem"), (w_gate[0], "hbm"), (w_up[0], "hbm"), (w_down[0], "hbm")],
        [((units, half), bf16, "vmem")] * 2 + [((columns, units), bf16, "vmem")],
        [pltpu.SemaphoreType.DMA((3 * PIECES,))],
        "fetch",
    )
    earlier_other = swapped(earlier_kv, "exp", 1)
    pieces[0][1], gate_2, up_2, down_mine, earlier_other = lax.optimization_barrier(
        (pieces[0][1], gate_2, up_2, down_mine, earlier_other)
    )
    for number, (two, far) in enumerate(pieces):
        group = (two, far, swapped(two, "exp", 1), swapped(far, "exp", 1))
        pieces[number] = [(piece, "vmem") for piece in group]

    gate, up, pick, pick_far, coef = local_kernel(
        lambda *refs: first_kernel(
            *refs, unit=unit, tok_dev=tok_dev, capacity=capacity, topk=topk
        ),
        [*pieces[0], (gate_1, "vmem"), (up_1, "vmem")],
        [((count, units), f32, "vmem")] * 2
        + [((count, slots), bf16, "vmem")] * 2
        + [((count, 128), f32, "vmem")],
        [pltpu.VMEM((count, half), bf16), pltpu.VMEM((count, 128), bf16)],
        "gate_up_first",
    )
    few = 2 * units // 3 if units % 384 == 0 else units // 2
    sums_in = [(gate_2, "vmem"), (up_2, "vmem"), (gate, "vmem"), (up, "vmem"), (pick, "vmem")]
    act_a, packed_a, tokens = local_kernel(
        lambda *refs: second_kernel(*refs, unit=unit),
        [*pieces[1], *sums_in],
        [
            ((count, few), bf16, "vmem"),
            ((slots, few), bf16, "vmem"),
            ((count, half), bf16, "vmem"),
        ],
        [],
        "gate_up_second",
    )
    other_a = swapped(packed_a, "ctx", 1)
    act_b, packed_b = local_kernel(
        lambda *refs: third_kernel(*refs, start=few),
        [(tokens, "vmem"), *sums_in],
        [((count, units - few), bf16, "vmem"), ((slots, units - few), bf16, "vmem")],
        [],
        "gate_up_third",
    )
    other_b = swapped(packed_b, "ctx", 1)
    own, down_other = local_kernel(
        own_kernel,
        [(act_a, "vmem"), (act_b, "vmem"), (down_mine, "vmem"), (w_down[0], "hbm")],
        [((count, columns), f32, "vmem"), ((columns, units), bf16, "vmem")],
        [pltpu.SemaphoreType.DMA((PIECES,))],
        "down_own",
    )
    part = columns // 2
    crossing = []
    for start, y_first in ((0, True), (part, False)):
        keep, give = local_kernel(
            lambda *refs, start=start: other_kernel(*refs, start=start),
            [
                (other_a, "vmem"), (other_b, "vmem"), (pick_far, "vmem"), (coef, "vmem"),
                (down_other, "vmem"), (own, "vmem"),
            ],
            [((count // 2, part), bf16, "vmem")] * 2,
            [pltpu.VMEM((count, units), bf16)],
            "down_other",
        )
        send, stay = local_kernel(
            lambda *refs, y_first=y_first: spread_kernel(*refs, y_first=y_first),
            [(keep, "vmem"), (swapped(give, "exp", 1), "vmem")],
            [((2 * unit, part), bf16, "vmem"), ((2 * unit, part), f32, "vmem")],
            [],
            "spread",
        )
        crossing.append((y_first, stay, paired(send, over_y if y_first else over_x)))
    lines = []
    for y_first, stay, got in crossing:
        wide = part if y_first else 2 * part
        send, left = local_kernel(
            lambda *refs, y_first=y_first: cross_kernel(*refs, y_first=y_first),
            [(stay, "vmem"), (got, "vmem")],
            [((unit, wide), bf16, "vmem"), ((unit, wide), f32, "vmem")],
            [],
            "cross",
        )
        lines += [left, paired(send, over_x if y_first else over_y)]
    keep, *sends = local_kernel(
        line_kernel,
        [(block, "vmem") for block in lines],
        [((tok_dev, 2 * columns), f32, "vmem")]
        + [((tok_dev, 2 * columns), bf16, "vmem")] * (line - 1),
        [],
        "line",
    )
    pad = -key_width % 128
    (attended,) = local_kernel(
        attention_kernel,
        [(sends[0], "vmem"), (earlier_kv, "vmem"), (earlier_other, "vmem"), (queries_here, "vmem"), (latents_here, "vmem")],
        [((tok_att, heads_dev * LATENT), bf16, "hbm")],
        [
            pltpu.VMEM((key_width + pad, 2 * tok_att), bf16),
            pltpu.VMEM((key_width + pad, 2 * tok_att), bf16),
            pltpu.VMEM((tok_att, heads_dev * LATENT), bf16),
            pltpu.SemaphoreType.DMA((heads_dev,)),
        ],
        "attention",
    )
    sends = dict(zip(places, sends))
    got = [along_line(sends[d], d) for d in (3, 1, 2)]
    got[-1], attended = lax.optimization_barrier((got[-1], attended))
    (mixed,) = local_kernel(
        sum_kernel,
        [(block, "vmem") for block in (keep, *got)],
        [((tok_dev, 2 * columns), bf16, "result")],
        [],
        "sum",
    )
    return (attended, mixed[None])


def on_device_slots(hidden, queries, latents, expert_ids, route_weight, w_gate, w_up, w_down):
    tok_att = latents.shape[0]
    heads_dev = queries.shape[1] // (LATENT + ROPE)
    tok_dev = hidden.shape[1]
    width = hidden.shape[2]
    topk = expert_ids.shape[2]
    experts = lax.axis_size("exp")
    groups = lax.axis_size("ctx")
    capacity = min(tok_dev, max(2, 3 * topk * tok_dev // (2 * experts)))
    slots = experts * capacity
    earlier_kv = shifted(latents, "ctx", 1)
    keys = jnp.concatenate([earlier_kv, latents], axis=0)
    query_rows = queries.reshape(tok_att, heads_dev, LATENT + ROPE)
    scores = jnp.einsum("thc,kc->htk", query_rows, keys, preferred_element_type=jnp.float32) * SCALE
    row_pos = jnp.arange(tok_att, dtype=jnp.int32)
    key_pos = jnp.arange(2 * tok_att, dtype=jnp.int32)
    seen_own = (key_pos[None, :] >= tok_att) & (key_pos[None, :] - tok_att <= row_pos[:, None])
    seen_prev = (key_pos[None, :] < tok_att) & (lax.axis_index("ctx") > 0)
    scores = jnp.where((seen_own | seen_prev)[None, :, :], scores, jnp.float32(-1e30))
    top = jnp.max(scores, axis=-1, keepdims=True)
    expo = jnp.exp(scores - top)
    probs = (expo / jnp.sum(expo, axis=-1, keepdims=True)).astype(jnp.bfloat16)
    mixed_heads = jnp.einsum(
        "htk,kc->thc", probs, keys[:, :LATENT], preferred_element_type=jnp.float32
    )
    attended = mixed_heads.astype(jnp.bfloat16).reshape(tok_att, heads_dev * LATENT)
    tokens = hidden[0]
    picks = expert_ids[0]
    pick_weight = route_weight[0].reshape(-1)
    tok_hot = token_table(tok_dev, topk)
    slot_hot = place_picks(picks, experts, capacity)
    gate_w = w_gate[0]
    up_w = w_up[0]
    down_w = w_down[0]
    send_matrix = jnp.dot(slot_hot.T, tok_hot).astype(jnp.bfloat16)
    outgoing = jnp.dot(send_matrix, tokens, preferred_element_type=jnp.float32).astype(jnp.bfloat16)
    outgoing = outgoing.reshape(experts, capacity, width)
    arrived = lax.all_to_all(outgoing, "exp", split_axis=0, concat_axis=0, tiled=True)
    piece = lax.all_gather(arrived.reshape(slots, width), "ctx", axis=0, tiled=True)
    gate = times_rows(piece, gate_w)
    upper = times_rows(piece, up_w)
    hidden_units = (jax.nn.silu(gate) * upper).astype(jnp.bfloat16)
    projected = times_rows(lax.all_gather(hidden_units, "ctx", axis=1, tiled=True), down_w)
    columns = projected.astype(jnp.bfloat16).reshape(groups, experts, capacity, down_w.shape[0])
    by_block = lax.all_to_all(columns, "ctx", split_axis=0, concat_axis=3, tiled=True)
    returned = lax.all_to_all(by_block, "exp", split_axis=1, concat_axis=1, tiled=True)
    combine_matrix = jnp.dot(
        slot_hot.T, tok_hot * pick_weight[:, None], precision=lax.Precision.HIGHEST
    )
    back_rows = returned.reshape(slots, width).astype(jnp.float32)
    mixed = jnp.dot(combine_matrix.T, back_rows, precision=lax.Precision.HIGHEST).astype(
        jnp.bfloat16
    )
    return (attended, mixed[None])


def solution(mesh):
    experts, groups = mesh.shape["exp"], mesh.shape["ctx"]
    whole = groups == 2 and experts == 16
    on_device = on_device_gathered if whole else on_device_slots
    placed = (
        P("exp", "ctx", None),
        P("ctx", "exp"),
        P("ctx", None),
        P("exp", "ctx", None),
        P("exp", "ctx", None),
        P("exp", "ctx", None),
        P("exp", "ctx", None),
        P("exp", "ctx", None),
    )
    return jax.shard_map(
        on_device,
        mesh=mesh,
        in_specs=placed,
        out_specs=(P("ctx", "exp"), P("exp", "ctx", None)),
        check_vma=False,
    )
```

```python
import jax
import jax.numpy as jnp
from jax import lax
from jax.experimental import pallas as pl
from jax.experimental.pallas import tpu as pltpu
from jax.sharding import PartitionSpec as P

LATENT = 512
ROPE = 64


SCALE = 0.07216878364870322


def shifted(block, axis, distance):
    devices = range(lax.axis_size(axis))
    route = [(i - distance, i) for i in devices if i - distance in devices]
    return lax.ppermute(block, axis, route)


def place_picks(picks, experts, capacity):
    flat = picks.reshape(-1)
    onehot = (flat[:, None] == jnp.arange(experts, dtype=jnp.int32)[None, :]).astype(jnp.int32)
    earlier = jnp.cumsum(onehot, axis=0) - onehot
    rank = jnp.sum(earlier * onehot, axis=1)
    target = flat * capacity + rank
    return (target[:, None] == jnp.arange(experts * capacity, dtype=jnp.int32)[None, :]).astype(
        jnp.float32
    )


def token_table(tok_count, topk):
    owner = jnp.arange(tok_count * topk, dtype=jnp.int32) // topk
    return (owner[:, None] == jnp.arange(tok_count, dtype=jnp.int32)[None, :]).astype(jnp.float32)


def times_rows(left, right):
    return lax.dot_general(
        left, right, (((1,), (1,)), ((), ())), preferred_element_type=jnp.float32
    )


def swapped(block, axis, bit):
    return lax.ppermute(block, axis, [(i, i ^ bit) for i in range(lax.axis_size(axis))])


def along_line(block, steps):
    return lax.ppermute(
        block, "exp", [(i, i ^ (4 * steps)) for i in range(lax.axis_size("exp"))]
    )


def paired(block, partner):
    count = lax.axis_size("exp")
    both = lax.axis_size("ctx") * count
    route = []
    for i in range(both):
        ctx, exp = partner(i // count, i % count)
        route.append((i, ctx * count + exp))
    return lax.ppermute(block, ("ctx", "exp"), route)


def over_y(ctx, exp):
    return ctx, exp ^ 2


def over_x(ctx, exp):
    return 1 - ctx, exp


def times_rows_in(left, right):
    return lax.dot_general(
        left, right, (((1,), (1,)), ((), ())), preferred_element_type=jnp.float32
    )


def in_vmem(array):
    return pltpu.with_memory_space_constraint(array, pltpu.VMEM)


def in_hbm(array):
    return pltpu.with_memory_space_constraint(array, pltpu.HBM)


def local_kernel(body, ins, outs, scratch, name):
    kinds = {"vmem": pltpu.VMEM, "hbm": pl.ANY, "result": pltpu.VMEM}
    place = {"vmem": in_vmem, "hbm": in_hbm}
    made = [
        pltpu.VMEM(shape, dtype) if kind == "vmem" else jax.ShapeDtypeStruct(shape, dtype)
        for shape, dtype, kind in outs
    ]
    return pl.pallas_call(
        body,
        in_specs=[pl.BlockSpec(memory_space=kinds[kind]) for _, kind in ins],
        out_specs=[pl.BlockSpec(memory_space=kinds[kind]) for _, _, kind in outs],
        out_shape=made,
        scratch_shapes=scratch,
        compiler_params=pltpu.CompilerParams(vmem_limit_bytes=20 * 1024 * 1024),
        cost_estimate=pl.CostEstimate(flops=0, bytes_accessed=0, transcendentals=0),
        name=name,
    )(*[place[kind](array) for array, kind in ins])


def start_copies(pairs, sems, pieces):
    copies = []
    for number, (source, target) in enumerate(pairs):
        step = target.shape[0] // pieces
        for piece in range(pieces):
            span = pl.ds(piece * step, step)
            copy = pltpu.make_async_copy(
                source.at[span, :], target.at[span, :], sems.at[number * pieces + piece]
            )
            copy.start()
            copies.append(copy)
    return copies


PIECES = 4


def rows_kernel(
    tokens_in, names_in, weights_in, latents_in, out, latents, tokens, names, weights, sems, *, half, topk
):
    share = latents.shape[0]
    at = pl.multiple_of(lax.axis_index("exp") % 2 * share, 16)
    copies = [
        pltpu.make_async_copy(source, target, sems.at[number])
        for number, (source, target) in enumerate(
            (
                (tokens_in, tokens),
                (names_in, names),
                (weights_in, weights),
                (latents_in.at[pl.ds(at, share), :], latents),
            )
        )
    ]
    for copy in copies:
        copy.start()
    for copy in copies:
        copy.wait()
    count = tokens.shape[0]
    width = tokens.shape[1]
    out[:, :half] = tokens[:, :half]
    out[:, half + 128 :] = tokens[:, half:width]
    lane = lax.broadcasted_iota(jnp.int32, (count, 128), 1)
    same = lax.broadcasted_iota(jnp.int32, (count, count), 0) == lax.broadcasted_iota(
        jnp.int32, (count, count), 1
    )

    def column(row):
        return jnp.sum(
            jnp.where(same, jnp.broadcast_to(row, same.shape), 0.0), axis=1, keepdims=True
        )

    note = jnp.zeros((count, 128), jnp.float32)
    for k in range(topk):
        name = column(names[k].astype(jnp.float32))
        weight = column(weights[k])
        low = weight - weight.astype(jnp.bfloat16).astype(jnp.float32)
        for value, at in ((name, k), (weight, topk + k), (low, 2 * topk + k)):
            note = jnp.where(lane == at, value, note)
    out[:, half : half + 128] = note.astype(jnp.bfloat16)


def fetch_kernel(after, *refs, start):
    count = len(refs) // 2
    ins, outs, sems = refs[:count], refs[count:-1], refs[-1]
    pairs = [(a.at[:, start : start + b.shape[1]], b) for a, b in zip(ins[:2], outs[:2])]
    for source, target in zip(ins[2:], outs[2:]):
        width = target.shape[1]
        if source.shape[1] != width:
            own_at = pl.multiple_of(lax.axis_index("ctx") * width, 128)
            source = source.at[:, pl.ds(own_at, width)]
        pairs.append((source, target))
    for copy in start_copies(pairs, sems, PIECES):
        copy.wait()


def stack_kernel(*refs, cuts):
    ins, outs = refs[: len(refs) - len(cuts)], refs[len(refs) - len(cuts) :]
    for out, (low, high) in zip(outs, cuts):
        if ins[0].shape[0] % 16 == 0:
            at = 0
            for ref in ins:
                out[at : at + ref.shape[0], :] = ref[:, low:high]
                at += ref.shape[0]
        else:
            rows = [ref[:, low:high].astype(jnp.float32) for ref in ins]
            out[...] = jnp.concatenate(rows, axis=0).astype(out.dtype)


def attention_kernel(
    after, earlier, earlier_other, queries, latents, attended, even, odd, mixed, sems
):
    width, rows = latents.shape
    pad = even.shape[0] - width
    even[width:, :] = jnp.zeros((pad, 2 * rows), jnp.bfloat16)
    odd[:pad, :] = jnp.zeros((pad, 2 * rows), jnp.bfloat16)
    share = width // 2
    core = lax.axis_index("exp") % 2
    for side, ref in ((core, earlier), (1 - core, earlier_other)):
        even[pl.ds(pl.multiple_of(side * share, 16), share), :rows] = ref[...]
        odd[pl.ds(pl.multiple_of(side * share + pad, 16), share), :rows] = ref[...]
    even[:width, rows:] = latents[...]
    odd[pad:, rows:] = latents[...]
    row = lax.broadcasted_iota(jnp.int32, (rows, 2 * rows), 0)
    key = lax.broadcasted_iota(jnp.int32, (rows, 2 * rows), 1)
    nearest = jnp.where(lax.axis_index("ctx") > 0, 0, rows)
    seen = (key >= nearest) & (key <= row + rows)
    heads = attended.shape[1] // LATENT
    writes = []
    for head in range(heads):
        start = head * width
        keys, start = (even, start) if start % 128 == 0 else (odd, start - pad)
        scores = jnp.dot(
            queries[:, start : start + width + pad], keys[...], preferred_element_type=jnp.float32
        )
        scores = jnp.where(seen, scores * SCALE, jnp.float32(-1e30))
        expo = jnp.exp(scores - jnp.max(scores, axis=-1, keepdims=True))
        probs = (expo / jnp.sum(expo, axis=-1, keepdims=True)).astype(jnp.bfloat16)
        span = slice(head * LATENT, (head + 1) * LATENT)
        mixed[:, span] = times_rows_in(probs, even[:LATENT, :]).astype(jnp.bfloat16)
        write = pltpu.make_async_copy(mixed.at[:, span], attended.at[:, span], sems.at[head])
        write.start()
        writes.append(write)
    for copy in writes:
        copy.wait()


def assemble(place, two_ref, far_ref, two_other_ref, far_other_ref, unit, y_first, start=0):
    span = slice(start, start + place.shape[1])
    order = (0, 2, 1, 3) if y_first else (0, 1, 2, 3)
    for lane, two, far in ((0, two_ref, far_ref), (1, two_other_ref, far_other_ref)):
        for number, block in enumerate(order):
            ref = (two, far)[number // 2]
            rows = slice(number % 2 * unit, (number % 2 + 1) * unit)
            base = (lane * 4 + block) * unit
            place[base : base + unit, :] = ref[rows, span]


def first_kernel(
    two, far, two_other, far_other, gate_w, up_w,
    gate_out, up_out, pick_out, pick_far_out, coef_out,
    tokens, notes, *, unit, tok_dev, capacity, topk,
):
    width = tokens.shape[1]
    rows = tokens.shape[0]
    slots = pick_out.shape[1]
    expert = lax.axis_index("exp")
    assemble(tokens, two, far, two_other, far_other, unit, True)
    gate_out[...] = times_rows_in(tokens[...], gate_w[...])
    up_out[...] = times_rows_in(tokens[...], up_w[...])

    assemble(notes, two, far, two_other, far_other, unit, True, width)
    note = notes[...].astype(jnp.float32)
    lane = lax.broadcasted_iota(jnp.int32, note.shape, 1)
    mine = (note == expert.astype(jnp.float32)) & (lane < topk)
    weight = pltpu.roll(note, 128 - topk, 1) + pltpu.roll(note, 128 - 2 * topk, 1)
    coef = jnp.sum(jnp.where(mine, weight, 0.0), axis=1, keepdims=True)
    hit = jnp.sum(mine.astype(jnp.float32), axis=1, keepdims=True)
    shift = tok_dev.bit_length() - 1
    at = lax.broadcasted_iota(jnp.int32, (rows, rows), 0)
    before = lax.broadcasted_iota(jnp.int32, (rows, rows), 1)
    earlier = ((at >> shift) == (before >> shift)) & (before < at)
    hits = jnp.broadcast_to(hit, (rows, slots))
    rank = jnp.dot(
        earlier.astype(jnp.float32).astype(jnp.bfloat16),
        hits.astype(jnp.bfloat16),
        preferred_element_type=jnp.float32,
    ).astype(jnp.int32)
    row = lax.broadcasted_iota(jnp.int32, (rows, slots), 0)
    slot = (row >> shift) * capacity + rank
    group = unit // tok_dev * capacity
    away = ((row >> (unit.bit_length() - 1)) & 1) == 0
    slot_far = slot + jnp.where(away, group, -group)
    column = lax.broadcasted_iota(jnp.int32, (rows, slots), 1)
    pick_out[...] = jnp.where(slot == column, hits, 0.0).astype(jnp.bfloat16)
    pick_far_out[...] = jnp.where(slot_far == column, hits, 0.0).astype(jnp.bfloat16)
    coef_out[...] = jnp.broadcast_to(coef, coef_out.shape)


def finish_units(tokens, gate_w, up_w, gate_in, up_in, pick, act_out, packed_out, start):
    span = slice(start, start + act_out.shape[1])
    gate = gate_in[:, span] + times_rows_in(tokens[...], gate_w[span, :])
    upper = up_in[:, span] + times_rows_in(tokens[...], up_w[span, :])
    act = (gate / (1.0 + jnp.exp(-gate)) * upper).astype(jnp.bfloat16)
    act_out[...] = act
    packed_out[...] = lax.dot_general(
        pick[...], act, (((0,), (0,)), ((), ())), preferred_element_type=jnp.float32
    ).astype(jnp.bfloat16)


def second_kernel(
    two, far, two_other, far_other, gate_w, up_w, gate_in, up_in, pick,
    act_out, packed_out, tokens, *, unit,
):
    assemble(tokens, two, far, two_other, far_other, unit, False)
    finish_units(tokens, gate_w, up_w, gate_in, up_in, pick, act_out, packed_out, 0)


def third_kernel(tokens, gate_w, up_w, gate_in, up_in, pick, act_out, packed_out, *, start):
    finish_units(tokens, gate_w, up_w, gate_in, up_in, pick, act_out, packed_out, start)


def own_kernel(act_a, act_b, down_own, down_w, out, down_other, sems):
    units = down_own.shape[1]
    few = act_a.shape[1]
    other_at = pl.multiple_of((1 - lax.axis_index("ctx")) * units, 128)
    copies = start_copies([(down_w.at[:, pl.ds(other_at, units)], down_other)], sems, PIECES)
    tall = out.shape[1] // 5 if out.shape[1] % 640 == 0 else out.shape[1]
    for n in range(0, out.shape[1], tall):
        span = slice(n, n + tall)
        out[:, span] = times_rows_in(act_a[...], down_own[span, :few]) + times_rows_in(
            act_b[...], down_own[span, few:]
        )
    for copy in copies:
        copy.wait()


def other_kernel(packed_a, packed_b, pick, coef, down_w, own, keep, give, act, *, start):
    few = packed_a.shape[1]
    for packed, span in ((packed_a, slice(0, few)), (packed_b, slice(few, act.shape[1]))):
        act[:, span] = jnp.dot(
            pick[...], packed[...], preferred_element_type=jnp.float32
        ).astype(jnp.bfloat16)
    half, part = keep.shape
    tall = part // 5 if part % 5 == 0 else part
    for n in range(0, part, tall):
        span = slice(start + n, start + n + tall)
        projected = own[:, span] + times_rows_in(act[...], down_w[span, :])
        projected = projected * coef[:, :1]
        keep[:, n : n + tall] = projected[:half]
        give[:, n : n + tall] = projected[half:].astype(jnp.bfloat16)


def spread_kernel(keep, got, send, stay, *, y_first):
    unit = keep.shape[0] // 4
    stays, sends = ((0, 1), (2, 3)) if y_first else ((0, 2), (1, 3))
    for out, blocks in ((stay, stays), (send, sends)):
        for number, block in enumerate(blocks):
            span = slice(block * unit, (block + 1) * unit)
            total = keep[span, :] + got[span, :].astype(jnp.float32)
            out[number * unit : (number + 1) * unit, :] = total.astype(out.dtype)


def cross_kernel(stay, got, send, left, *, y_first):
    unit, part = send.shape[0], stay.shape[1]
    if y_first:
        left[...] = stay[:unit, :] + got[:unit, :].astype(jnp.float32)
        send[...] = (stay[unit:, :] + got[unit:, :].astype(jnp.float32)).astype(jnp.bfloat16)
    else:
        left[:, :part] = stay[:unit, :]
        left[:, part:] = got[:unit, :].astype(jnp.float32)
        send[:, :part] = stay[unit:, :].astype(jnp.bfloat16)
        send[:, part:] = got[unit:, :]


def line_kernel(left_y, got_x, left_x, got_y, *outs):
    ctx = lax.axis_index("ctx")
    count, part = outs[0].shape[0], left_y.shape[1]
    whole = left_x[...] + got_y[...].astype(jnp.float32)
    blocks = (
        (left_y[...], ctx, 0),
        (got_x[...].astype(jnp.float32), 1 - ctx, 0),
        (whole[:, :part], ctx, 1),
        (whole[:, part:], 1 - ctx, 1),
    )
    for value, side, number in blocks:
        at = pl.multiple_of(side * 2 * part + number * part, 128)
        for place, out in enumerate(outs):
            rows = value[place * count : (place + 1) * count]
            out[:, pl.ds(at, part)] = rows.astype(out.dtype)


def sum_kernel(first, *refs):
    total = first[...]
    for ref in refs[:-1]:
        total = total + ref[...].astype(jnp.float32)
    refs[-1][...] = total.astype(refs[-1].dtype)


def on_device_gathered(
    hidden, queries, latents, expert_ids, route_weight, w_gate, w_up, w_down
):
    tok_dev = hidden.shape[1]
    width = hidden.shape[2]
    topk = expert_ids.shape[2]
    units = w_gate.shape[1]
    columns = w_down.shape[1]
    tok_att, key_width = latents.shape
    heads_dev = queries.shape[1] // key_width
    experts = lax.axis_size("exp")
    line = experts // 4
    capacity = min(tok_dev, max(2, 3 * topk * tok_dev // (2 * experts)))
    half = width // 2
    unit = line * tok_dev
    count = 8 * unit
    slots = count // tok_dev * capacity
    bf16, f32 = jnp.bfloat16, jnp.float32

    rows, latents_half = local_kernel(
        lambda *refs: rows_kernel(*refs, half=half, topk=topk),
        [
            (hidden[0], "hbm"),
            (jnp.transpose(expert_ids, (2, 0, 1)), "hbm"),
            (jnp.transpose(route_weight, (2, 0, 1)), "hbm"),
            (latents.T, "hbm"),
        ],
        [((tok_dev, width + 128), bf16, "vmem"), ((key_width // 2, tok_att), bf16, "vmem")],
        [
            pltpu.VMEM((tok_dev, width), bf16),
            pltpu.VMEM((topk, 1, tok_dev), jnp.int32),
            pltpu.VMEM((topk, 1, tok_dev), f32),
            pltpu.SemaphoreType.DMA((4,)),
        ],
        "rows",
    )
    places = (3, 2, 1)
    along = [rows] + [along_line(rows, d) for d in places]
    earlier_kv = swapped(latents_half, "ctx", 1)
    gate_1, up_1, queries_here, latents_here = local_kernel(
        lambda *refs: fetch_kernel(*refs, start=0),
        [
            (rows, "vmem"), (w_gate[0], "hbm"), (w_up[0], "hbm"),
            (queries, "hbm"), (latents.T, "hbm"),
        ],
        [((units, half), bf16, "vmem")] * 2
        + [(queries.shape, bf16, "vmem"), ((key_width, tok_att), bf16, "vmem")],
        [pltpu.SemaphoreType.DMA((4 * PIECES,))],
        "fetch",
    )
    *along, earlier_kv, gate_1, up_1 = lax.optimization_barrier((*along, earlier_kv, gate_1, up_1))
    cuts = ((0, half + 128), (half + 128, width + 128))
    nears = local_kernel(
        lambda *refs: stack_kernel(*refs, cuts=cuts),
        [(row, "vmem") for row in along],
        [((unit, high - low), bf16, "vmem") for low, high in cuts],
        [],
        "stack_line",
    )
    pieces = []
    for near, first, then in zip(nears, (over_y, over_x), (over_x, over_y)):
        got = paired(near, first)
        (two,) = local_kernel(
            lambda *refs, cut=near.shape[1]: stack_kernel(*refs, cuts=((0, cut),)),
            [(near, "vmem"), (got, "vmem")],
            [((2 * unit, near.shape[1]), bf16, "vmem")],
            [],
            "stack_two",
        )
        pieces.append([two, paired(two, then)])
    gate_2, up_2, down_mine = local_kernel(
        lambda *refs: fetch_kernel(*refs, start=half),
        [(pieces[1][0], "vmem"), (w_gate[0], "hbm"), (w_up[0], "hbm"), (w_down[0], "hbm")],
        [((units, half), bf16, "vmem")] * 2 + [((columns, units), bf16, "vmem")],
        [pltpu.SemaphoreType.DMA((3 * PIECES,))],
        "fetch",
    )
    earlier_other = swapped(earlier_kv, "exp", 1)
    pieces[0][1], gate_2, up_2, down_mine, earlier_other = lax.optimization_barrier(
        (pieces[0][1], gate_2, up_2, down_mine, earlier_other)
    )
    for number, (two, far) in enumerate(pieces):
        group = (two, far, swapped(two, "exp", 1), swapped(far, "exp", 1))
        pieces[number] = [(piece, "vmem") for piece in group]

    gate, up, pick, pick_far, coef = local_kernel(
        lambda *refs: first_kernel(
            *refs, unit=unit, tok_dev=tok_dev, capacity=capacity, topk=topk
        ),
        [*pieces[0], (gate_1, "vmem"), (up_1, "vmem")],
        [((count, units), f32, "vmem")] * 2
        + [((count, slots), bf16, "vmem")] * 2
        + [((count, 128), f32, "vmem")],
        [pltpu.VMEM((count, half), bf16), pltpu.VMEM((count, 128), bf16)],
        "gate_up_first",
    )
    few = 2 * units // 3 if units % 384 == 0 else units // 2
    sums_in = [(gate_2, "vmem"), (up_2, "vmem"), (gate, "vmem"), (up, "vmem"), (pick, "vmem")]
    act_a, packed_a, tokens = local_kernel(
        lambda *refs: second_kernel(*refs, unit=unit),
        [*pieces[1], *sums_in],
        [
            ((count, few), bf16, "vmem"),
            ((slots, few), bf16, "vmem"),
            ((count, half), bf16, "vmem"),
        ],
        [],
        "gate_up_second",
    )
    other_a = swapped(packed_a, "ctx", 1)
    act_b, packed_b = local_kernel(
        lambda *refs: third_kernel(*refs, start=few),
        [(tokens, "vmem"), *sums_in],
        [((count, units - few), bf16, "vmem"), ((slots, units - few), bf16, "vmem")],
        [],
        "gate_up_third",
    )
    other_b = swapped(packed_b, "ctx", 1)
    own, down_other = local_kernel(
        own_kernel,
        [(act_a, "vmem"), (act_b, "vmem"), (down_mine, "vmem"), (w_down[0], "hbm")],
        [((count, columns), f32, "vmem"), ((columns, units), bf16, "vmem")],
        [pltpu.SemaphoreType.DMA((PIECES,))],
        "down_own",
    )
    part = columns // 2
    crossing = []
    for start, y_first in ((0, True), (part, False)):
        keep, give = local_kernel(
            lambda *refs, start=start: other_kernel(*refs, start=start),
            [
                (other_a, "vmem"), (other_b, "vmem"), (pick_far, "vmem"), (coef, "vmem"),
                (down_other, "vmem"), (own, "vmem"),
            ],
            [((count // 2, part), f32, "vmem"), ((count // 2, part), bf16, "vmem")],
            [pltpu.VMEM((count, units), bf16)],
            "down_other",
        )
        send, stay = local_kernel(
            lambda *refs, y_first=y_first: spread_kernel(*refs, y_first=y_first),
            [(keep, "vmem"), (swapped(give, "exp", 1), "vmem")],
            [((2 * unit, part), bf16, "vmem"), ((2 * unit, part), f32, "vmem")],
            [],
            "spread",
        )
        crossing.append((y_first, stay, paired(send, over_y if y_first else over_x)))
    lines = []
    for y_first, stay, got in crossing:
        wide = part if y_first else 2 * part
        send, left = local_kernel(
            lambda *refs, y_first=y_first: cross_kernel(*refs, y_first=y_first),
            [(stay, "vmem"), (got, "vmem")],
            [((unit, wide), bf16, "vmem"), ((unit, wide), f32, "vmem")],
            [],
            "cross",
        )
        lines += [left, paired(send, over_x if y_first else over_y)]
    keep, *sends = local_kernel(
        line_kernel,
        [(block, "vmem") for block in lines],
        [((tok_dev, 2 * columns), f32, "vmem")]
        + [((tok_dev, 2 * columns), bf16, "vmem")] * (line - 1),
        [],
        "line",
    )
    pad = -key_width % 128
    (attended,) = local_kernel(
        attention_kernel,
        [(sends[0], "vmem"), (earlier_kv, "vmem"), (earlier_other, "vmem"), (queries_here, "vmem"), (latents_here, "vmem")],
        [((tok_att, heads_dev * LATENT), bf16, "hbm")],
        [
            pltpu.VMEM((key_width + pad, 2 * tok_att), bf16),
            pltpu.VMEM((key_width + pad, 2 * tok_att), bf16),
            pltpu.VMEM((tok_att, heads_dev * LATENT), bf16),
            pltpu.SemaphoreType.DMA((heads_dev,)),
        ],
        "attention",
    )
    sends = dict(zip(places, sends))
    got = [along_line(sends[d], d) for d in (3, 1, 2)]
    got[-1], attended = lax.optimization_barrier((got[-1], attended))
    (mixed,) = local_kernel(
        sum_kernel,
        [(block, "vmem") for block in (keep, *got)],
        [((tok_dev, 2 * columns), bf16, "result")],
        [],
        "sum",
    )
    return (attended, mixed[None])


def on_device_slots(hidden, queries, latents, expert_ids, route_weight, w_gate, w_up, w_down):
    tok_att = latents.shape[0]
    heads_dev = queries.shape[1] // (LATENT + ROPE)
    tok_dev = hidden.shape[1]
    width = hidden.shape[2]
    topk = expert_ids.shape[2]
    experts = lax.axis_size("exp")
    groups = lax.axis_size("ctx")
    capacity = min(tok_dev, max(2, 3 * topk * tok_dev // (2 * experts)))
    slots = experts * capacity
    earlier_kv = shifted(latents, "ctx", 1)
    keys = jnp.concatenate([earlier_kv, latents], axis=0)
    query_rows = queries.reshape(tok_att, heads_dev, LATENT + ROPE)
    scores = jnp.einsum("thc,kc->htk", query_rows, keys, preferred_element_type=jnp.float32) * SCALE
    row_pos = jnp.arange(tok_att, dtype=jnp.int32)
    key_pos = jnp.arange(2 * tok_att, dtype=jnp.int32)
    seen_own = (key_pos[None, :] >= tok_att) & (key_pos[None, :] - tok_att <= row_pos[:, None])
    seen_prev = (key_pos[None, :] < tok_att) & (lax.axis_index("ctx") > 0)
    scores = jnp.where((seen_own | seen_prev)[None, :, :], scores, jnp.float32(-1e30))
    top = jnp.max(scores, axis=-1, keepdims=True)
    expo = jnp.exp(scores - top)
    probs = (expo / jnp.sum(expo, axis=-1, keepdims=True)).astype(jnp.bfloat16)
    mixed_heads = jnp.einsum(
        "htk,kc->thc", probs, keys[:, :LATENT], preferred_element_type=jnp.float32
    )
    attended = mixed_heads.astype(jnp.bfloat16).reshape(tok_att, heads_dev * LATENT)
    tokens = hidden[0]
    picks = expert_ids[0]
    pick_weight = route_weight[0].reshape(-1)
    tok_hot = token_table(tok_dev, topk)
    slot_hot = place_picks(picks, experts, capacity)
    gate_w = w_gate[0]
    up_w = w_up[0]
    down_w = w_down[0]
    send_matrix = jnp.dot(slot_hot.T, tok_hot).astype(jnp.bfloat16)
    outgoing = jnp.dot(send_matrix, tokens, preferred_element_type=jnp.float32).astype(jnp.bfloat16)
    outgoing = outgoing.reshape(experts, capacity, width)
    arrived = lax.all_to_all(outgoing, "exp", split_axis=0, concat_axis=0, tiled=True)
    piece = lax.all_gather(arrived.reshape(slots, width), "ctx", axis=0, tiled=True)
    gate = times_rows(piece, gate_w)
    upper = times_rows(piece, up_w)
    hidden_units = (jax.nn.silu(gate) * upper).astype(jnp.bfloat16)
    projected = times_rows(lax.all_gather(hidden_units, "ctx", axis=1, tiled=True), down_w)
    columns = projected.astype(jnp.bfloat16).reshape(groups, experts, capacity, down_w.shape[0])
    by_block = lax.all_to_all(columns, "ctx", split_axis=0, concat_axis=3, tiled=True)
    returned = lax.all_to_all(by_block, "exp", split_axis=1, concat_axis=1, tiled=True)
    combine_matrix = jnp.dot(
        slot_hot.T, tok_hot * pick_weight[:, None], precision=lax.Precision.HIGHEST
    )
    back_rows = returned.reshape(slots, width).astype(jnp.float32)
    mixed = jnp.dot(combine_matrix.T, back_rows, precision=lax.Precision.HIGHEST).astype(
        jnp.bfloat16
    )
    return (attended, mixed[None])


def solution(mesh):
    experts, groups = mesh.shape["exp"], mesh.shape["ctx"]
    whole = groups == 2 and experts == 16
    on_device = on_device_gathered if whole else on_device_slots
    placed = (
        P("exp", "ctx", None),
        P("ctx", "exp"),
        P("ctx", None),
        P("exp", "ctx", None),
        P("exp", "ctx", None),
        P("exp", "ctx", None),
        P("exp", "ctx", None),
        P("exp", "ctx", None),
    )
    return jax.shard_map(
        on_device,
        mesh=mesh,
        in_specs=placed,
        out_specs=(P("ctx", "exp"), P("exp", "ctx", None)),
        check_vma=False,
    )
```

```python
import jax
import jax.numpy as jnp
from jax import lax
from jax.experimental import pallas as pl
from jax.experimental.pallas import tpu as pltpu
from jax.sharding import PartitionSpec as P

LATENT = 512
ROPE = 64


SCALE = 0.07216878364870322


def shifted(block, axis, distance):
    devices = range(lax.axis_size(axis))
    route = [(i - distance, i) for i in devices if i - distance in devices]
    return lax.ppermute(block, axis, route)


def place_picks(picks, experts, capacity):
    flat = picks.reshape(-1)
    onehot = (flat[:, None] == jnp.arange(experts, dtype=jnp.int32)[None, :]).astype(jnp.int32)
    earlier = jnp.cumsum(onehot, axis=0) - onehot
    rank = jnp.sum(earlier * onehot, axis=1)
    target = flat * capacity + rank
    return (target[:, None] == jnp.arange(experts * capacity, dtype=jnp.int32)[None, :]).astype(
        jnp.float32
    )


def token_table(tok_count, topk):
    owner = jnp.arange(tok_count * topk, dtype=jnp.int32) // topk
    return (owner[:, None] == jnp.arange(tok_count, dtype=jnp.int32)[None, :]).astype(jnp.float32)


def times_rows(left, right):
    return lax.dot_general(
        left, right, (((1,), (1,)), ((), ())), preferred_element_type=jnp.float32
    )


def swapped(block, axis, bit):
    return lax.ppermute(block, axis, [(i, i ^ bit) for i in range(lax.axis_size(axis))])


def along_line(block, steps):
    return lax.ppermute(
        block, "exp", [(i, i ^ (4 * steps)) for i in range(lax.axis_size("exp"))]
    )


def paired(block, partner):
    count = lax.axis_size("exp")
    both = lax.axis_size("ctx") * count
    route = []
    for i in range(both):
        ctx, exp = partner(i // count, i % count)
        route.append((i, ctx * count + exp))
    return lax.ppermute(block, ("ctx", "exp"), route)


def over_y(ctx, exp):
    return ctx, exp ^ 2


def over_x(ctx, exp):
    return 1 - ctx, exp


def times_rows_in(left, right):
    return lax.dot_general(
        left, right, (((1,), (1,)), ((), ())), preferred_element_type=jnp.float32
    )


def in_vmem(array):
    return pltpu.with_memory_space_constraint(array, pltpu.VMEM)


def in_hbm(array):
    return pltpu.with_memory_space_constraint(array, pltpu.HBM)


def local_kernel(body, ins, outs, scratch, name):
    kinds = {"vmem": pltpu.VMEM, "hbm": pl.ANY, "result": pltpu.VMEM}
    place = {"vmem": in_vmem, "hbm": in_hbm}
    made = [
        pltpu.VMEM(shape, dtype) if kind == "vmem" else jax.ShapeDtypeStruct(shape, dtype)
        for shape, dtype, kind in outs
    ]
    return pl.pallas_call(
        body,
        in_specs=[pl.BlockSpec(memory_space=kinds[kind]) for _, kind in ins],
        out_specs=[pl.BlockSpec(memory_space=kinds[kind]) for _, _, kind in outs],
        out_shape=made,
        scratch_shapes=scratch,
        compiler_params=pltpu.CompilerParams(vmem_limit_bytes=20 * 1024 * 1024),
        cost_estimate=pl.CostEstimate(flops=0, bytes_accessed=0, transcendentals=0),
        name=name,
    )(*[place[kind](array) for array, kind in ins])


def start_copies(pairs, sems, pieces):
    copies = []
    for number, (source, target) in enumerate(pairs):
        step = target.shape[0] // pieces
        for piece in range(pieces):
            span = pl.ds(piece * step, step)
            copy = pltpu.make_async_copy(
                source.at[span, :], target.at[span, :], sems.at[number * pieces + piece]
            )
            copy.start()
            copies.append(copy)
    return copies


PIECES = 4


def rows_kernel(
    tokens_in, names_in, weights_in, latents_in, out, latents, tokens, names, weights, sems, *, half, topk
):
    share = latents.shape[0]
    at = pl.multiple_of(lax.axis_index("exp") % 2 * share, 16)
    copies = [
        pltpu.make_async_copy(source, target, sems.at[number])
        for number, (source, target) in enumerate(
            (
                (names_in, names),
                (weights_in, weights),
                (tokens_in, tokens),
                (latents_in.at[pl.ds(at, share), :], latents),
            )
        )
    ]
    for copy in copies:
        copy.start()
    count = tokens.shape[0]
    width = tokens.shape[1]
    lane = lax.broadcasted_iota(jnp.int32, (count, 128), 1)
    same = lax.broadcasted_iota(jnp.int32, (count, count), 0) == lax.broadcasted_iota(
        jnp.int32, (count, count), 1
    )

    def column(row):
        return jnp.sum(
            jnp.where(same, jnp.broadcast_to(row, same.shape), 0.0), axis=1, keepdims=True
        )

    for copy in copies[:2]:
        copy.wait()
    note = jnp.zeros((count, 128), jnp.float32)
    for k in range(topk):
        name = column(names[k].astype(jnp.float32))
        weight = column(weights[k])
        low = weight - weight.astype(jnp.bfloat16).astype(jnp.float32)
        for value, at in ((name, k), (weight, topk + k), (low, 2 * topk + k)):
            note = jnp.where(lane == at, value, note)
    out[:, half : half + 128] = note.astype(jnp.bfloat16)
    for copy in copies[2:]:
        copy.wait()
    out[:, :half] = tokens[:, :half]
    out[:, half + 128 :] = tokens[:, half:width]


def fetch_kernel(after, *refs, start):
    count = len(refs) // 2
    ins, outs, sems = refs[:count], refs[count:-1], refs[-1]
    pairs = [(a.at[:, start : start + b.shape[1]], b) for a, b in zip(ins[:2], outs[:2])]
    for source, target in zip(ins[2:], outs[2:]):
        width = target.shape[1]
        if source.shape[1] != width:
            own_at = pl.multiple_of(lax.axis_index("ctx") * width, 128)
            source = source.at[:, pl.ds(own_at, width)]
        pairs.append((source, target))
    for copy in start_copies(pairs, sems, PIECES):
        copy.wait()


def stack_kernel(*refs, cuts):
    ins, outs = refs[: len(refs) - len(cuts)], refs[len(refs) - len(cuts) :]
    for out, (low, high) in zip(outs, cuts):
        if ins[0].shape[0] % 16 == 0:
            at = 0
            for ref in ins:
                out[at : at + ref.shape[0], :] = ref[:, low:high]
                at += ref.shape[0]
        else:
            rows = [ref[:, low:high].astype(jnp.float32) for ref in ins]
            out[...] = jnp.concatenate(rows, axis=0).astype(out.dtype)


def attention_kernel(
    after, earlier, earlier_other, queries, latents, attended, even, odd, mixed, sems
):
    width, rows = latents.shape
    pad = even.shape[0] - width
    even[width:, :] = jnp.zeros((pad, 2 * rows), jnp.bfloat16)
    odd[:pad, :] = jnp.zeros((pad, 2 * rows), jnp.bfloat16)
    share = width // 2
    core = lax.axis_index("exp") % 2
    for side, ref in ((core, earlier), (1 - core, earlier_other)):
        even[pl.ds(pl.multiple_of(side * share, 16), share), :rows] = ref[...]
        odd[pl.ds(pl.multiple_of(side * share + pad, 16), share), :rows] = ref[...]
    even[:width, rows:] = latents[...]
    odd[pad:, rows:] = latents[...]
    row = lax.broadcasted_iota(jnp.int32, (rows, 2 * rows), 0)
    key = lax.broadcasted_iota(jnp.int32, (rows, 2 * rows), 1)
    nearest = jnp.where(lax.axis_index("ctx") > 0, 0, rows)
    seen = (key >= nearest) & (key <= row + rows)
    heads = attended.shape[1] // LATENT
    writes = []
    for head in range(heads):
        start = head * width
        keys, start = (even, start) if start % 128 == 0 else (odd, start - pad)
        scores = jnp.dot(
            queries[:, start : start + width + pad], keys[...], preferred_element_type=jnp.float32
        )
        scores = jnp.where(seen, scores * SCALE, jnp.float32(-1e30))
        expo = jnp.exp(scores - jnp.max(scores, axis=-1, keepdims=True))
        probs = (expo / jnp.sum(expo, axis=-1, keepdims=True)).astype(jnp.bfloat16)
        span = slice(head * LATENT, (head + 1) * LATENT)
        mixed[:, span] = times_rows_in(probs, even[:LATENT, :]).astype(jnp.bfloat16)
        write = pltpu.make_async_copy(mixed.at[:, span], attended.at[:, span], sems.at[head])
        write.start()
        writes.append(write)
    for copy in writes:
        copy.wait()


def assemble(place, two_ref, far_ref, two_other_ref, far_other_ref, unit, y_first, start=0):
    span = slice(start, start + place.shape[1])
    order = (0, 2, 1, 3) if y_first else (0, 1, 2, 3)
    for lane, two, far in ((0, two_ref, far_ref), (1, two_other_ref, far_other_ref)):
        for number, block in enumerate(order):
            ref = (two, far)[number // 2]
            rows = slice(number % 2 * unit, (number % 2 + 1) * unit)
            base = (lane * 4 + block) * unit
            place[base : base + unit, :] = ref[rows, span]


def first_kernel(
    two, far, two_other, far_other, gate_w, up_w,
    gate_out, up_out, pick_out, pick_far_out, coef_out,
    tokens, notes, *, unit, tok_dev, capacity, topk,
):
    width = tokens.shape[1]
    rows = tokens.shape[0]
    slots = pick_out.shape[1]
    expert = lax.axis_index("exp")
    assemble(tokens, two, far, two_other, far_other, unit, False)
    gate_out[...] = times_rows_in(tokens[...], gate_w[...])
    up_out[...] = times_rows_in(tokens[...], up_w[...])

    assemble(notes, two, far, two_other, far_other, unit, False, width)
    note = notes[...].astype(jnp.float32)
    lane = lax.broadcasted_iota(jnp.int32, note.shape, 1)
    mine = (note == expert.astype(jnp.float32)) & (lane < topk)
    weight = pltpu.roll(note, 128 - topk, 1) + pltpu.roll(note, 128 - 2 * topk, 1)
    coef = jnp.sum(jnp.where(mine, weight, 0.0), axis=1, keepdims=True)
    hit = jnp.sum(mine.astype(jnp.float32), axis=1, keepdims=True)
    shift = tok_dev.bit_length() - 1
    at = lax.broadcasted_iota(jnp.int32, (rows, rows), 0)
    before = lax.broadcasted_iota(jnp.int32, (rows, rows), 1)
    earlier = ((at >> shift) == (before >> shift)) & (before < at)
    hits = jnp.broadcast_to(hit, (rows, slots))
    rank = jnp.dot(
        earlier.astype(jnp.float32).astype(jnp.bfloat16),
        hits.astype(jnp.bfloat16),
        preferred_element_type=jnp.float32,
    ).astype(jnp.int32)
    row = lax.broadcasted_iota(jnp.int32, (rows, slots), 0)
    slot = (row >> shift) * capacity + rank
    group = unit // tok_dev * capacity
    away = ((row >> (unit.bit_length() - 1)) & 1) == 0
    slot_far = slot + jnp.where(away, group, -group)
    column = lax.broadcasted_iota(jnp.int32, (rows, slots), 1)
    pick_out[...] = jnp.where(slot == column, hits, 0.0).astype(jnp.bfloat16)
    pick_far_out[...] = jnp.where(slot_far == column, hits, 0.0).astype(jnp.bfloat16)
    coef_out[...] = jnp.broadcast_to(coef, coef_out.shape)


def finish_units(tokens, gate_w, up_w, gate_in, up_in, pick, act_out, packed_out, start):
    span = slice(start, start + act_out.shape[1])
    gate = gate_in[:, span] + times_rows_in(tokens[...], gate_w[span, :])
    upper = up_in[:, span] + times_rows_in(tokens[...], up_w[span, :])
    act = (gate / (1.0 + jnp.exp(-gate)) * upper).astype(jnp.bfloat16)
    act_out[...] = act
    packed_out[...] = lax.dot_general(
        pick[...], act, (((0,), (0,)), ((), ())), preferred_element_type=jnp.float32
    ).astype(jnp.bfloat16)


def second_kernel(
    two, far, two_other, far_other, gate_w, up_w, gate_in, up_in, pick,
    act_out, packed_out, tokens, *, unit,
):
    assemble(tokens, two, far, two_other, far_other, unit, True)
    finish_units(tokens, gate_w, up_w, gate_in, up_in, pick, act_out, packed_out, 0)


def third_kernel(tokens, gate_w, up_w, gate_in, up_in, pick, act_out, packed_out, *, start):
    finish_units(tokens, gate_w, up_w, gate_in, up_in, pick, act_out, packed_out, start)


def own_kernel(act_a, act_b, down_own, down_w, out, down_other, sems):
    units = down_own.shape[1]
    few = act_a.shape[1]
    other_at = pl.multiple_of((1 - lax.axis_index("ctx")) * units, 128)
    copies = start_copies([(down_w.at[:, pl.ds(other_at, units)], down_other)], sems, PIECES)
    tall = out.shape[1] // 5 if out.shape[1] % 640 == 0 else out.shape[1]
    for n in range(0, out.shape[1], tall):
        span = slice(n, n + tall)
        out[:, span] = times_rows_in(act_a[...], down_own[span, :few]) + times_rows_in(
            act_b[...], down_own[span, few:]
        )
    for copy in copies:
        copy.wait()


def other_kernel(packed_a, packed_b, pick, coef, down_w, own, keep, give, act, *, start):
    few = packed_a.shape[1]
    for packed, span in ((packed_a, slice(0, few)), (packed_b, slice(few, act.shape[1]))):
        act[:, span] = jnp.dot(
            pick[...], packed[...], preferred_element_type=jnp.float32
        ).astype(jnp.bfloat16)
    half, part = keep.shape
    tall = part // 5 if part % 5 == 0 else part
    for n in range(0, part, tall):
        span = slice(start + n, start + n + tall)
        projected = own[:, span] + times_rows_in(act[...], down_w[span, :])
        projected = projected * coef[:, :1]
        keep[:, n : n + tall] = projected[:half]
        give[:, n : n + tall] = projected[half:].astype(jnp.bfloat16)


def spread_kernel(keep, got, send, stay, *, y_first):
    unit = keep.shape[0] // 4
    stays, sends = ((0, 1), (2, 3)) if y_first else ((0, 2), (1, 3))
    for out, blocks in ((stay, stays), (send, sends)):
        for number, block in enumerate(blocks):
            span = slice(block * unit, (block + 1) * unit)
            total = keep[span, :] + got[span, :].astype(jnp.float32)
            out[number * unit : (number + 1) * unit, :] = total.astype(out.dtype)


def cross_kernel(stay, got, send, left, *, y_first):
    unit, part = send.shape[0], stay.shape[1]
    if y_first:
        left[...] = stay[:unit, :] + got[:unit, :].astype(jnp.float32)
        send[...] = (stay[unit:, :] + got[unit:, :].astype(jnp.float32)).astype(jnp.bfloat16)
    else:
        left[:, :part] = stay[:unit, :]
        left[:, part:] = got[:unit, :].astype(jnp.float32)
        send[:, :part] = stay[unit:, :].astype(jnp.bfloat16)
        send[:, part:] = got[unit:, :]


def line_kernel(left_x, got_y, left_y, got_x, *outs):
    ctx = lax.axis_index("ctx")
    count, part = outs[0].shape[0], left_y.shape[1]
    whole = left_x[...] + got_y[...].astype(jnp.float32)
    blocks = (
        (left_y[...], ctx, 0),
        (got_x[...].astype(jnp.float32), 1 - ctx, 0),
        (whole[:, :part], ctx, 1),
        (whole[:, part:], 1 - ctx, 1),
    )
    for value, side, number in blocks:
        at = pl.multiple_of(side * 2 * part + number * part, 128)
        for place, out in enumerate(outs):
            rows = value[place * count : (place + 1) * count]
            out[:, pl.ds(at, part)] = rows.astype(out.dtype)


def sum_kernel(first, *refs):
    total = first[...]
    for ref in refs[:-1]:
        total = total + ref[...].astype(jnp.float32)
    refs[-1][...] = total.astype(refs[-1].dtype)


def on_device_gathered(
    hidden, queries, latents, expert_ids, route_weight, w_gate, w_up, w_down
):
    tok_dev = hidden.shape[1]
    width = hidden.shape[2]
    topk = expert_ids.shape[2]
    units = w_gate.shape[1]
    columns = w_down.shape[1]
    tok_att, key_width = latents.shape
    heads_dev = queries.shape[1] // key_width
    experts = lax.axis_size("exp")
    line = experts // 4
    capacity = min(tok_dev, max(2, 3 * topk * tok_dev // (2 * experts)))
    half = width // 2
    unit = line * tok_dev
    count = 8 * unit
    slots = count // tok_dev * capacity
    bf16, f32 = jnp.bfloat16, jnp.float32

    rows, latents_half = local_kernel(
        lambda *refs: rows_kernel(*refs, half=half, topk=topk),
        [
            (hidden[0], "hbm"),
            (jnp.transpose(expert_ids, (2, 0, 1)), "hbm"),
            (jnp.transpose(route_weight, (2, 0, 1)), "hbm"),
            (latents.T, "hbm"),
        ],
        [((tok_dev, width + 128), bf16, "vmem"), ((key_width // 2, tok_att), bf16, "vmem")],
        [
            pltpu.VMEM((tok_dev, width), bf16),
            pltpu.VMEM((topk, 1, tok_dev), jnp.int32),
            pltpu.VMEM((topk, 1, tok_dev), f32),
            pltpu.SemaphoreType.DMA((4,)),
        ],
        "rows",
    )
    places = (3, 2, 1)
    along = [rows] + [along_line(rows, d) for d in places]
    earlier_kv = swapped(latents_half, "ctx", 1)
    gate_1, up_1, queries_here, latents_here = local_kernel(
        lambda *refs: fetch_kernel(*refs, start=0),
        [
            (rows, "vmem"), (w_gate[0], "hbm"), (w_up[0], "hbm"),
            (queries, "hbm"), (latents.T, "hbm"),
        ],
        [((units, half), bf16, "vmem")] * 2
        + [(queries.shape, bf16, "vmem"), ((key_width, tok_att), bf16, "vmem")],
        [pltpu.SemaphoreType.DMA((4 * PIECES,))],
        "fetch",
    )
    *along, earlier_kv, gate_1, up_1 = lax.optimization_barrier((*along, earlier_kv, gate_1, up_1))
    cuts = ((0, half + 128), (half + 128, width + 128))
    nears = local_kernel(
        lambda *refs: stack_kernel(*refs, cuts=cuts),
        [(row, "vmem") for row in along],
        [((unit, high - low), bf16, "vmem") for low, high in cuts],
        [],
        "stack_line",
    )
    pieces = []
    for near, first, then in zip(nears, (over_x, over_y), (over_y, over_x)):
        got = paired(near, first)
        (two,) = local_kernel(
            lambda *refs, cut=near.shape[1]: stack_kernel(*refs, cuts=((0, cut),)),
            [(near, "vmem"), (got, "vmem")],
            [((2 * unit, near.shape[1]), bf16, "vmem")],
            [],
            "stack_two",
        )
        pieces.append([two, paired(two, then)])
    gate_2, up_2, down_mine = local_kernel(
        lambda *refs: fetch_kernel(*refs, start=half),
        [(pieces[1][0], "vmem"), (w_gate[0], "hbm"), (w_up[0], "hbm"), (w_down[0], "hbm")],
        [((units, half), bf16, "vmem")] * 2 + [((columns, units), bf16, "vmem")],
        [pltpu.SemaphoreType.DMA((3 * PIECES,))],
        "fetch",
    )
    earlier_other = swapped(earlier_kv, "exp", 1)
    pieces[0][1], gate_2, up_2, down_mine, earlier_other = lax.optimization_barrier(
        (pieces[0][1], gate_2, up_2, down_mine, earlier_other)
    )
    for number, (two, far) in enumerate(pieces):
        group = (two, far, swapped(two, "exp", 1), swapped(far, "exp", 1))
        pieces[number] = [(piece, "vmem") for piece in group]

    gate, up, pick, pick_far, coef = local_kernel(
        lambda *refs: first_kernel(
            *refs, unit=unit, tok_dev=tok_dev, capacity=capacity, topk=topk
        ),
        [*pieces[0], (gate_1, "vmem"), (up_1, "vmem")],
        [((count, units), f32, "vmem")] * 2
        + [((count, slots), bf16, "vmem")] * 2
        + [((count, 128), f32, "vmem")],
        [pltpu.VMEM((count, half), bf16), pltpu.VMEM((count, 128), bf16)],
        "gate_up_first",
    )
    few = 2 * units // 3 if units % 384 == 0 else units // 2
    sums_in = [(gate_2, "vmem"), (up_2, "vmem"), (gate, "vmem"), (up, "vmem"), (pick, "vmem")]
    act_a, packed_a, tokens = local_kernel(
        lambda *refs: second_kernel(*refs, unit=unit),
        [*pieces[1], *sums_in],
        [
            ((count, few), bf16, "vmem"),
            ((slots, few), bf16, "vmem"),
            ((count, half), bf16, "vmem"),
        ],
        [],
        "gate_up_second",
    )
    other_a = swapped(packed_a, "ctx", 1)
    act_b, packed_b = local_kernel(
        lambda *refs: third_kernel(*refs, start=few),
        [(tokens, "vmem"), *sums_in],
        [((count, units - few), bf16, "vmem"), ((slots, units - few), bf16, "vmem")],
        [],
        "gate_up_third",
    )
    other_b = swapped(packed_b, "ctx", 1)
    own, down_other = local_kernel(
        own_kernel,
        [(act_a, "vmem"), (act_b, "vmem"), (down_mine, "vmem"), (w_down[0], "hbm")],
        [((count, columns), f32, "vmem"), ((columns, units), bf16, "vmem")],
        [pltpu.SemaphoreType.DMA((PIECES,))],
        "down_own",
    )
    part = columns // 2
    crossing = []
    for start, y_first in ((part, False), (0, True)):
        keep, give = local_kernel(
            lambda *refs, start=start: other_kernel(*refs, start=start),
            [
                (other_a, "vmem"), (other_b, "vmem"), (pick_far, "vmem"), (coef, "vmem"),
                (down_other, "vmem"), (own, "vmem"),
            ],
            [((count // 2, part), f32, "vmem"), ((count // 2, part), bf16, "vmem")],
            [pltpu.VMEM((count, units), bf16)],
            "down_other",
        )
        send, stay = local_kernel(
            lambda *refs, y_first=y_first: spread_kernel(*refs, y_first=y_first),
            [(keep, "vmem"), (swapped(give, "exp", 1), "vmem")],
            [((2 * unit, part), bf16, "vmem"), ((2 * unit, part), f32, "vmem")],
            [],
            "spread",
        )
        crossing.append((y_first, stay, paired(send, over_y if y_first else over_x)))
    lines = []
    for y_first, stay, got in crossing:
        wide = part if y_first else 2 * part
        send, left = local_kernel(
            lambda *refs, y_first=y_first: cross_kernel(*refs, y_first=y_first),
            [(stay, "vmem"), (got, "vmem")],
            [((unit, wide), bf16, "vmem"), ((unit, wide), f32, "vmem")],
            [],
            "cross",
        )
        lines += [left, paired(send, over_x if y_first else over_y)]
    keep, *sends = local_kernel(
        line_kernel,
        [(block, "vmem") for block in lines],
        [((tok_dev, 2 * columns), f32, "vmem")]
        + [((tok_dev, 2 * columns), bf16, "vmem")] * (line - 1),
        [],
        "line",
    )
    pad = -key_width % 128
    (attended,) = local_kernel(
        attention_kernel,
        [(sends[0], "vmem"), (earlier_kv, "vmem"), (earlier_other, "vmem"), (queries_here, "vmem"), (latents_here, "vmem")],
        [((tok_att, heads_dev * LATENT), bf16, "hbm")],
        [
            pltpu.VMEM((key_width + pad, 2 * tok_att), bf16),
            pltpu.VMEM((key_width + pad, 2 * tok_att), bf16),
            pltpu.VMEM((tok_att, heads_dev * LATENT), bf16),
            pltpu.SemaphoreType.DMA((heads_dev,)),
        ],
        "attention",
    )
    sends = dict(zip(places, sends))
    got = [along_line(sends[d], d) for d in (3, 1, 2)]
    got[-1], attended = lax.optimization_barrier((got[-1], attended))
    (mixed,) = local_kernel(
        sum_kernel,
        [(block, "vmem") for block in (keep, *got)],
        [((tok_dev, 2 * columns), bf16, "result")],
        [],
        "sum",
    )
    return (attended, mixed[None])


def on_device_slots(hidden, queries, latents, expert_ids, route_weight, w_gate, w_up, w_down):
    tok_att = latents.shape[0]
    heads_dev = queries.shape[1] // (LATENT + ROPE)
    tok_dev = hidden.shape[1]
    width = hidden.shape[2]
    topk = expert_ids.shape[2]
    experts = lax.axis_size("exp")
    groups = lax.axis_size("ctx")
    capacity = min(tok_dev, max(2, 3 * topk * tok_dev // (2 * experts)))
    slots = experts * capacity
    earlier_kv = shifted(latents, "ctx", 1)
    keys = jnp.concatenate([earlier_kv, latents], axis=0)
    query_rows = queries.reshape(tok_att, heads_dev, LATENT + ROPE)
    scores = jnp.einsum("thc,kc->htk", query_rows, keys, preferred_element_type=jnp.float32) * SCALE
    row_pos = jnp.arange(tok_att, dtype=jnp.int32)
    key_pos = jnp.arange(2 * tok_att, dtype=jnp.int32)
    seen_own = (key_pos[None, :] >= tok_att) & (key_pos[None, :] - tok_att <= row_pos[:, None])
    seen_prev = (key_pos[None, :] < tok_att) & (lax.axis_index("ctx") > 0)
    scores = jnp.where((seen_own | seen_prev)[None, :, :], scores, jnp.float32(-1e30))
    top = jnp.max(scores, axis=-1, keepdims=True)
    expo = jnp.exp(scores - top)
    probs = (expo / jnp.sum(expo, axis=-1, keepdims=True)).astype(jnp.bfloat16)
    mixed_heads = jnp.einsum(
        "htk,kc->thc", probs, keys[:, :LATENT], preferred_element_type=jnp.float32
    )
    attended = mixed_heads.astype(jnp.bfloat16).reshape(tok_att, heads_dev * LATENT)
    tokens = hidden[0]
    picks = expert_ids[0]
    pick_weight = route_weight[0].reshape(-1)
    tok_hot = token_table(tok_dev, topk)
    slot_hot = place_picks(picks, experts, capacity)
    gate_w = w_gate[0]
    up_w = w_up[0]
    down_w = w_down[0]
    send_matrix = jnp.dot(slot_hot.T, tok_hot).astype(jnp.bfloat16)
    outgoing = jnp.dot(send_matrix, tokens, preferred_element_type=jnp.float32).astype(jnp.bfloat16)
    outgoing = outgoing.reshape(experts, capacity, width)
    arrived = lax.all_to_all(outgoing, "exp", split_axis=0, concat_axis=0, tiled=True)
    piece = lax.all_gather(arrived.reshape(slots, width), "ctx", axis=0, tiled=True)
    gate = times_rows(piece, gate_w)
    upper = times_rows(piece, up_w)
    hidden_units = (jax.nn.silu(gate) * upper).astype(jnp.bfloat16)
    projected = times_rows(lax.all_gather(hidden_units, "ctx", axis=1, tiled=True), down_w)
    columns = projected.astype(jnp.bfloat16).reshape(groups, experts, capacity, down_w.shape[0])
    by_block = lax.all_to_all(columns, "ctx", split_axis=0, concat_axis=3, tiled=True)
    returned = lax.all_to_all(by_block, "exp", split_axis=1, concat_axis=1, tiled=True)
    combine_matrix = jnp.dot(
        slot_hot.T, tok_hot * pick_weight[:, None], precision=lax.Precision.HIGHEST
    )
    back_rows = returned.reshape(slots, width).astype(jnp.float32)
    mixed = jnp.dot(combine_matrix.T, back_rows, precision=lax.Precision.HIGHEST).astype(
        jnp.bfloat16
    )
    return (attended, mixed[None])


def solution(mesh):
    experts, groups = mesh.shape["exp"], mesh.shape["ctx"]
    whole = groups == 2 and experts == 16
    on_device = on_device_gathered if whole else on_device_slots
    placed = (
        P("exp", "ctx", None),
        P("ctx", "exp"),
        P("ctx", None),
        P("exp", "ctx", None),
        P("exp", "ctx", None),
        P("exp", "ctx", None),
        P("exp", "ctx", None),
        P("exp", "ctx", None),
    )
    return jax.shard_map(
        on_device,
        mesh=mesh,
        in_specs=placed,
        out_specs=(P("ctx", "exp"), P("exp", "ctx", None)),
        check_vma=False,
    )
```

```python
import jax
import jax.numpy as jnp
from jax import lax
from jax.experimental import pallas as pl
from jax.experimental.pallas import tpu as pltpu
from jax.sharding import PartitionSpec as P

LATENT = 512
ROPE = 64


SCALE = 0.07216878364870322


def shifted(block, axis, distance):
    devices = range(lax.axis_size(axis))
    route = [(i - distance, i) for i in devices if i - distance in devices]
    return lax.ppermute(block, axis, route)


def place_picks(picks, experts, capacity):
    flat = picks.reshape(-1)
    onehot = (flat[:, None] == jnp.arange(experts, dtype=jnp.int32)[None, :]).astype(jnp.int32)
    earlier = jnp.cumsum(onehot, axis=0) - onehot
    rank = jnp.sum(earlier * onehot, axis=1)
    target = flat * capacity + rank
    return (target[:, None] == jnp.arange(experts * capacity, dtype=jnp.int32)[None, :]).astype(
        jnp.float32
    )


def token_table(tok_count, topk):
    owner = jnp.arange(tok_count * topk, dtype=jnp.int32) // topk
    return (owner[:, None] == jnp.arange(tok_count, dtype=jnp.int32)[None, :]).astype(jnp.float32)


def times_rows(left, right):
    return lax.dot_general(
        left, right, (((1,), (1,)), ((), ())), preferred_element_type=jnp.float32
    )


def swapped(block, axis, bit):
    return lax.ppermute(block, axis, [(i, i ^ bit) for i in range(lax.axis_size(axis))])


def along_line(block, steps):
    return lax.ppermute(
        block, "exp", [(i, i ^ (4 * steps)) for i in range(lax.axis_size("exp"))]
    )


def paired(block, partner):
    count = lax.axis_size("exp")
    both = lax.axis_size("ctx") * count
    route = []
    for i in range(both):
        ctx, exp = partner(i // count, i % count)
        route.append((i, ctx * count + exp))
    return lax.ppermute(block, ("ctx", "exp"), route)


def over_y(ctx, exp):
    return ctx, exp ^ 2


def over_x(ctx, exp):
    return 1 - ctx, exp


def times_rows_in(left, right):
    return lax.dot_general(
        left, right, (((1,), (1,)), ((), ())), preferred_element_type=jnp.float32
    )


def in_vmem(array):
    return pltpu.with_memory_space_constraint(array, pltpu.VMEM)


def in_hbm(array):
    return pltpu.with_memory_space_constraint(array, pltpu.HBM)


def local_kernel(body, ins, outs, scratch, name):
    kinds = {"vmem": pltpu.VMEM, "hbm": pl.ANY, "result": pltpu.VMEM}
    place = {"vmem": in_vmem, "hbm": in_hbm}
    made = [
        pltpu.VMEM(shape, dtype) if kind == "vmem" else jax.ShapeDtypeStruct(shape, dtype)
        for shape, dtype, kind in outs
    ]
    return pl.pallas_call(
        body,
        in_specs=[pl.BlockSpec(memory_space=kinds[kind]) for _, kind in ins],
        out_specs=[pl.BlockSpec(memory_space=kinds[kind]) for _, _, kind in outs],
        out_shape=made,
        scratch_shapes=scratch,
        compiler_params=pltpu.CompilerParams(vmem_limit_bytes=20 * 1024 * 1024),
        cost_estimate=pl.CostEstimate(flops=0, bytes_accessed=0, transcendentals=0),
        name=name,
    )(*[place[kind](array) for array, kind in ins])


def start_copies(pairs, sems, pieces):
    copies = []
    for number, (source, target) in enumerate(pairs):
        step = target.shape[0] // pieces
        for piece in range(pieces):
            span = pl.ds(piece * step, step)
            copy = pltpu.make_async_copy(
                source.at[span, :], target.at[span, :], sems.at[number * pieces + piece]
            )
            copy.start()
            copies.append(copy)
    return copies


PIECES = 4


def rows_kernel(
    tokens_in, names_in, weights_in, latents_in, out, latents, tokens, names, weights, sems, *, half, topk
):
    share = latents.shape[0]
    at = pl.multiple_of(lax.axis_index("exp") % 2 * share, 16)
    copies = [
        pltpu.make_async_copy(source, target, sems.at[number])
        for number, (source, target) in enumerate(
            (
                (names_in, names),
                (weights_in, weights),
                (tokens_in, tokens),
                (latents_in.at[pl.ds(at, share), :], latents),
            )
        )
    ]
    for copy in copies:
        copy.start()
    count = tokens.shape[0]
    width = tokens.shape[1]
    lane = lax.broadcasted_iota(jnp.int32, (count, 128), 1)
    same = lax.broadcasted_iota(jnp.int32, (count, count), 0) == lax.broadcasted_iota(
        jnp.int32, (count, count), 1
    )

    def column(row):
        return jnp.sum(
            jnp.where(same, jnp.broadcast_to(row, same.shape), 0.0), axis=1, keepdims=True
        )

    for copy in copies[:2]:
        copy.wait()
    note = jnp.zeros((count, 128), jnp.float32)
    for k in range(topk):
        name = column(names[k].astype(jnp.float32))
        weight = column(weights[k])
        low = weight - weight.astype(jnp.bfloat16).astype(jnp.float32)
        for value, at in ((name, k), (weight, topk + k), (low, 2 * topk + k)):
            note = jnp.where(lane == at, value, note)
    out[:, half : half + 128] = note.astype(jnp.bfloat16)
    for copy in copies[2:]:
        copy.wait()
    out[:, :half] = tokens[:, :half]
    out[:, half + 128 :] = tokens[:, half:width]


def fetch_kernel(after, *refs, start):
    count = len(refs) // 2
    ins, outs, sems = refs[:count], refs[count:-1], refs[-1]
    pairs = [(a.at[:, start : start + b.shape[1]], b) for a, b in zip(ins[:2], outs[:2])]
    for source, target in zip(ins[2:], outs[2:]):
        width = target.shape[1]
        if source.shape[1] != width:
            own_at = pl.multiple_of(lax.axis_index("ctx") * width, 128)
            source = source.at[:, pl.ds(own_at, width)]
        pairs.append((source, target))
    for copy in start_copies(pairs, sems, PIECES):
        copy.wait()


def fetch_other_kernel(after, source, target, sems):
    width = target.shape[1]
    at = pl.multiple_of((1 - lax.axis_index("ctx")) * width, 128)
    for copy in start_copies([(source.at[:, pl.ds(at, width)], target)], sems, PIECES):
        copy.wait()


def stack_kernel(*refs, cuts):
    ins, outs = refs[: len(refs) - len(cuts)], refs[len(refs) - len(cuts) :]
    for out, (low, high) in zip(outs, cuts):
        if ins[0].shape[0] % 16 == 0:
            at = 0
            for ref in ins:
                out[at : at + ref.shape[0], :] = ref[:, low:high]
                at += ref.shape[0]
        else:
            rows = [ref[:, low:high].astype(jnp.float32) for ref in ins]
            out[...] = jnp.concatenate(rows, axis=0).astype(out.dtype)


def attention_kernel(
    after, earlier, earlier_other, queries, latents, attended, even, odd, mixed, sems
):
    width, rows = latents.shape
    pad = even.shape[0] - width
    even[width:, :] = jnp.zeros((pad, 2 * rows), jnp.bfloat16)
    odd[:pad, :] = jnp.zeros((pad, 2 * rows), jnp.bfloat16)
    share = width // 2
    core = lax.axis_index("exp") % 2
    for side, ref in ((core, earlier), (1 - core, earlier_other)):
        even[pl.ds(pl.multiple_of(side * share, 16), share), :rows] = ref[...]
        odd[pl.ds(pl.multiple_of(side * share + pad, 16), share), :rows] = ref[...]
    even[:width, rows:] = latents[...]
    odd[pad:, rows:] = latents[...]
    row = lax.broadcasted_iota(jnp.int32, (rows, 2 * rows), 0)
    key = lax.broadcasted_iota(jnp.int32, (rows, 2 * rows), 1)
    nearest = jnp.where(lax.axis_index("ctx") > 0, 0, rows)
    seen = (key >= nearest) & (key <= row + rows)
    heads = attended.shape[1] // LATENT
    writes = []
    for head in range(heads):
        start = head * width
        keys, start = (even, start) if start % 128 == 0 else (odd, start - pad)
        scores = jnp.dot(
            queries[:, start : start + width + pad], keys[...], preferred_element_type=jnp.float32
        )
        scores = jnp.where(seen, scores * SCALE, jnp.float32(-1e30))
        expo = jnp.exp(scores - jnp.max(scores, axis=-1, keepdims=True))
        probs = (expo / jnp.sum(expo, axis=-1, keepdims=True)).astype(jnp.bfloat16)
        span = slice(head * LATENT, (head + 1) * LATENT)
        mixed[:, span] = times_rows_in(probs, even[:LATENT, :]).astype(jnp.bfloat16)
        write = pltpu.make_async_copy(mixed.at[:, span], attended.at[:, span], sems.at[head])
        write.start()
        writes.append(write)
    for copy in writes:
        copy.wait()


def assemble(place, two_ref, far_ref, two_other_ref, far_other_ref, unit, y_first, start=0):
    span = slice(start, start + place.shape[1])
    order = (0, 2, 1, 3) if y_first else (0, 1, 2, 3)
    for lane, two, far in ((0, two_ref, far_ref), (1, two_other_ref, far_other_ref)):
        for number, block in enumerate(order):
            ref = (two, far)[number // 2]
            rows = slice(number % 2 * unit, (number % 2 + 1) * unit)
            base = (lane * 4 + block) * unit
            place[base : base + unit, :] = ref[rows, span]


def first_kernel(
    two, far, two_other, far_other, gate_w, up_w,
    gate_out, up_out, pick_out, pick_far_out, coef_out,
    tokens, notes, *, unit, tok_dev, capacity, topk,
):
    width = tokens.shape[1]
    rows = tokens.shape[0]
    slots = pick_out.shape[1]
    expert = lax.axis_index("exp")
    assemble(tokens, two, far, two_other, far_other, unit, False)
    gate_out[...] = times_rows_in(tokens[...], gate_w[...])
    up_out[...] = times_rows_in(tokens[...], up_w[...])

    assemble(notes, two, far, two_other, far_other, unit, False, width)
    note = notes[...].astype(jnp.float32)
    lane = lax.broadcasted_iota(jnp.int32, note.shape, 1)
    mine = (note == expert.astype(jnp.float32)) & (lane < topk)
    weight = pltpu.roll(note, 128 - topk, 1) + pltpu.roll(note, 128 - 2 * topk, 1)
    coef = jnp.sum(jnp.where(mine, weight, 0.0), axis=1, keepdims=True)
    hit = jnp.sum(mine.astype(jnp.float32), axis=1, keepdims=True)
    shift = tok_dev.bit_length() - 1
    at = lax.broadcasted_iota(jnp.int32, (rows, rows), 0)
    before = lax.broadcasted_iota(jnp.int32, (rows, rows), 1)
    earlier = ((at >> shift) == (before >> shift)) & (before < at)
    hits = jnp.broadcast_to(hit, (rows, slots))
    rank = jnp.dot(
        earlier.astype(jnp.float32).astype(jnp.bfloat16),
        hits.astype(jnp.bfloat16),
        preferred_element_type=jnp.float32,
    ).astype(jnp.int32)
    row = lax.broadcasted_iota(jnp.int32, (rows, slots), 0)
    slot = (row >> shift) * capacity + rank
    group = unit // tok_dev * capacity
    away = ((row >> (unit.bit_length() - 1)) & 1) == 0
    slot_far = slot + jnp.where(away, group, -group)
    column = lax.broadcasted_iota(jnp.int32, (rows, slots), 1)
    pick_out[...] = jnp.where(slot == column, hits, 0.0).astype(jnp.bfloat16)
    pick_far_out[...] = jnp.where(slot_far == column, hits, 0.0).astype(jnp.bfloat16)
    coef_out[...] = jnp.broadcast_to(coef, coef_out.shape)


def finish_units(tokens, gate_w, up_w, gate_in, up_in, pick, act_out, packed_out, start):
    span = slice(start, start + act_out.shape[1])
    gate = gate_in[:, span] + times_rows_in(tokens[...], gate_w[span, :])
    upper = up_in[:, span] + times_rows_in(tokens[...], up_w[span, :])
    act = (gate / (1.0 + jnp.exp(-gate)) * upper).astype(jnp.bfloat16)
    act_out[...] = act
    packed_out[...] = lax.dot_general(
        pick[...], act, (((0,), (0,)), ((), ())), preferred_element_type=jnp.float32
    ).astype(jnp.bfloat16)


def second_kernel(
    two, far, two_other, far_other, gate_w, up_w, gate_in, up_in, pick,
    act_out, packed_out, tokens, *, unit,
):
    assemble(tokens, two, far, two_other, far_other, unit, True)
    finish_units(tokens, gate_w, up_w, gate_in, up_in, pick, act_out, packed_out, 0)


def third_kernel(tokens, gate_w, up_w, gate_in, up_in, pick, act_out, packed_out, *, start):
    finish_units(tokens, gate_w, up_w, gate_in, up_in, pick, act_out, packed_out, start)


def own_kernel(act_a, act_b, down_own, out):
    few = act_a.shape[1]
    tall = 512 if out.shape[1] % 512 == 0 else out.shape[1]
    for n in range(0, out.shape[1], tall):
        span = slice(n, n + tall)
        out[:, span] = times_rows_in(act_a[...], down_own[span, :few]) + times_rows_in(
            act_b[...], down_own[span, few:]
        )


def more_kernel(packed, pick, down_w, own, out, act):
    few = act.shape[1]
    act[...] = jnp.dot(pick[...], packed[...], preferred_element_type=jnp.float32).astype(
        jnp.bfloat16
    )
    tall = 512 if out.shape[1] % 512 == 0 else out.shape[1]
    for n in range(0, out.shape[1], tall):
        span = slice(n, n + tall)
        out[:, span] = own[:, span] + times_rows_in(act[...], down_w[span, :few])


def other_kernel(packed, pick, coef, down_w, own, keep, give, act, *, start):
    act[...] = jnp.dot(pick[...], packed[...], preferred_element_type=jnp.float32).astype(
        jnp.bfloat16
    )
    few = down_w.shape[1] - act.shape[1]
    half, part = keep.shape
    tall = part // 5 if part % 5 == 0 else part
    for n in range(0, part, tall):
        span = slice(start + n, start + n + tall)
        projected = own[:, span] + times_rows_in(act[...], down_w[span, few:])
        projected = projected * coef[:, :1]
        keep[:, n : n + tall] = projected[:half]
        give[:, n : n + tall] = projected[half:].astype(jnp.bfloat16)


def spread_kernel(keep, got, send, stay, *, y_first):
    unit = keep.shape[0] // 4
    stays, sends = ((0, 1), (2, 3)) if y_first else ((0, 2), (1, 3))
    for out, blocks in ((stay, stays), (send, sends)):
        for number, block in enumerate(blocks):
            span = slice(block * unit, (block + 1) * unit)
            total = keep[span, :] + got[span, :].astype(jnp.float32)
            out[number * unit : (number + 1) * unit, :] = total.astype(out.dtype)


def cross_kernel(stay, got, send, left, *, y_first):
    unit, part = send.shape[0], stay.shape[1]
    if y_first:
        left[...] = stay[:unit, :] + got[:unit, :].astype(jnp.float32)
        send[...] = (stay[unit:, :] + got[unit:, :].astype(jnp.float32)).astype(jnp.bfloat16)
    else:
        left[:, :part] = stay[:unit, :]
        left[:, part:] = got[:unit, :].astype(jnp.float32)
        send[:, :part] = stay[unit:, :].astype(jnp.bfloat16)
        send[:, part:] = got[unit:, :]


def line_kernel(left_x, got_y, left_y, got_x, *outs):
    ctx = lax.axis_index("ctx")
    count, part = outs[0].shape[0], left_y.shape[1]
    whole = left_x[...] + got_y[...].astype(jnp.float32)
    blocks = (
        (left_y[...], ctx, 0),
        (got_x[...].astype(jnp.float32), 1 - ctx, 0),
        (whole[:, :part], ctx, 1),
        (whole[:, part:], 1 - ctx, 1),
    )
    for value, side, number in blocks:
        at = pl.multiple_of(side * 2 * part + number * part, 128)
        for place, out in enumerate(outs):
            rows = value[place * count : (place + 1) * count]
            out[:, pl.ds(at, part)] = rows.astype(out.dtype)


def sum_kernel(first, *refs):
    total = first[...]
    for ref in refs[:-1]:
        total = total + ref[...].astype(jnp.float32)
    refs[-1][...] = total.astype(refs[-1].dtype)


def on_device_gathered(
    hidden, queries, latents, expert_ids, route_weight, w_gate, w_up, w_down
):
    tok_dev = hidden.shape[1]
    width = hidden.shape[2]
    topk = expert_ids.shape[2]
    units = w_gate.shape[1]
    columns = w_down.shape[1]
    tok_att, key_width = latents.shape
    heads_dev = queries.shape[1] // key_width
    experts = lax.axis_size("exp")
    line = experts // 4
    capacity = min(tok_dev, max(2, 3 * topk * tok_dev // (2 * experts)))
    half = width // 2
    unit = line * tok_dev
    count = 8 * unit
    slots = count // tok_dev * capacity
    bf16, f32 = jnp.bfloat16, jnp.float32

    rows, latents_half = local_kernel(
        lambda *refs: rows_kernel(*refs, half=half, topk=topk),
        [
            (hidden[0], "hbm"),
            (jnp.transpose(expert_ids, (2, 0, 1)), "hbm"),
            (jnp.transpose(route_weight, (2, 0, 1)), "hbm"),
            (latents.T, "hbm"),
        ],
        [((tok_dev, width + 128), bf16, "vmem"), ((key_width // 2, tok_att), bf16, "vmem")],
        [
            pltpu.VMEM((tok_dev, width), bf16),
            pltpu.VMEM((topk, 1, tok_dev), jnp.int32),
            pltpu.VMEM((topk, 1, tok_dev), f32),
            pltpu.SemaphoreType.DMA((4,)),
        ],
        "rows",
    )
    places = (3, 2, 1)
    along = [rows] + [along_line(rows, d) for d in places]
    earlier_kv = swapped(latents_half, "ctx", 1)
    gate_1, up_1, queries_here, latents_here = local_kernel(
        lambda *refs: fetch_kernel(*refs, start=0),
        [
            (rows, "vmem"), (w_gate[0], "hbm"), (w_up[0], "hbm"),
            (queries, "hbm"), (latents.T, "hbm"),
        ],
        [((units, half), bf16, "vmem")] * 2
        + [(queries.shape, bf16, "vmem"), ((key_width, tok_att), bf16, "vmem")],
        [pltpu.SemaphoreType.DMA((4 * PIECES,))],
        "fetch",
    )
    *along, earlier_kv, gate_1, up_1 = lax.optimization_barrier((*along, earlier_kv, gate_1, up_1))
    cuts = ((0, half + 128), (half + 128, width + 128))
    nears = local_kernel(
        lambda *refs: stack_kernel(*refs, cuts=cuts),
        [(row, "vmem") for row in along],
        [((unit, high - low), bf16, "vmem") for low, high in cuts],
        [],
        "stack_line",
    )
    (down_other,) = local_kernel(
        fetch_other_kernel,
        [(nears[1], "vmem"), (w_down[0], "hbm")],
        [((columns, units), bf16, "vmem")],
        [pltpu.SemaphoreType.DMA((PIECES,))],
        "fetch",
    )
    pieces = []
    for near, first, then in zip(nears, (over_x, over_y), (over_y, over_x)):
        got = paired(near, first)
        if first is over_x:
            got, down_other = lax.optimization_barrier((got, down_other))
        (two,) = local_kernel(
            lambda *refs, cut=near.shape[1]: stack_kernel(*refs, cuts=((0, cut),)),
            [(near, "vmem"), (got, "vmem")],
            [((2 * unit, near.shape[1]), bf16, "vmem")],
            [],
            "stack_two",
        )
        pieces.append([two, paired(two, then)])
    gate_2, up_2, down_mine = local_kernel(
        lambda *refs: fetch_kernel(*refs, start=half),
        [(pieces[1][0], "vmem"), (w_gate[0], "hbm"), (w_up[0], "hbm"), (w_down[0], "hbm")],
        [((units, half), bf16, "vmem")] * 2 + [((columns, units), bf16, "vmem")],
        [pltpu.SemaphoreType.DMA((3 * PIECES,))],
        "fetch",
    )
    earlier_other = swapped(earlier_kv, "exp", 1)
    pieces[0][1], gate_2, up_2, down_mine, earlier_other = lax.optimization_barrier(
        (pieces[0][1], gate_2, up_2, down_mine, earlier_other)
    )
    for number, (two, far) in enumerate(pieces):
        group = (two, far, swapped(two, "exp", 1), swapped(far, "exp", 1))
        pieces[number] = [(piece, "vmem") for piece in group]

    gate, up, pick, pick_far, coef = local_kernel(
        lambda *refs: first_kernel(
            *refs, unit=unit, tok_dev=tok_dev, capacity=capacity, topk=topk
        ),
        [*pieces[0], (gate_1, "vmem"), (up_1, "vmem")],
        [((count, units), f32, "vmem")] * 2
        + [((count, slots), bf16, "vmem")] * 2
        + [((count, 128), f32, "vmem")],
        [pltpu.VMEM((count, half), bf16), pltpu.VMEM((count, 128), bf16)],
        "gate_up_first",
    )
    few = 2 * units // 3 if units % 384 == 0 else units // 2
    sums_in = [(gate_2, "vmem"), (up_2, "vmem"), (gate, "vmem"), (up, "vmem"), (pick, "vmem")]
    act_a, packed_a, tokens = local_kernel(
        lambda *refs: second_kernel(*refs, unit=unit),
        [*pieces[1], *sums_in],
        [
            ((count, few), bf16, "vmem"),
            ((slots, few), bf16, "vmem"),
            ((count, half), bf16, "vmem"),
        ],
        [],
        "gate_up_second",
    )
    other_a = swapped(packed_a, "ctx", 1)
    act_b, packed_b = local_kernel(
        lambda *refs: third_kernel(*refs, start=few),
        [(tokens, "vmem"), *sums_in],
        [((count, units - few), bf16, "vmem"), ((slots, units - few), bf16, "vmem")],
        [],
        "gate_up_third",
    )
    other_b = swapped(packed_b, "ctx", 1)
    (own,) = local_kernel(
        own_kernel,
        [(act_a, "vmem"), (act_b, "vmem"), (down_mine, "vmem")],
        [((count, columns), f32, "vmem")],
        [],
        "down_own",
    )
    (own,) = local_kernel(
        more_kernel,
        [(other_a, "vmem"), (pick_far, "vmem"), (down_other, "vmem"), (own, "vmem")],
        [((count, columns), f32, "vmem")],
        [pltpu.VMEM((count, few), bf16)],
        "down_more",
    )
    part = columns // 2
    crossing = []
    for start, y_first in ((part, False), (0, True)):
        keep, give = local_kernel(
            lambda *refs, start=start: other_kernel(*refs, start=start),
            [
                (other_b, "vmem"), (pick_far, "vmem"), (coef, "vmem"),
                (down_other, "vmem"), (own, "vmem"),
            ],
            [((count // 2, part), f32, "vmem"), ((count // 2, part), bf16, "vmem")],
            [pltpu.VMEM((count, units - few), bf16)],
            "down_other",
        )
        send, stay = local_kernel(
            lambda *refs, y_first=y_first: spread_kernel(*refs, y_first=y_first),
            [(keep, "vmem"), (swapped(give, "exp", 1), "vmem")],
            [((2 * unit, part), bf16, "vmem"), ((2 * unit, part), f32, "vmem")],
            [],
            "spread",
        )
        crossing.append((y_first, stay, paired(send, over_y if y_first else over_x)))
    lines = []
    for y_first, stay, got in crossing:
        wide = part if y_first else 2 * part
        send, left = local_kernel(
            lambda *refs, y_first=y_first: cross_kernel(*refs, y_first=y_first),
            [(stay, "vmem"), (got, "vmem")],
            [((unit, wide), bf16, "vmem"), ((unit, wide), f32, "vmem")],
            [],
            "cross",
        )
        lines += [left, paired(send, over_x if y_first else over_y)]
    keep, *sends = local_kernel(
        line_kernel,
        [(block, "vmem") for block in lines],
        [((tok_dev, 2 * columns), f32, "vmem")]
        + [((tok_dev, 2 * columns), bf16, "vmem")] * (line - 1),
        [],
        "line",
    )
    pad = -key_width % 128
    (attended,) = local_kernel(
        attention_kernel,
        [(sends[0], "vmem"), (earlier_kv, "vmem"), (earlier_other, "vmem"), (queries_here, "vmem"), (latents_here, "vmem")],
        [((tok_att, heads_dev * LATENT), bf16, "hbm")],
        [
            pltpu.VMEM((key_width + pad, 2 * tok_att), bf16),
            pltpu.VMEM((key_width + pad, 2 * tok_att), bf16),
            pltpu.VMEM((tok_att, heads_dev * LATENT), bf16),
            pltpu.SemaphoreType.DMA((heads_dev,)),
        ],
        "attention",
    )
    sends = dict(zip(places, sends))
    got = [along_line(sends[d], d) for d in (3, 1, 2)]
    got[-1], attended = lax.optimization_barrier((got[-1], attended))
    (mixed,) = local_kernel(
        sum_kernel,
        [(block, "vmem") for block in (keep, *got)],
        [((tok_dev, 2 * columns), bf16, "result")],
        [],
        "sum",
    )
    return (attended, mixed[None])


def on_device_slots(hidden, queries, latents, expert_ids, route_weight, w_gate, w_up, w_down):
    tok_att = latents.shape[0]
    heads_dev = queries.shape[1] // (LATENT + ROPE)
    tok_dev = hidden.shape[1]
    width = hidden.shape[2]
    topk = expert_ids.shape[2]
    experts = lax.axis_size("exp")
    groups = lax.axis_size("ctx")
    capacity = min(tok_dev, max(2, 3 * topk * tok_dev // (2 * experts)))
    slots = experts * capacity
    earlier_kv = shifted(latents, "ctx", 1)
    keys = jnp.concatenate([earlier_kv, latents], axis=0)
    query_rows = queries.reshape(tok_att, heads_dev, LATENT + ROPE)
    scores = jnp.einsum("thc,kc->htk", query_rows, keys, preferred_element_type=jnp.float32) * SCALE
    row_pos = jnp.arange(tok_att, dtype=jnp.int32)
    key_pos = jnp.arange(2 * tok_att, dtype=jnp.int32)
    seen_own = (key_pos[None, :] >= tok_att) & (key_pos[None, :] - tok_att <= row_pos[:, None])
    seen_prev = (key_pos[None, :] < tok_att) & (lax.axis_index("ctx") > 0)
    scores = jnp.where((seen_own | seen_prev)[None, :, :], scores, jnp.float32(-1e30))
    top = jnp.max(scores, axis=-1, keepdims=True)
    expo = jnp.exp(scores - top)
    probs = (expo / jnp.sum(expo, axis=-1, keepdims=True)).astype(jnp.bfloat16)
    mixed_heads = jnp.einsum(
        "htk,kc->thc", probs, keys[:, :LATENT], preferred_element_type=jnp.float32
    )
    attended = mixed_heads.astype(jnp.bfloat16).reshape(tok_att, heads_dev * LATENT)
    tokens = hidden[0]
    picks = expert_ids[0]
    pick_weight = route_weight[0].reshape(-1)
    tok_hot = token_table(tok_dev, topk)
    slot_hot = place_picks(picks, experts, capacity)
    gate_w = w_gate[0]
    up_w = w_up[0]
    down_w = w_down[0]
    send_matrix = jnp.dot(slot_hot.T, tok_hot).astype(jnp.bfloat16)
    outgoing = jnp.dot(send_matrix, tokens, preferred_element_type=jnp.float32).astype(jnp.bfloat16)
    outgoing = outgoing.reshape(experts, capacity, width)
    arrived = lax.all_to_all(outgoing, "exp", split_axis=0, concat_axis=0, tiled=True)
    piece = lax.all_gather(arrived.reshape(slots, width), "ctx", axis=0, tiled=True)
    gate = times_rows(piece, gate_w)
    upper = times_rows(piece, up_w)
    hidden_units = (jax.nn.silu(gate) * upper).astype(jnp.bfloat16)
    projected = times_rows(lax.all_gather(hidden_units, "ctx", axis=1, tiled=True), down_w)
    columns = projected.astype(jnp.bfloat16).reshape(groups, experts, capacity, down_w.shape[0])
    by_block = lax.all_to_all(columns, "ctx", split_axis=0, concat_axis=3, tiled=True)
    returned = lax.all_to_all(by_block, "exp", split_axis=1, concat_axis=1, tiled=True)
    combine_matrix = jnp.dot(
        slot_hot.T, tok_hot * pick_weight[:, None], precision=lax.Precision.HIGHEST
    )
    back_rows = returned.reshape(slots, width).astype(jnp.float32)
    mixed = jnp.dot(combine_matrix.T, back_rows, precision=lax.Precision.HIGHEST).astype(
        jnp.bfloat16
    )
    return (attended, mixed[None])


def solution(mesh):
    experts, groups = mesh.shape["exp"], mesh.shape["ctx"]
    whole = groups == 2 and experts == 16
    on_device = on_device_gathered if whole else on_device_slots
    placed = (
        P("exp", "ctx", None),
        P("ctx", "exp"),
        P("ctx", None),
        P("exp", "ctx", None),
        P("exp", "ctx", None),
        P("exp", "ctx", None),
        P("exp", "ctx", None),
        P("exp", "ctx", None),
    )
    return jax.shard_map(
        on_device,
        mesh=mesh,
        in_specs=placed,
        out_specs=(P("ctx", "exp"), P("exp", "ctx", None)),
        check_vma=False,
    )
```

```python
import jax
import jax.numpy as jnp
from jax import lax
from jax.experimental import pallas as pl
from jax.experimental.pallas import tpu as pltpu
from jax.sharding import PartitionSpec as P

LATENT = 512
ROPE = 64


SCALE = 0.07216878364870322


def shifted(block, axis, distance):
    devices = range(lax.axis_size(axis))
    route = [(i - distance, i) for i in devices if i - distance in devices]
    return lax.ppermute(block, axis, route)


def place_picks(picks, experts, capacity):
    flat = picks.reshape(-1)
    onehot = (flat[:, None] == jnp.arange(experts, dtype=jnp.int32)[None, :]).astype(jnp.int32)
    earlier = jnp.cumsum(onehot, axis=0) - onehot
    rank = jnp.sum(earlier * onehot, axis=1)
    target = flat * capacity + rank
    return (target[:, None] == jnp.arange(experts * capacity, dtype=jnp.int32)[None, :]).astype(
        jnp.float32
    )


def token_table(tok_count, topk):
    owner = jnp.arange(tok_count * topk, dtype=jnp.int32) // topk
    return (owner[:, None] == jnp.arange(tok_count, dtype=jnp.int32)[None, :]).astype(jnp.float32)


def times_rows(left, right):
    return lax.dot_general(
        left, right, (((1,), (1,)), ((), ())), preferred_element_type=jnp.float32
    )


def swapped(block, axis, bit):
    return lax.ppermute(block, axis, [(i, i ^ bit) for i in range(lax.axis_size(axis))])


def along_line(block, steps):
    return lax.ppermute(
        block, "exp", [(i, i ^ (4 * steps)) for i in range(lax.axis_size("exp"))]
    )


def paired(block, partner):
    count = lax.axis_size("exp")
    both = lax.axis_size("ctx") * count
    route = []
    for i in range(both):
        ctx, exp = partner(i // count, i % count)
        route.append((i, ctx * count + exp))
    return lax.ppermute(block, ("ctx", "exp"), route)


def over_y(ctx, exp):
    return ctx, exp ^ 2


def over_x(ctx, exp):
    return 1 - ctx, exp


def times_rows_in(left, right):
    return lax.dot_general(
        left, right, (((1,), (1,)), ((), ())), preferred_element_type=jnp.float32
    )


def in_vmem(array):
    return pltpu.with_memory_space_constraint(array, pltpu.VMEM)


def in_hbm(array):
    return pltpu.with_memory_space_constraint(array, pltpu.HBM)


def local_kernel(body, ins, outs, scratch, name):
    kinds = {"vmem": pltpu.VMEM, "hbm": pl.ANY, "result": pltpu.VMEM}
    place = {"vmem": in_vmem, "hbm": in_hbm}
    made = [
        pltpu.VMEM(shape, dtype) if kind == "vmem" else jax.ShapeDtypeStruct(shape, dtype)
        for shape, dtype, kind in outs
    ]
    return pl.pallas_call(
        body,
        in_specs=[pl.BlockSpec(memory_space=kinds[kind]) for _, kind in ins],
        out_specs=[pl.BlockSpec(memory_space=kinds[kind]) for _, _, kind in outs],
        out_shape=made,
        scratch_shapes=scratch,
        compiler_params=pltpu.CompilerParams(vmem_limit_bytes=20 * 1024 * 1024),
        cost_estimate=pl.CostEstimate(flops=0, bytes_accessed=0, transcendentals=0),
        name=name,
    )(*[place[kind](array) for array, kind in ins])


def start_copies(pairs, sems, pieces):
    copies = []
    for number, (source, target) in enumerate(pairs):
        step = target.shape[0] // pieces
        for piece in range(pieces):
            span = pl.ds(piece * step, step)
            copy = pltpu.make_async_copy(
                source.at[span, :], target.at[span, :], sems.at[number * pieces + piece]
            )
            copy.start()
            copies.append(copy)
    return copies


PIECES = 4


def rows_kernel(
    tokens_in, names_in, weights_in, latents_in, out, latents, tokens, names, weights, sems, *, half, topk
):
    share = latents.shape[0]
    at = pl.multiple_of(lax.axis_index("exp") % 2 * share, 16)
    copies = [
        pltpu.make_async_copy(source, target, sems.at[number])
        for number, (source, target) in enumerate(
            (
                (names_in, names),
                (weights_in, weights),
                (tokens_in, tokens),
                (latents_in.at[pl.ds(at, share), :], latents),
            )
        )
    ]
    for copy in copies:
        copy.start()
    count = tokens.shape[0]
    width = tokens.shape[1]
    lane = lax.broadcasted_iota(jnp.int32, (count, 128), 1)
    same = lax.broadcasted_iota(jnp.int32, (count, count), 0) == lax.broadcasted_iota(
        jnp.int32, (count, count), 1
    )

    def column(row):
        return jnp.sum(
            jnp.where(same, jnp.broadcast_to(row, same.shape), 0.0), axis=1, keepdims=True
        )

    for copy in copies[:2]:
        copy.wait()
    note = jnp.zeros((count, 128), jnp.float32)
    for k in range(topk):
        name = column(names[k].astype(jnp.float32))
        weight = column(weights[k])
        low = weight - weight.astype(jnp.bfloat16).astype(jnp.float32)
        for value, at in ((name, k), (weight, topk + k), (low, 2 * topk + k)):
            note = jnp.where(lane == at, value, note)
    out[:, half : half + 128] = note.astype(jnp.bfloat16)
    for copy in copies[2:]:
        copy.wait()
    out[:, :half] = tokens[:, :half]
    out[:, half + 128 :] = tokens[:, half:width]


def fetch_kernel(after, *refs, start):
    count = len(refs) // 2
    ins, outs, sems = refs[:count], refs[count:-1], refs[-1]
    pairs = [(a.at[:, start : start + b.shape[1]], b) for a, b in zip(ins[:2], outs[:2])]
    for source, target in zip(ins[2:], outs[2:]):
        width = target.shape[1]
        if source.shape[1] != width:
            own_at = pl.multiple_of(lax.axis_index("ctx") * width, 128)
            source = source.at[:, pl.ds(own_at, width)]
        pairs.append((source, target))
    for copy in start_copies(pairs, sems, PIECES):
        copy.wait()


def fetch_other_kernel(after, source, target, sems):
    width = target.shape[1]
    at = pl.multiple_of((1 - lax.axis_index("ctx")) * width, 128)
    for copy in start_copies([(source.at[:, pl.ds(at, width)], target)], sems, PIECES):
        copy.wait()


def stack_kernel(*refs, cuts):
    ins, outs = refs[: len(refs) - len(cuts)], refs[len(refs) - len(cuts) :]
    for out, (low, high) in zip(outs, cuts):
        if ins[0].shape[0] % 16 == 0:
            at = 0
            for ref in ins:
                out[at : at + ref.shape[0], :] = ref[:, low:high]
                at += ref.shape[0]
        else:
            rows = [ref[:, low:high].astype(jnp.float32) for ref in ins]
            out[...] = jnp.concatenate(rows, axis=0).astype(out.dtype)


def attention_kernel(
    after, earlier, earlier_other, queries, latents, attended, even, odd, mixed, sems
):
    width, rows = latents.shape
    pad = even.shape[0] - width
    even[width:, :] = jnp.zeros((pad, 2 * rows), jnp.bfloat16)
    odd[:pad, :] = jnp.zeros((pad, 2 * rows), jnp.bfloat16)
    share = width // 2
    core = lax.axis_index("exp") % 2
    for side, ref in ((core, earlier), (1 - core, earlier_other)):
        even[pl.ds(pl.multiple_of(side * share, 16), share), :rows] = ref[...]
        odd[pl.ds(pl.multiple_of(side * share + pad, 16), share), :rows] = ref[...]
    even[:width, rows:] = latents[...]
    odd[pad:, rows:] = latents[...]
    row = lax.broadcasted_iota(jnp.int32, (rows, 2 * rows), 0)
    key = lax.broadcasted_iota(jnp.int32, (rows, 2 * rows), 1)
    nearest = jnp.where(lax.axis_index("ctx") > 0, 0, rows)
    seen = (key >= nearest) & (key <= row + rows)
    heads = attended.shape[1] // LATENT
    writes = []
    for head in range(heads):
        start = head * width
        keys, start = (even, start) if start % 128 == 0 else (odd, start - pad)
        scores = jnp.dot(
            queries[:, start : start + width + pad], keys[...], preferred_element_type=jnp.float32
        )
        scores = jnp.where(seen, scores * SCALE, jnp.float32(-1e30))
        expo = jnp.exp(scores - jnp.max(scores, axis=-1, keepdims=True))
        probs = (expo / jnp.sum(expo, axis=-1, keepdims=True)).astype(jnp.bfloat16)
        span = slice(head * LATENT, (head + 1) * LATENT)
        mixed[:, span] = times_rows_in(probs, even[:LATENT, :]).astype(jnp.bfloat16)
        write = pltpu.make_async_copy(mixed.at[:, span], attended.at[:, span], sems.at[head])
        write.start()
        writes.append(write)
    for copy in writes:
        copy.wait()


def assemble(place, two_ref, far_ref, two_other_ref, far_other_ref, unit, y_first, start=0):
    span = slice(start, start + place.shape[1])
    order = (0, 2, 1, 3) if y_first else (0, 1, 2, 3)
    for lane, two, far in ((0, two_ref, far_ref), (1, two_other_ref, far_other_ref)):
        for number, block in enumerate(order):
            ref = (two, far)[number // 2]
            rows = slice(number % 2 * unit, (number % 2 + 1) * unit)
            base = (lane * 4 + block) * unit
            place[base : base + unit, :] = ref[rows, span]


def first_kernel(
    two, far, two_other, far_other, gate_w, up_w,
    gate_out, up_out, pick_out, pick_far_out, coef_out, tokens,
    notes, *, unit, tok_dev, capacity, topk,
):
    width = tokens.shape[1]
    rows = tokens.shape[0]
    slots = pick_out.shape[1]
    expert = lax.axis_index("exp")
    assemble(tokens, two, far, two_other, far_other, unit, False)
    few = gate_out.shape[1]
    gate_out[...] = times_rows_in(tokens[...], gate_w[:few, :])
    up_out[...] = times_rows_in(tokens[...], up_w[:few, :])

    assemble(notes, two, far, two_other, far_other, unit, False, width)
    note = notes[...].astype(jnp.float32)
    lane = lax.broadcasted_iota(jnp.int32, note.shape, 1)
    mine = (note == expert.astype(jnp.float32)) & (lane < topk)
    weight = pltpu.roll(note, 128 - topk, 1) + pltpu.roll(note, 128 - 2 * topk, 1)
    coef = jnp.sum(jnp.where(mine, weight, 0.0), axis=1, keepdims=True)
    hit = jnp.sum(mine.astype(jnp.float32), axis=1, keepdims=True)
    shift = tok_dev.bit_length() - 1
    at = lax.broadcasted_iota(jnp.int32, (rows, rows), 0)
    before = lax.broadcasted_iota(jnp.int32, (rows, rows), 1)
    earlier = ((at >> shift) == (before >> shift)) & (before < at)
    hits = jnp.broadcast_to(hit, (rows, slots))
    rank = jnp.dot(
        earlier.astype(jnp.float32).astype(jnp.bfloat16),
        hits.astype(jnp.bfloat16),
        preferred_element_type=jnp.float32,
    ).astype(jnp.int32)
    row = lax.broadcasted_iota(jnp.int32, (rows, slots), 0)
    slot = (row >> shift) * capacity + rank
    group = unit // tok_dev * capacity
    away = ((row >> (unit.bit_length() - 1)) & 1) == 0
    slot_far = slot + jnp.where(away, group, -group)
    column = lax.broadcasted_iota(jnp.int32, (rows, slots), 1)
    pick_out[...] = jnp.where(slot == column, hits, 0.0).astype(jnp.bfloat16)
    pick_far_out[...] = jnp.where(slot_far == column, hits, 0.0).astype(jnp.bfloat16)
    coef_out[...] = jnp.broadcast_to(coef, coef_out.shape)


def finish_units(gate, upper, pick, act_out, packed_out):
    act = (gate / (1.0 + jnp.exp(-gate)) * upper).astype(jnp.bfloat16)
    act_out[...] = act
    packed_out[...] = lax.dot_general(
        pick[...], act, (((0,), (0,)), ((), ())), preferred_element_type=jnp.float32
    ).astype(jnp.bfloat16)


def second_kernel(
    two, far, two_other, far_other, gate_w, up_w, gate_in, up_in, pick,
    act_out, packed_out, tokens, *, unit,
):
    assemble(tokens, two, far, two_other, far_other, unit, True)
    few = act_out.shape[1]
    gate = gate_in[...] + times_rows_in(tokens[...], gate_w[:few, :])
    upper = up_in[...] + times_rows_in(tokens[...], up_w[:few, :])
    finish_units(gate, upper, pick, act_out, packed_out)


def third_kernel(first, gate_1, up_1, second, gate_2, up_2, pick, act_out, packed_out, *, start):
    gate = times_rows_in(first[...], gate_1[start:, :]) + times_rows_in(
        second[...], gate_2[start:, :]
    )
    upper = times_rows_in(first[...], up_1[start:, :]) + times_rows_in(second[...], up_2[start:, :])
    finish_units(gate, upper, pick, act_out, packed_out)


def own_kernel(act_a, act_b, down_own, out):
    few = act_a.shape[1]
    tall = 512 if out.shape[1] % 512 == 0 else out.shape[1]
    for n in range(0, out.shape[1], tall):
        span = slice(n, n + tall)
        out[:, span] = times_rows_in(act_a[...], down_own[span, :few]) + times_rows_in(
            act_b[...], down_own[span, few:]
        )


def more_kernel(packed, pick, down_w, own, out, act):
    few = act.shape[1]
    act[...] = jnp.dot(pick[...], packed[...], preferred_element_type=jnp.float32).astype(
        jnp.bfloat16
    )
    tall = 512 if out.shape[1] % 512 == 0 else out.shape[1]
    for n in range(0, out.shape[1], tall):
        span = slice(n, n + tall)
        out[:, span] = own[:, span] + times_rows_in(act[...], down_w[span, :few])


def other_kernel(packed, pick, coef, down_w, own, keep, give, act, *, start):
    act[...] = jnp.dot(pick[...], packed[...], preferred_element_type=jnp.float32).astype(
        jnp.bfloat16
    )
    few = down_w.shape[1] - act.shape[1]
    half, part = keep.shape
    tall = part // 5 if part % 5 == 0 else part
    for n in range(0, part, tall):
        span = slice(start + n, start + n + tall)
        projected = own[:, span] + times_rows_in(act[...], down_w[span, few:])
        projected = projected * coef[:, :1]
        keep[:, n : n + tall] = projected[:half]
        give[:, n : n + tall] = projected[half:].astype(jnp.bfloat16)


def spread_kernel(keep, got, send, stay, *, y_first):
    unit = keep.shape[0] // 4
    stays, sends = ((0, 1), (2, 3)) if y_first else ((0, 2), (1, 3))
    for out, blocks in ((stay, stays), (send, sends)):
        for number, block in enumerate(blocks):
            span = slice(block * unit, (block + 1) * unit)
            total = keep[span, :] + got[span, :].astype(jnp.float32)
            out[number * unit : (number + 1) * unit, :] = total.astype(out.dtype)


def cross_kernel(stay, got, send, left, *, y_first):
    unit, part = send.shape[0], stay.shape[1]
    if y_first:
        left[...] = stay[:unit, :] + got[:unit, :].astype(jnp.float32)
        send[...] = (stay[unit:, :] + got[unit:, :].astype(jnp.float32)).astype(jnp.bfloat16)
    else:
        left[:, :part] = stay[:unit, :]
        left[:, part:] = got[:unit, :].astype(jnp.float32)
        send[:, :part] = stay[unit:, :].astype(jnp.bfloat16)
        send[:, part:] = got[unit:, :]


def line_kernel(left_x, got_y, left_y, got_x, *outs):
    ctx = lax.axis_index("ctx")
    count, part = outs[0].shape[0], left_y.shape[1]
    whole = left_x[...] + got_y[...].astype(jnp.float32)
    blocks = (
        (left_y[...], ctx, 0),
        (got_x[...].astype(jnp.float32), 1 - ctx, 0),
        (whole[:, :part], ctx, 1),
        (whole[:, part:], 1 - ctx, 1),
    )
    for value, side, number in blocks:
        at = pl.multiple_of(side * 2 * part + number * part, 128)
        for place, out in enumerate(outs):
            rows = value[place * count : (place + 1) * count]
            out[:, pl.ds(at, part)] = rows.astype(out.dtype)


def sum_kernel(first, *refs):
    total = first[...]
    for ref in refs[:-1]:
        total = total + ref[...].astype(jnp.float32)
    refs[-1][...] = total.astype(refs[-1].dtype)


def on_device_gathered(
    hidden, queries, latents, expert_ids, route_weight, w_gate, w_up, w_down
):
    tok_dev = hidden.shape[1]
    width = hidden.shape[2]
    topk = expert_ids.shape[2]
    units = w_gate.shape[1]
    columns = w_down.shape[1]
    tok_att, key_width = latents.shape
    heads_dev = queries.shape[1] // key_width
    experts = lax.axis_size("exp")
    line = experts // 4
    capacity = min(tok_dev, max(2, 3 * topk * tok_dev // (2 * experts)))
    half = width // 2
    unit = line * tok_dev
    count = 8 * unit
    slots = count // tok_dev * capacity
    bf16, f32 = jnp.bfloat16, jnp.float32

    rows, latents_half = local_kernel(
        lambda *refs: rows_kernel(*refs, half=half, topk=topk),
        [
            (hidden[0], "hbm"),
            (jnp.transpose(expert_ids, (2, 0, 1)), "hbm"),
            (jnp.transpose(route_weight, (2, 0, 1)), "hbm"),
            (latents.T, "hbm"),
        ],
        [((tok_dev, width + 128), bf16, "vmem"), ((key_width // 2, tok_att), bf16, "vmem")],
        [
            pltpu.VMEM((tok_dev, width), bf16),
            pltpu.VMEM((topk, 1, tok_dev), jnp.int32),
            pltpu.VMEM((topk, 1, tok_dev), f32),
            pltpu.SemaphoreType.DMA((4,)),
        ],
        "rows",
    )
    places = (3, 2, 1)
    along = [rows] + [along_line(rows, d) for d in places]
    earlier_kv = swapped(latents_half, "ctx", 1)
    gate_1, up_1, queries_here, latents_here = local_kernel(
        lambda *refs: fetch_kernel(*refs, start=0),
        [
            (rows, "vmem"), (w_gate[0], "hbm"), (w_up[0], "hbm"),
            (queries, "hbm"), (latents.T, "hbm"),
        ],
        [((units, half), bf16, "vmem")] * 2
        + [(queries.shape, bf16, "vmem"), ((key_width, tok_att), bf16, "vmem")],
        [pltpu.SemaphoreType.DMA((4 * PIECES,))],
        "fetch",
    )
    *along, earlier_kv, gate_1, up_1 = lax.optimization_barrier((*along, earlier_kv, gate_1, up_1))
    cuts = ((0, half + 128), (half + 128, width + 128))
    nears = local_kernel(
        lambda *refs: stack_kernel(*refs, cuts=cuts),
        [(row, "vmem") for row in along],
        [((unit, high - low), bf16, "vmem") for low, high in cuts],
        [],
        "stack_line",
    )
    (down_other,) = local_kernel(
        fetch_other_kernel,
        [(nears[1], "vmem"), (w_down[0], "hbm")],
        [((columns, units), bf16, "vmem")],
        [pltpu.SemaphoreType.DMA((PIECES,))],
        "fetch",
    )
    pieces = []
    for near, first, then in zip(nears, (over_x, over_y), (over_y, over_x)):
        got = paired(near, first)
        if first is over_x:
            got, down_other = lax.optimization_barrier((got, down_other))
        (two,) = local_kernel(
            lambda *refs, cut=near.shape[1]: stack_kernel(*refs, cuts=((0, cut),)),
            [(near, "vmem"), (got, "vmem")],
            [((2 * unit, near.shape[1]), bf16, "vmem")],
            [],
            "stack_two",
        )
        pieces.append([two, paired(two, then)])
    gate_2, up_2, down_mine = local_kernel(
        lambda *refs: fetch_kernel(*refs, start=half),
        [(pieces[1][0], "vmem"), (w_gate[0], "hbm"), (w_up[0], "hbm"), (w_down[0], "hbm")],
        [((units, half), bf16, "vmem")] * 2 + [((columns, units), bf16, "vmem")],
        [pltpu.SemaphoreType.DMA((3 * PIECES,))],
        "fetch",
    )
    earlier_other = swapped(earlier_kv, "exp", 1)
    pieces[0][1], gate_2, up_2, down_mine, earlier_other = lax.optimization_barrier(
        (pieces[0][1], gate_2, up_2, down_mine, earlier_other)
    )
    for number, (two, far) in enumerate(pieces):
        group = (two, far, swapped(two, "exp", 1), swapped(far, "exp", 1))
        pieces[number] = [(piece, "vmem") for piece in group]

    few = 2 * units // 3 if units % 384 == 0 else units // 2
    gate, up, pick, pick_far, coef, tokens_1 = local_kernel(
        lambda *refs: first_kernel(
            *refs, unit=unit, tok_dev=tok_dev, capacity=capacity, topk=topk
        ),
        [*pieces[0], (gate_1, "vmem"), (up_1, "vmem")],
        [((count, few), f32, "vmem")] * 2
        + [((count, slots), bf16, "vmem")] * 2
        + [((count, 128), f32, "vmem"), ((count, half), bf16, "vmem")],
        [pltpu.VMEM((count, 128), bf16)],
        "gate_up_first",
    )
    sums_in = [(gate_2, "vmem"), (up_2, "vmem"), (gate, "vmem"), (up, "vmem"), (pick, "vmem")]
    act_a, packed_a, tokens_2 = local_kernel(
        lambda *refs: second_kernel(*refs, unit=unit),
        [*pieces[1], *sums_in],
        [
            ((count, few), bf16, "vmem"),
            ((slots, few), bf16, "vmem"),
            ((count, half), bf16, "vmem"),
        ],
        [],
        "gate_up_second",
    )
    other_a = swapped(packed_a, "ctx", 1)
    act_b, packed_b = local_kernel(
        lambda *refs: third_kernel(*refs, start=few),
        [
            (tokens_1, "vmem"), (gate_1, "vmem"), (up_1, "vmem"),
            (tokens_2, "vmem"), (gate_2, "vmem"), (up_2, "vmem"), (pick, "vmem"),
        ],
        [((count, units - few), bf16, "vmem"), ((slots, units - few), bf16, "vmem")],
        [],
        "gate_up_third",
    )
    other_b = swapped(packed_b, "ctx", 1)
    (own,) = local_kernel(
        own_kernel,
        [(act_a, "vmem"), (act_b, "vmem"), (down_mine, "vmem")],
        [((count, columns), f32, "vmem")],
        [],
        "down_own",
    )
    (own,) = local_kernel(
        more_kernel,
        [(other_a, "vmem"), (pick_far, "vmem"), (down_other, "vmem"), (own, "vmem")],
        [((count, columns), f32, "vmem")],
        [pltpu.VMEM((count, few), bf16)],
        "down_more",
    )
    part = columns // 2
    crossing = []
    for start, y_first in ((part, False), (0, True)):
        keep, give = local_kernel(
            lambda *refs, start=start: other_kernel(*refs, start=start),
            [
                (other_b, "vmem"), (pick_far, "vmem"), (coef, "vmem"),
                (down_other, "vmem"), (own, "vmem"),
            ],
            [((count // 2, part), f32, "vmem"), ((count // 2, part), bf16, "vmem")],
            [pltpu.VMEM((count, units - few), bf16)],
            "down_other",
        )
        send, stay = local_kernel(
            lambda *refs, y_first=y_first: spread_kernel(*refs, y_first=y_first),
            [(keep, "vmem"), (swapped(give, "exp", 1), "vmem")],
            [((2 * unit, part), bf16, "vmem"), ((2 * unit, part), f32, "vmem")],
            [],
            "spread",
        )
        crossing.append((y_first, stay, paired(send, over_y if y_first else over_x)))
    lines = []
    for y_first, stay, got in crossing:
        wide = part if y_first else 2 * part
        send, left = local_kernel(
            lambda *refs, y_first=y_first: cross_kernel(*refs, y_first=y_first),
            [(stay, "vmem"), (got, "vmem")],
            [((unit, wide), bf16, "vmem"), ((unit, wide), f32, "vmem")],
            [],
            "cross",
        )
        lines += [left, paired(send, over_x if y_first else over_y)]
    keep, *sends = local_kernel(
        line_kernel,
        [(block, "vmem") for block in lines],
        [((tok_dev, 2 * columns), f32, "vmem")]
        + [((tok_dev, 2 * columns), bf16, "vmem")] * (line - 1),
        [],
        "line",
    )
    pad = -key_width % 128
    (attended,) = local_kernel(
        attention_kernel,
        [(sends[0], "vmem"), (earlier_kv, "vmem"), (earlier_other, "vmem"), (queries_here, "vmem"), (latents_here, "vmem")],
        [((tok_att, heads_dev * LATENT), bf16, "hbm")],
        [
            pltpu.VMEM((key_width + pad, 2 * tok_att), bf16),
            pltpu.VMEM((key_width + pad, 2 * tok_att), bf16),
            pltpu.VMEM((tok_att, heads_dev * LATENT), bf16),
            pltpu.SemaphoreType.DMA((heads_dev,)),
        ],
        "attention",
    )
    sends = dict(zip(places, sends))
    got = [along_line(sends[d], d) for d in (1, 2, 3)]
    got[-1], attended = lax.optimization_barrier((got[-1], attended))
    (mixed,) = local_kernel(
        sum_kernel,
        [(block, "vmem") for block in (keep, *got)],
        [((tok_dev, 2 * columns), bf16, "result")],
        [],
        "sum",
    )
    return (attended, mixed[None])


def on_device_slots(hidden, queries, latents, expert_ids, route_weight, w_gate, w_up, w_down):
    tok_att = latents.shape[0]
    heads_dev = queries.shape[1] // (LATENT + ROPE)
    tok_dev = hidden.shape[1]
    width = hidden.shape[2]
    topk = expert_ids.shape[2]
    experts = lax.axis_size("exp")
    groups = lax.axis_size("ctx")
    capacity = min(tok_dev, max(2, 3 * topk * tok_dev // (2 * experts)))
    slots = experts * capacity
    earlier_kv = shifted(latents, "ctx", 1)
    keys = jnp.concatenate([earlier_kv, latents], axis=0)
    query_rows = queries.reshape(tok_att, heads_dev, LATENT + ROPE)
    scores = jnp.einsum("thc,kc->htk", query_rows, keys, preferred_element_type=jnp.float32) * SCALE
    row_pos = jnp.arange(tok_att, dtype=jnp.int32)
    key_pos = jnp.arange(2 * tok_att, dtype=jnp.int32)
    seen_own = (key_pos[None, :] >= tok_att) & (key_pos[None, :] - tok_att <= row_pos[:, None])
    seen_prev = (key_pos[None, :] < tok_att) & (lax.axis_index("ctx") > 0)
    scores = jnp.where((seen_own | seen_prev)[None, :, :], scores, jnp.float32(-1e30))
    top = jnp.max(scores, axis=-1, keepdims=True)
    expo = jnp.exp(scores - top)
    probs = (expo / jnp.sum(expo, axis=-1, keepdims=True)).astype(jnp.bfloat16)
    mixed_heads = jnp.einsum(
        "htk,kc->thc", probs, keys[:, :LATENT], preferred_element_type=jnp.float32
    )
    attended = mixed_heads.astype(jnp.bfloat16).reshape(tok_att, heads_dev * LATENT)
    tokens = hidden[0]
    picks = expert_ids[0]
    pick_weight = route_weight[0].reshape(-1)
    tok_hot = token_table(tok_dev, topk)
    slot_hot = place_picks(picks, experts, capacity)
    gate_w = w_gate[0]
    up_w = w_up[0]
    down_w = w_down[0]
    send_matrix = jnp.dot(slot_hot.T, tok_hot).astype(jnp.bfloat16)
    outgoing = jnp.dot(send_matrix, tokens, preferred_element_type=jnp.float32).astype(jnp.bfloat16)
    outgoing = outgoing.reshape(experts, capacity, width)
    arrived = lax.all_to_all(outgoing, "exp", split_axis=0, concat_axis=0, tiled=True)
    piece = lax.all_gather(arrived.reshape(slots, width), "ctx", axis=0, tiled=True)
    gate = times_rows(piece, gate_w)
    upper = times_rows(piece, up_w)
    hidden_units = (jax.nn.silu(gate) * upper).astype(jnp.bfloat16)
    projected = times_rows(lax.all_gather(hidden_units, "ctx", axis=1, tiled=True), down_w)
    columns = projected.astype(jnp.bfloat16).reshape(groups, experts, capacity, down_w.shape[0])
    by_block = lax.all_to_all(columns, "ctx", split_axis=0, concat_axis=3, tiled=True)
    returned = lax.all_to_all(by_block, "exp", split_axis=1, concat_axis=1, tiled=True)
    combine_matrix = jnp.dot(
        slot_hot.T, tok_hot * pick_weight[:, None], precision=lax.Precision.HIGHEST
    )
    back_rows = returned.reshape(slots, width).astype(jnp.float32)
    mixed = jnp.dot(combine_matrix.T, back_rows, precision=lax.Precision.HIGHEST).astype(
        jnp.bfloat16
    )
    return (attended, mixed[None])


def solution(mesh):
    experts, groups = mesh.shape["exp"], mesh.shape["ctx"]
    whole = groups == 2 and experts == 16
    on_device = on_device_gathered if whole else on_device_slots
    placed = (
        P("exp", "ctx", None),
        P("ctx", "exp"),
        P("ctx", None),
        P("exp", "ctx", None),
        P("exp", "ctx", None),
        P("exp", "ctx", None),
        P("exp", "ctx", None),
        P("exp", "ctx", None),
    )
    return jax.shard_map(
        on_device,
        mesh=mesh,
        in_specs=placed,
        out_specs=(P("ctx", "exp"), P("exp", "ctx", None)),
        check_vma=False,
    )
```
